32 devices in a mesh: section: 2 (over core), dp: 4 (over y, x), shard: 4 (over z).
Axes of the slice: x: 2, y: 2, z: 4, core: 2. Of those that a mesh axis runs over, the one named last changes fastest.
Arguments:
- boundary: bfloat16 [2, 4, 4, 1024, 1024], P('section', None, 'shard', 'dp'), may hold values from -6 to 6
- first_len: int32 [4, 4], P(None, 'shard'), may hold values from 256 to 1024, as said below
- qkv_weight: bfloat16 [2, 1024, 3072], P('section', 'shard'), may hold values from -0.1875 to 0.1875
- out_weight: bfloat16 [2, 1024, 1024], P('section', 'shard'), may hold values from -0.1875 to 0.1875
- up_weight: bfloat16 [2, 1024, 4096], P('section', 'shard'), may hold values from -0.1875 to 0.1875
- down_weight: bfloat16 [2, 4096, 1024], P('section', 'shard'), may hold values from -0.09375 to 0.09375
- norm_gain: float32 [2, 3, 1024], P('section'), may hold values from 0.5 to 1.5
- norm_shift: float32 [2, 3, 1024], P('section'), may hold values from -1.5 to 1.5
- mid_gain: float32 [2, 4096], P('section'), may hold values from 0.5 to 1.5
- mid_shift: float32 [2, 4096], P('section'), may hold values from -1.5 to 1.5
- head_scale: float32 [2, 16], P('section'), may hold values from 0.25 to 1.75
Outputs:
- ends: bfloat16 [2, 4, 4, 1024, 1024], P('section', None, 'shard', 'dp')
- grad_qkv: float32 [2, 1024, 3072], P('section', 'shard')
- grad_out: float32 [2, 1024, 1024], P('section', 'shard')
- grad_up: float32 [2, 1024, 4096], P('section', 'shard')
- grad_down: float32 [2, 4096, 1024], P('section', 'shard')
- grad_norm_gain: float32 [2, 3, 1024], P('section')
- grad_norm_shift: float32 [2, 3, 1024], P('section')
- grad_mid_gain: float32 [2, 4096], P('section')
- grad_mid_shift: float32 [2, 4096], P('section')
- grad_head_scale: float32 [2, 16], P('section')
The draws below stay inside these ranges and needn't reach their ends.
Inputs may be any that keep to these rules, and one draw needn't show every extreme that they name: The first document runs from position 0 to first_len - 1 and the second fills the rest of the stream (empty when first_len = 1024). For every stream index g, at least one micro-batch has first_len = 1024.
All inputs are finite; a program needn't handle non-finite values.
Results may differ from the reference program's by a relative error of at most 0.015.
Values may be sent and summed in bfloat16 or wider, within the bound.
A program may use at most 320 MiB of HBM per device.

```python
import jax
import jax.numpy as jnp
from jax import lax

D = 1024
FF = 4096
HEADS = 16
HEAD_DIM = 64
MICRO = 4
LEN = 1024
GROUPS = 4


def draw_first_len(key, part):
    key = jax.random.fold_in(key, 11)
    key_part, key_whole, key_pick = jax.random.split(key, 3)
    partial_len = jax.random.randint(key_part, (MICRO, GROUPS), LEN // 4, 3 * LEN // 4 + 1)
    whole = jax.random.randint(key_whole, (MICRO, GROUPS), 0, 5) < 2
    picked = jax.random.randint(key_pick, (GROUPS,), 0, MICRO)
    forced = jnp.arange(MICRO, dtype=jnp.int32)[:, None] == picked[None, :]
    return jnp.where(whole | forced, LEN, partial_len).astype(jnp.int32)


def levels(rng, shape, pieces, least, high):
    level, own = 1.0, jax.random.fold_in(rng, 6)
    for dim, blocks in pieces:
        heights = jnp.exp(jax.random.uniform(jax.random.fold_in(own, dim), (blocks,), jnp.float32, least / len(pieces), high / len(pieces)))
        level = level * jnp.repeat(heights, shape[dim] // blocks).reshape([-1 if axis == dim else 1 for axis in range(len(shape))])
    return level


def bell_draw(key, extent, scale, limit, cuts=(), held_as=jnp.bfloat16):
    factor_of = levels(key, extent, cuts, -0.22, 0.18) if cuts else 1.0
    values = jax.random.normal(key, extent, jnp.float32) * scale * factor_of
    return jnp.minimum(jnp.maximum(values, -limit), limit).astype(held_as)


def setup_inputs(seed: int = 0) -> dict:
    streams_of = jax.random.split(jax.random.key(seed), 12)
    return {
        "boundary": bell_draw(streams_of[0], (2, MICRO, GROUPS, LEN, D), 1.0, 6.0, ((0, 2), (2, 4), (3, 4))),
        "first_len": draw_first_len(jax.random.fold_in(streams_of[11], 71), 0),
        "qkv_weight": bell_draw(streams_of[2], (2, D, 3 * D), D ** -0.5, 0.1875, ((0, 2), (1, 4))),
        "out_weight": bell_draw(streams_of[3], (2, D, D), D ** -0.5, 0.1875, ((0, 2), (1, 4))),
        "up_weight": bell_draw(streams_of[4], (2, D, FF), D ** -0.5, 0.1875, ((0, 2), (1, 4))),
        "down_weight": bell_draw(streams_of[5], (2, FF, D), FF ** -0.5, 0.09375, ((0, 2), (1, 4))),
        "norm_gain": jnp.clip(1.0 + 0.1 * jax.random.normal(streams_of[6], (2, 3, D), jnp.float32), 0.5, 1.5),
        "norm_shift": bell_draw(streams_of[7], (2, 3, D), 0.3, 1.5, ((0, 2),), jnp.float32),
        "mid_gain": jnp.clip(1.0 + 0.1 * jax.random.normal(streams_of[8], (2, FF), jnp.float32), 0.5, 1.5),
        "mid_shift": bell_draw(streams_of[9], (2, FF), 0.3, 1.5, ((0, 2),), jnp.float32),
        "head_scale": jnp.clip(1.0 + 0.15 * jax.random.normal(streams_of[10], (2, HEADS), jnp.float32), 0.25, 1.75),
    }


EPSILON = 1e-05
PRECISE = lax.Precision.HIGHEST

@jax.custom_vjp
def low(v):
    return lax.optimization_barrier(v.astype(jnp.bfloat16)).astype(jnp.float32)

@jax.custom_vjp
def low_back(v):
    return v

def low_keep(v):
    return (low(v), None)

def low_pass(kept, grad):
    return (grad,)

def back_keep(v):
    return (v, None)

def back_low(kept, grad):
    return (low(grad),)
low.defvjp(low_keep, low_pass)
low_back.defvjp(back_keep, back_low)

def normalize(values_in, gain, shift):
    centre = values_in - lax.optimization_barrier(jnp.mean(values_in, axis=-1, keepdims=True))
    spread = lax.optimization_barrier(jnp.mean(centre * centre, axis=-1, keepdims=True))
    return centre * lax.rsqrt(spread + EPSILON) * gain + shift

def visible(split_at):
    places = jnp.arange(LEN, dtype=jnp.int32)
    same_doc = (places[:, None] < split_at) == (places[None, :] < split_at)
    return same_doc & (places[None, :] <= places[:, None])

def block_forward(stream_in, params, allowed):
    weight_qkv, weight_out, weight_up, weight_down, gains, shifts, mid_gain, mid_shift, head_scale = params
    normed = low(normalize(stream_in, gains[0], shifts[0]))
    projected = low_back(low(jnp.dot(normed, weight_qkv, precision=PRECISE)))
    queries = projected[:, :D].reshape(LEN, HEADS, HEAD_DIM)
    key_rows = projected[:, D:2 * D].reshape(LEN, HEADS, HEAD_DIM)
    value_rows = projected[:, 2 * D:].reshape(LEN, HEADS, HEAD_DIM)
    scores = jnp.einsum('qhd,khd->hqk', queries, key_rows, precision=PRECISE) * HEAD_DIM ** (-0.5)
    scores = low_back(scores)
    scores = jnp.where(allowed[None], scores, -1e+30)
    row_max = lax.optimization_barrier(jnp.max(scores, axis=-1, keepdims=True))
    exp_scores = jnp.exp(scores - row_max)
    attend = low(exp_scores / lax.optimization_barrier(jnp.sum(exp_scores, axis=-1, keepdims=True)))
    head_out = low_back(jnp.einsum('hqk,khd->qhd', attend, value_rows, precision=PRECISE))
    scaled = low(head_out * head_scale[None, :, None]).reshape(LEN, D)
    branch = low_back(jnp.dot(scaled, weight_out, precision=PRECISE))
    residual = stream_in + normalize(branch, gains[1], shifts[1])
    ffn_input = low(normalize(residual, gains[2], shifts[2]))
    hidden = low_back(jnp.dot(ffn_input, weight_up, precision=PRECISE))
    middle = low(normalize(jax.nn.gelu(hidden, approximate=False), mid_gain, mid_shift))
    ffn_out = low_back(jnp.dot(middle, weight_down, precision=PRECISE))
    return residual + ffn_out

def add_up(first_term, second_term):
    return first_term + second_term

def reference(boundary, first_len, qkv_weight, out_weight, up_weight, down_weight, norm_gain, norm_shift, mid_gain, mid_shift, head_scale):
    params = tuple((item.astype(jnp.float32) for item in (qkv_weight, out_weight, up_weight, down_weight, norm_gain, norm_shift, mid_gain, mid_shift, head_scale)))
    inputs = boundary[0].astype(jnp.float32).reshape(MICRO * GROUPS, LEN, D)
    cotangents = boundary[1].astype(jnp.float32).reshape(MICRO * GROUPS, LEN, D)
    splits = first_len.reshape(MICRO * GROUPS).astype(jnp.int32)

    def one_stream(totals, stream_item):
        stream_in, cotangent, split_at = stream_item
        allowed = visible(split_at)

        def both_layers(weights, entry):
            between = low_back(low(block_forward(entry, tuple((w_item[0] for w_item in weights)), allowed)))
            return block_forward(between, tuple((w_item[1] for w_item in weights)), allowed)
        output, pullback = jax.vjp(both_layers, params, stream_in)
        grads, d_entry = pullback(cotangent)
        totals = jax.tree.map(add_up, totals, grads)
        return (totals, (output.astype(jnp.bfloat16), d_entry.astype(jnp.bfloat16)))
    zeros = jax.tree.map(jnp.zeros_like, params)
    totals, (outputs, d_entries) = lax.scan(one_stream, zeros, (inputs, cotangents, splits))
    ends = jnp.stack([d_entries.reshape(MICRO, GROUPS, LEN, D), outputs.reshape(MICRO, GROUPS, LEN, D)])
    return (ends, totals[0], totals[1], totals[2], totals[3], totals[4], totals[5], totals[6], totals[7], totals[8])
```

```python
import math

import jax
import jax.numpy as jnp
from jax import lax
from jax.experimental import pallas as pl
from jax.experimental.pallas import tpu as pltpu
from jax.sharding import PartitionSpec as P

EPSILON = 1e-05


def shifted(value, axis, steps):
    count = lax.axis_size(axis)
    first, last = (max(0, -steps), min(count, count - steps))
    return lax.ppermute(value, axis, [(source, source + steps) for source in range(first, last)])


def normalize(values_in, gain, shift):
    centre = values_in - jnp.mean(values_in, axis=-1, keepdims=True)
    spread = jnp.mean(centre * centre, axis=-1, keepdims=True)
    return centre * lax.rsqrt(spread + EPSILON) * gain + shift


def middle_norm(hidden, mid_gain, mid_shift):
    return normalize(jax.nn.gelu(hidden, approximate=False), mid_gain, mid_shift)


def contract_rows(left, right):
    return lax.dot_general(
        left, right, (((0,), (0,)), ((), ())), preferred_element_type=jnp.float32
    )


def contract_cols(left, right):
    return lax.dot_general(
        left, right, (((1,), (1,)), ((), ())), preferred_element_type=jnp.float32
    )


def visible(query_place, key_place, split_at):
    same_doc = (query_place[:, None] < split_at) == (key_place[None, :] < split_at)
    return same_doc & (key_place[None, :] <= query_place[:, None])


def forward_parts(stream_in, weights, small, split_at, head_count):
    weight_qkv, weight_out, weight_up, weight_down = weights
    gains, shifts, mid_gain, mid_shift, head_scale = small
    row_count, model_width = stream_in.shape
    head_dim = model_width // head_count
    factor = 1.0 / math.sqrt(head_dim)
    normed = normalize(stream_in, gains[0], shifts[0]).astype(jnp.bfloat16)
    projected = jnp.dot(normed, weight_qkv, preferred_element_type=jnp.float32).astype(jnp.bfloat16)
    queries = projected[:, :model_width].reshape(row_count, head_count, head_dim)
    key_rows = projected[:, model_width : 2 * model_width].reshape(row_count, head_count, head_dim)
    value_rows = projected[:, 2 * model_width :].reshape(row_count, head_count, head_dim)
    keys_all, values_all = (
        lax.all_gather(key_rows, "dp", axis=0, tiled=True),
        lax.all_gather(value_rows, "dp", axis=0, tiled=True),
    )
    seq_len = keys_all.shape[0]
    own_place = lax.axis_index("dp") * row_count + jnp.arange(row_count, dtype=jnp.int32)
    all_place = jnp.arange(seq_len, dtype=jnp.int32)
    allowed = visible(own_place, all_place, split_at)
    scores = (
        jnp.einsum("qhd,khd->hqk", queries, keys_all, preferred_element_type=jnp.float32) * factor
    )
    scores = jnp.where(allowed[None], scores, -1e30)
    row_max = jnp.max(scores, axis=-1, keepdims=True)
    log_total = row_max + jnp.log(jnp.sum(jnp.exp(scores - row_max), axis=-1, keepdims=True))
    attend = jnp.exp(scores - log_total)
    attend_low = attend.astype(jnp.bfloat16)
    head_out = jnp.einsum(
        "hqk,khd->qhd", attend_low, values_all, preferred_element_type=jnp.float32
    )
    scaled = (
        (head_out * head_scale[None, :, None]).astype(jnp.bfloat16).reshape(row_count, model_width)
    )
    branch = jnp.dot(scaled, weight_out, preferred_element_type=jnp.float32)
    residual = stream_in + normalize(branch, gains[1], shifts[1])
    ffn_input = normalize(residual, gains[2], shifts[2]).astype(jnp.bfloat16)
    hidden = jnp.dot(ffn_input, weight_up, preferred_element_type=jnp.float32)
    middle = middle_norm(hidden, mid_gain, mid_shift).astype(jnp.bfloat16)
    return dict(
        normed=normed,
        queries=queries,
        key_rows=key_rows,
        value_rows=value_rows,
        keys_all=keys_all,
        values_all=values_all,
        own_place=own_place,
        all_place=all_place,
        attend=attend,
        attend_low=attend_low,
        log_total=log_total,
        head_out=head_out,
        scaled=scaled,
        branch=branch,
        residual=residual,
        ffn_input=ffn_input,
        hidden=hidden,
        middle=middle,
        factor=factor,
    )


def backward_parts(stream_in, grad_in, weights, small, split_at, head_count):
    weight_qkv, weight_out, weight_up, weight_down = weights
    gains, shifts, mid_gain, mid_shift, head_scale = small
    parts = forward_parts(stream_in, weights, small, split_at, head_count)
    row_count, model_width = stream_in.shape
    head_dim = model_width // head_count
    factor = parts["factor"]
    grad_down = contract_rows(parts["middle"], grad_in)
    d_middle = contract_cols(grad_in, weight_down)
    unused, pull_middle = jax.vjp(middle_norm, parts["hidden"], mid_gain, mid_shift)
    d_hidden, grad_mid_gain, grad_mid_shift = pull_middle(d_middle)
    d_hidden = d_hidden.astype(jnp.bfloat16)
    grad_up = contract_rows(parts["ffn_input"], d_hidden)
    d_ffn_input = contract_cols(d_hidden, weight_up)
    unused, pull_third = jax.vjp(normalize, parts["residual"], gains[2], shifts[2])
    d_residual, gain_third, shift_third = pull_third(d_ffn_input)
    d_residual = d_residual + grad_in.astype(jnp.float32)
    unused, pull_second = jax.vjp(normalize, parts["branch"], gains[1], shifts[1])
    d_branch, gain_second, shift_second = pull_second(d_residual)
    d_branch = d_branch.astype(jnp.bfloat16)
    grad_out = contract_rows(parts["scaled"], d_branch)
    d_scaled = contract_cols(d_branch, weight_out).reshape(row_count, head_count, head_dim)
    grad_head_scale = jnp.sum(d_scaled * parts["head_out"], axis=(0, 2))
    d_heads = (d_scaled * head_scale[None, :, None]).astype(jnp.bfloat16)
    attend = parts["attend"]
    d_attend = jnp.einsum(
        "qhd,khd->hqk", d_heads, parts["values_all"], preferred_element_type=jnp.float32
    )
    row_dot = jnp.sum(attend * d_attend, axis=-1, keepdims=True)
    d_scores = (attend * (d_attend - row_dot)).astype(jnp.bfloat16)
    d_query = (
        jnp.einsum("hqk,khd->qhd", d_scores, parts["keys_all"], preferred_element_type=jnp.float32)
        * factor
    ).astype(jnp.bfloat16)
    full_keys = (
        jnp.einsum("hqk,qhd->khd", d_scores, parts["queries"], preferred_element_type=jnp.float32)
        * factor
    )
    full_values = jnp.einsum(
        "hqk,qhd->khd", parts["attend_low"], d_heads, preferred_element_type=jnp.float32
    )
    d_keys, d_values = (
        lax.psum_scatter(full_keys, "dp", scatter_dimension=0, tiled=True),
        lax.psum_scatter(full_values, "dp", scatter_dimension=0, tiled=True),
    )
    d_projected = jnp.concatenate(
        [
            d_query.reshape(row_count, model_width),
            d_keys.astype(jnp.bfloat16).reshape(row_count, model_width),
            d_values.astype(jnp.bfloat16).reshape(row_count, model_width),
        ],
        axis=1,
    )
    grad_qkv = contract_rows(parts["normed"], d_projected)
    d_normed = contract_cols(d_projected, weight_qkv)
    unused, pull_first = jax.vjp(normalize, stream_in, gains[0], shifts[0])
    d_entry, gain_first, shift_first = pull_first(d_normed)
    d_entry = d_entry + d_residual
    big_grads = (grad_qkv, grad_out, grad_up, grad_down)
    small_grads = (
        jnp.stack([gain_first, gain_second, gain_third]),
        jnp.stack([shift_first, shift_second, shift_third]),
        grad_mid_gain,
        grad_mid_shift,
        grad_head_scale,
    )
    return (d_entry, big_grads, small_grads)


def add_up(first_term, second_term):
    return first_term + second_term


def general(
    boundary,
    first_len,
    qkv_weight,
    out_weight,
    up_weight,
    down_weight,
    norm_gain,
    norm_shift,
    mid_gain,
    mid_shift,
    head_scale,
):
    section_index = lax.axis_index("section")
    gathered = (
        lax.all_gather(qkv_weight, "shard", axis=1, tiled=True),
        lax.all_gather(out_weight, "shard", axis=1, tiled=True),
        lax.all_gather(up_weight, "shard", axis=1, tiled=True),
        lax.all_gather(down_weight, "shard", axis=1, tiled=True),
    )
    weights = tuple((piece[0] for piece in gathered))
    small = (norm_gain[0], norm_shift[0], mid_gain[0], mid_shift[0], head_scale[0])
    head_count = head_scale.shape[1]
    micro = boundary.shape[1]
    row_count = boundary.shape[3]
    model_width = boundary.shape[4]
    local_ends = boundary[0, :, 0]
    splits = first_len[:, 0]

    def forward_tick(step_index, carry):
        incoming, kept, ends = carry
        index = step_index - section_index
        active = (index >= 0) & (index < micro)
        slot = jnp.clip(index, 0, micro - 1)
        entry = jnp.where(section_index == 0, local_ends[slot], incoming)
        parts = forward_parts(entry.astype(jnp.float32), weights, small, splits[slot], head_count)
        result = (
            parts["residual"]
            + jnp.dot(parts["middle"], weights[3], preferred_element_type=jnp.float32)
        ).astype(jnp.bfloat16)
        kept = kept.at[slot].set(jnp.where(active, entry, kept[slot]))
        ends = ends.at[slot].set(jnp.where(active, result, ends[slot]))
        incoming = shifted(result, "section", 1)
        return (incoming, kept, ends)

    blank = jnp.zeros((row_count, model_width), jnp.bfloat16)
    stack_blank = jnp.zeros((micro, row_count, model_width), jnp.bfloat16)
    unused, kept, ends = lax.fori_loop(
        0, micro + 1, forward_tick, (blank, stack_blank, stack_blank)
    )

    def backward_tick(step_index, carry):
        incoming, ends, big_sums, small_sums = carry
        index = micro - step_index - section_index
        active = (index >= 0) & (index < micro)
        slot = jnp.clip(index, 0, micro - 1)
        grad_in = jnp.where(section_index == 1, local_ends[slot], incoming)
        grad_in = jnp.where(active, grad_in, jnp.zeros_like(grad_in))
        d_entry, big_grads, small_grads = backward_parts(
            kept[slot].astype(jnp.float32), grad_in, weights, small, splits[slot], head_count
        )
        d_low = d_entry.astype(jnp.bfloat16)
        ends = ends.at[slot].set(jnp.where(active & (section_index == 0), d_low, ends[slot]))
        big_sums = jax.tree.map(add_up, big_sums, big_grads)
        small_sums = jax.tree.map(add_up, small_sums, small_grads)
        incoming = shifted(d_low, "section", -1)
        return (incoming, ends, big_sums, small_sums)

    big_zero = tuple((jnp.zeros(item.shape, jnp.float32) for item in weights))
    small_zero = tuple((jnp.zeros(item.shape, jnp.float32) for item in small))
    unused, ends, big_sums, small_sums = lax.fori_loop(
        0, micro + 1, backward_tick, (blank, ends, big_zero, small_zero)
    )
    shares = (
        lax.psum_scatter(big_sums[0][None], "shard", scatter_dimension=1, tiled=True),
        lax.psum_scatter(big_sums[1][None], "shard", scatter_dimension=1, tiled=True),
        lax.psum_scatter(big_sums[2][None], "shard", scatter_dimension=1, tiled=True),
        lax.psum_scatter(big_sums[3][None], "shard", scatter_dimension=1, tiled=True),
    )
    shares = lax.psum((shares[0], shares[1], shares[2], shares[3]), "dp")
    totals = lax.psum(
        (small_sums[0], small_sums[1], small_sums[2], small_sums[3], small_sums[4]), ("dp", "shard")
    )
    return (
        ends[None, :, None],
        shares[0],
        shares[1],
        shares[2],
        shares[3],
        totals[0][None],
        totals[1][None],
        totals[2][None],
        totals[3][None],
        totals[4][None],
    )


def core_swap(value):
    return lax.ppermute(value, "section", [(0, 1), (1, 0)])


def pick(value, index):
    return lax.dynamic_index_in_dim(value, index, 0, keepdims=False)


BF16 = jnp.bfloat16
F32 = jnp.float32
TILE = 256
VMEM_BYTES = 56 * 2**20


def rows_spec(columns):
    return pl.BlockSpec((TILE, columns), lambda step: (step, 0))


def group_spec(columns):
    return pl.BlockSpec((4, TILE, columns), lambda step: (0, step, 0))


def fixed_spec(shape):
    return pl.BlockSpec(shape, lambda step: (0,) * len(shape))


def call_rows(kernel, out_shapes, out_specs, in_specs, flops, moved):
    return pl.pallas_call(
        kernel,
        grid=(4,),
        in_specs=in_specs,
        out_specs=out_specs,
        out_shape=out_shapes,
        compiler_params=pltpu.CompilerParams(vmem_limit_bytes=VMEM_BYTES),
        cost_estimate=pl.CostEstimate(flops=flops, bytes_accessed=moved, transcendentals=0),
    )


def array(shape, dtype):
    return jax.ShapeDtypeStruct(shape, dtype)


def dot(left, right):
    return jnp.dot(left, right, preferred_element_type=F32)


def dot_nt(left, right):
    return lax.dot_general(left, right, (((1,), (1,)), ((), ())), preferred_element_type=F32)


def standard(values_in):
    centre = values_in - jnp.mean(values_in, axis=-1, keepdims=True)
    spread_of = jnp.mean(centre * centre, axis=-1, keepdims=True)
    scale = lax.rsqrt(spread_of + EPSILON)
    return centre * scale, scale


def standard_back(unit_values, scale, gain, grad):
    inner = grad * gain
    first = jnp.mean(inner, axis=-1, keepdims=True)
    second = jnp.mean(inner * unit_values, axis=-1, keepdims=True)
    back = scale * (inner - first - unit_values * second)
    return back, jnp.sum(grad * unit_values, axis=0, keepdims=True), jnp.sum(grad, axis=0, keepdims=True)


def add_rows(ref, row, value):
    ref[row : row + 1, :] += value


def clear_first(*refs):
    @pl.when(pl.program_id(0) == 0)
    def unused():
        for ref in refs:
            ref[...] = jnp.zeros_like(ref)


def project(entry, gain, shift, weight):
    def kernel(x_ref, gain_ref, shift_ref, w_ref, normed_ref, proj_ref):
        unit_x, unused = standard(x_ref[...].astype(F32))
        normed = (unit_x * gain_ref[...] + shift_ref[...]).astype(BF16)
        normed_ref[...] = normed
        for group in range(4):
            proj_ref[group] = dot(normed, w_ref[group]).astype(BF16)

    return call_rows(
        kernel,
        (array((1024, 1024), BF16), array((4, 1024, 384), BF16)),
        (rows_spec(1024), group_spec(384)),
        [rows_spec(1024), fixed_spec((1, 1024)), fixed_spec((1, 1024)), fixed_spec((4, 1024, 384))],
        2 * 1024 * 1024 * 1536,
        10 * 2**20,
    )(entry, gain, shift, weight)


def project_next(residual, part_own, part_other, gain, shift, weight):
    def kernel(res_ref, a_ref, b_ref, gain_ref, shift_ref, w_ref, entry_ref, normed_ref, proj_ref):
        entry = (res_ref[...] + (a_ref[...].astype(F32) + b_ref[...].astype(F32))).astype(BF16)
        entry_ref[...] = entry
        unit_x, unused = standard(entry.astype(F32))
        normed = (unit_x * gain_ref[...] + shift_ref[...]).astype(BF16)
        normed_ref[...] = normed
        for group in range(4):
            proj_ref[group] = dot(normed, w_ref[group]).astype(BF16)

    return call_rows(
        kernel,
        (array((1024, 1024), BF16), array((1024, 1024), BF16), array((4, 1024, 384), BF16)),
        (rows_spec(1024), rows_spec(1024), group_spec(384)),
        [rows_spec(1024)] * 3
        + [fixed_spec((1, 1024)), fixed_spec((1, 1024)), fixed_spec((4, 1024, 384))],
        2 * 1024 * 1024 * 1536,
        18 * 2**20,
    )(residual, part_own, part_other, gain, shift, weight)


def lane_masks(rows):
    lanes = lax.broadcasted_iota(jnp.int32, (rows, 128), 1)
    return lanes < 64


def fill_bias(bias_ref, split_at):
    @pl.when(pl.program_id(0) == 0)
    def unused():
        for block in range(4):
            keys = lax.broadcasted_iota(jnp.int32, (256, 1024), 0) + block * 256
            queries = lax.broadcasted_iota(jnp.int32, (256, 1024), 1)
            allowed = ((queries < split_at) == (keys < split_at)) & (keys <= queries)
            bias_ref[pl.ds(block * 256, 256), :] = jnp.where(allowed, 0.0, -1e30)


def attend_kernel(split_ref, q_ref, k_ref, v_ref, scale_ref, out_ref, scaled_ref, log_ref, bias_ref, turned_ref):
    fill_bias(bias_ref, split_ref[0])
    turned_ref[...] = v_ref[0].astype(F32).T.astype(BF16)
    low_lanes = lane_masks(256)
    for block in range(4):
        seen = (block + 1) * 256
        span = pl.ds(block * 256, 256)
        q = q_ref[0, span, :] * 0.125
        keys = k_ref[0, pl.ds(0, seen), :]
        halves_out = []
        for half in range(2):
            q_half = jnp.where(low_lanes if half == 0 else ~low_lanes, q, 0.0).astype(BF16)
            scores = dot_nt(keys, q_half) + bias_ref[pl.ds(0, seen), span]
            top = jnp.max(scores, axis=0, keepdims=True)
            powers = jnp.exp(scores - top)
            total = jnp.sum(powers, axis=0, keepdims=True)
            log_ref[0, half : half + 1, span] = top + jnp.log(total)
            mixed = dot(turned_ref[half * 64 : half * 64 + 64, :seen], powers.astype(BF16))
            halves_out.append(mixed * (1.0 / total))
        head_out = jnp.concatenate(halves_out, axis=0).T
        out_ref[span, :] = head_out.astype(BF16)
        scaled_ref[span, :] = (head_out * scale_ref[0]).astype(BF16)


def attention(proj, split_at, scale_rows):
    def cut(third):
        return pl.BlockSpec((1, 1024, 128), lambda group, split: (group, 0, third))

    return pl.pallas_call(
        attend_kernel,
        grid_spec=pltpu.PrefetchScalarGridSpec(
            num_scalar_prefetch=1,
            grid=(4,),
            in_specs=[cut(0), cut(1), cut(2), pl.BlockSpec((1, 1, 128), lambda group, split: (group, 0, 0))],
            out_specs=[
                pl.BlockSpec((1024, 128), lambda group, split: (0, group)),
                pl.BlockSpec((1024, 128), lambda group, split: (0, group)),
                pl.BlockSpec((1, 2, 1024), lambda group, split: (group, 0, 0)),
            ],
            scratch_shapes=[pltpu.VMEM((1024, 1024), F32), pltpu.VMEM((128, 1024), BF16)],
        ),
        out_shape=(array((1024, 512), BF16), array((1024, 512), BF16), array((4, 2, 1024), F32)),
        compiler_params=pltpu.CompilerParams(vmem_limit_bytes=VMEM_BYTES),
        cost_estimate=pl.CostEstimate(flops=20 * 10**9, bytes_accessed=8 * 2**20, transcendentals=0),
    )(split_at, proj, proj, proj, scale_rows)


def attend_back_kernel(
    split_ref, q_ref, k_ref, v_ref, grad_ref, out_ref, log_ref, back_ref, bias_ref, turned_ref, dk_ref, dv_ref
):
    fill_bias(bias_ref, split_ref[0])
    turned_ref[...] = k_ref[0].astype(F32).T.astype(BF16)
    dk_ref[...] = jnp.zeros_like(dk_ref)
    dv_ref[...] = jnp.zeros_like(dv_ref)
    low_lanes = lane_masks(256)
    for block in range(4):
        seen = (block + 1) * 256
        span = pl.ds(block * 256, 256)
        q = q_ref[0, span, :] * 0.125
        grad = grad_ref[span, :]
        product = (grad.astype(F32) * out_ref[span, :].astype(F32)).T
        keys = k_ref[0, pl.ds(0, seen), :]
        values = v_ref[0, pl.ds(0, seen), :]
        dq_halves, lows, d_scores_all, q_halves, grad_halves = [], [], [], [], []
        for half in range(2):
            mask = low_lanes if half == 0 else ~low_lanes
            q_half = jnp.where(mask, q, 0.0).astype(BF16)
            grad_half = jnp.where(mask, grad, 0.0).astype(BF16)
            row_dot = jnp.sum(product[half * 64 : half * 64 + 64, :], axis=0, keepdims=True)
            scores = dot_nt(keys, q_half) + bias_ref[pl.ds(0, seen), span]
            attend = jnp.exp(scores - log_ref[0, half : half + 1, span])
            d_attend = dot_nt(values, grad_half)
            d_scores = (attend * (d_attend - row_dot)).astype(BF16)
            dq_halves.append(dot(turned_ref[half * 64 : half * 64 + 64, :seen], d_scores))
            lows.append(attend.astype(BF16))
            d_scores_all.append(d_scores)
            q_halves.append(q_half)
            grad_halves.append(grad_half)
        dv_ref[pl.ds(0, seen), :] += dot(jnp.concatenate(lows, axis=1), jnp.concatenate(grad_halves, axis=0))
        dk_ref[pl.ds(0, seen), :] += dot(jnp.concatenate(d_scores_all, axis=1), jnp.concatenate(q_halves, axis=0))
        back_ref[0, span, 0:128] = (jnp.concatenate(dq_halves, axis=0).T * 0.125).astype(BF16)
    back_ref[0, :, 128:256] = dk_ref[...].astype(BF16)
    back_ref[0, :, 256:384] = dv_ref[...].astype(BF16)


def attention_back(proj, split_at, grad, head_out, logs):
    def cut(third):
        return pl.BlockSpec((1, 1024, 128), lambda group, split: (group, 0, third))

    columns = pl.BlockSpec((1024, 128), lambda group, split: (0, group))
    return pl.pallas_call(
        attend_back_kernel,
        grid_spec=pltpu.PrefetchScalarGridSpec(
            num_scalar_prefetch=1,
            grid=(4,),
            in_specs=[cut(0), cut(1), cut(2), columns, columns, pl.BlockSpec((1, 2, 1024), lambda group, split: (group, 0, 0))],
            out_specs=pl.BlockSpec((1, 1024, 384), lambda group, split: (group, 0, 0)),
            scratch_shapes=[
                pltpu.VMEM((1024, 1024), F32),
                pltpu.VMEM((128, 1024), BF16),
                pltpu.VMEM((1024, 128), F32),
                pltpu.VMEM((1024, 128), F32),
            ],
        ),
        out_shape=array((4, 1024, 384), BF16),
        compiler_params=pltpu.CompilerParams(vmem_limit_bytes=VMEM_BYTES),
        cost_estimate=pl.CostEstimate(flops=40 * 10**9, bytes_accessed=10 * 2**20, transcendentals=0),
    )(split_at, proj, proj, proj, grad, head_out, logs)


def two_columns(first, second):
    return jnp.where(lane_masks(first.shape[0]), first, second)


def widen(entry, part_own, part_other, gains, shifts, weight):
    def kernel(x_ref, a_ref, b_ref, gain_ref, shift_ref, w_ref, res_ref, ffn_ref, gelu_ref, slope_ref, stat_ref):
        branch = a_ref[...].astype(F32) + b_ref[...].astype(F32)
        unit_b, unused = standard(branch)
        residual = x_ref[...].astype(F32) + unit_b * gain_ref[1:2] + shift_ref[1:2]
        res_ref[...] = residual
        unit_r, unused = standard(residual)
        ffn_input = (unit_r * gain_ref[2:3] + shift_ref[2:3]).astype(BF16)
        ffn_ref[...] = ffn_input
        first, second = [], []
        for group in range(4):
            hidden = dot(ffn_input, w_ref[group])
            half = 0.5 + 0.5 * lax.erf(hidden * math.sqrt(0.5))
            gelu = hidden * half
            bell = jnp.exp(-0.5 * hidden * hidden) * (1.0 / math.sqrt(2.0 * math.pi))
            gelu_ref[group] = gelu.astype(BF16)
            slope_ref[group] = (half + hidden * bell).astype(BF16)
            mean = jnp.mean(gelu, axis=-1, keepdims=True)
            centre = gelu - mean
            first.append(mean)
            second.append(jnp.mean(centre * centre, axis=-1, keepdims=True))
        mean = 0.25 * (first[0] + first[1] + first[2] + first[3])
        spread_of = sum(0.25 * (s + (m - mean) * (m - mean)) for m, s in zip(first, second))
        stat_ref[...] = two_columns(mean, spread_of)

    wide = array((4, 1024, 512), BF16)
    return call_rows(
        kernel,
        (array((1024, 1024), F32), array((1024, 1024), BF16), wide, wide, array((1024, 128), F32)),
        (rows_spec(1024), rows_spec(1024), group_spec(512), group_spec(512), rows_spec(128)),
        [rows_spec(1024)] * 3 + [fixed_spec((3, 1024)), fixed_spec((3, 1024)), fixed_spec((4, 1024, 512))],
        2 * 1024 * 1024 * 2048,
        30 * 2**20,
    )(entry, part_own, part_other, gains, shifts, weight)


def mid_stats(own, other):
    mean_own, mean_other = own[:, 0:1], other[:, 0:1]
    gap = mean_own - mean_other
    spread_of = 0.5 * (own[:, 64:65] + other[:, 64:65]) + 0.25 * gap * gap
    return 0.5 * (mean_own + mean_other), lax.rsqrt(spread_of + EPSILON)


def narrow(gelu, own, other, gain, shift, weight):
    def kernel(g_ref, own_ref, other_ref, gain_ref, shift_ref, w_ref, mid_ref, part_ref):
        mean, scale = mid_stats(own_ref[...], other_ref[...])
        total = jnp.zeros((TILE, 1024), F32)
        for group in range(4):
            unit_m = (g_ref[group].astype(F32) - mean) * scale
            middle = (unit_m * gain_ref[group : group + 1] + shift_ref[group : group + 1]).astype(BF16)
            mid_ref[group] = middle
            total = total + dot(middle, w_ref[group])
        part_ref[...] = total.astype(BF16)

    return call_rows(
        kernel,
        (array((4, 1024, 512), BF16), array((1024, 1024), BF16)),
        (group_spec(512), rows_spec(1024)),
        [group_spec(512), rows_spec(128), rows_spec(128), fixed_spec((4, 512)), fixed_spec((4, 512)), fixed_spec((4, 512, 1024))],
        2 * 1024 * 1024 * 2048,
        15 * 2**20,
    )(gelu, own, other, gain, shift, weight)


def narrow_back(grad, gelu, own, other, gain, weight):
    def kernel(c_ref, g_ref, own_ref, other_ref, gain_ref, w_ref, dm_ref, stat_ref, gg_ref, gs_ref):
        clear_first(gg_ref, gs_ref)
        mean, scale = mid_stats(own_ref[...], other_ref[...])
        grad_low = c_ref[...]
        first = jnp.zeros((TILE, 1), F32)
        second = jnp.zeros((TILE, 1), F32)
        for group in range(4):
            d_middle = dot_nt(grad_low, w_ref[group])
            dm_ref[group] = d_middle.astype(BF16)
            unit_m = (g_ref[group].astype(F32) - mean) * scale
            product = d_middle * unit_m
            add_rows(gg_ref, group, jnp.sum(product, axis=0, keepdims=True))
            add_rows(gs_ref, group, jnp.sum(d_middle, axis=0, keepdims=True))
            row_gain = gain_ref[group : group + 1]
            first = first + jnp.sum(d_middle * row_gain, axis=-1, keepdims=True)
            second = second + jnp.sum(product * row_gain, axis=-1, keepdims=True)
        stat_ref[...] = two_columns(first, second)

    return call_rows(
        kernel,
        (array((4, 1024, 512), BF16), array((1024, 128), F32), array((4, 512), F32), array((4, 512), F32)),
        (group_spec(512), rows_spec(128), fixed_spec((4, 512)), fixed_spec((4, 512))),
        [rows_spec(1024), group_spec(512), rows_spec(128), rows_spec(128), fixed_spec((4, 512)), fixed_spec((4, 512, 1024))],
        2 * 1024 * 1024 * 2048,
        15 * 2**20,
    )(grad, gelu, own, other, gain, weight)


def widen_back(d_middle, gelu, slope, own, other, sum_own, sum_other, gain, weight):
    def kernel(dm_ref, g_ref, s_ref, own_ref, other_ref, a_ref, b_ref, gain_ref, w_ref, dh_ref, part_ref):
        mean, scale = mid_stats(own_ref[...], other_ref[...])
        sums = (a_ref[...] + b_ref[...]) * (1.0 / 4096)
        first, second = sums[:, 0:1], sums[:, 64:65]
        total = jnp.zeros((TILE, 1024), F32)
        for group in range(4):
            unit_m = (g_ref[group].astype(F32) - mean) * scale
            inner = dm_ref[group].astype(F32) * gain_ref[group : group + 1]
            d_gelu = scale * (inner - first - unit_m * second)
            d_hidden = (d_gelu * s_ref[group].astype(F32)).astype(BF16)
            dh_ref[group] = d_hidden
            total = total + dot_nt(d_hidden, w_ref[group])
        part_ref[...] = total.astype(BF16)

    return call_rows(
        kernel,
        (array((4, 1024, 512), BF16), array((1024, 1024), BF16)),
        (group_spec(512), rows_spec(1024)),
        [group_spec(512)] * 3 + [rows_spec(128)] * 4 + [fixed_spec((4, 512)), fixed_spec((4, 1024, 512))],
        2 * 1024 * 1024 * 2048,
        20 * 2**20,
    )(d_middle, gelu, slope, own, other, sum_own, sum_other, gain, weight)


def norms_back(grad, residual, d_own, d_other, b_own, b_other, gains, head_out, scale_row, weight):
    def kernel(c_ref, res_ref, da_ref, db_ref, ba_ref, bb_ref, gain_ref, ho_ref, hs_ref, w_ref,
               dr_ref, dbr_ref, dh_ref, sum_ref, head_ref):
        clear_first(sum_ref, head_ref)
        unit_r, scale_r = standard(res_ref[...])
        d_ffn = da_ref[...].astype(F32) + db_ref[...].astype(F32)
        back, gain_third, shift_third = standard_back(unit_r, scale_r, gain_ref[2:3], d_ffn)
        d_residual = c_ref[...].astype(F32) + back
        dr_ref[...] = d_residual
        unit_b, scale_b = standard(ba_ref[...].astype(F32) + bb_ref[...].astype(F32))
        back, gain_second, shift_second = standard_back(unit_b, scale_b, gain_ref[1:2], d_residual)
        d_branch = back.astype(BF16)
        dbr_ref[...] = d_branch
        d_scaled = dot_nt(d_branch, w_ref[...])
        dh_ref[...] = (d_scaled * hs_ref[...]).astype(BF16)
        add_rows(head_ref, 0, jnp.sum(d_scaled * ho_ref[...].astype(F32), axis=0, keepdims=True))
        for row, value in enumerate((gain_second, gain_third, shift_second, shift_third)):
            add_rows(sum_ref, row, value)

    return call_rows(
        kernel,
        (
            array((1024, 1024), F32),
            array((1024, 1024), BF16),
            array((1024, 512), BF16),
            array((8, 1024), F32),
            array((8, 512), F32),
        ),
        (rows_spec(1024), rows_spec(1024), rows_spec(512), fixed_spec((8, 1024)), fixed_spec((8, 512))),
        [rows_spec(1024)] * 6
        + [fixed_spec((3, 1024)), rows_spec(512), fixed_spec((1, 512)), fixed_spec((512, 1024))],
        2 * 1024 * 1024 * 512,
        25 * 2**20,
    )(grad, residual, d_own, d_other, b_own, b_other, gains, head_out, scale_row, weight)


def project_back(d_proj, weight):
    def kernel(d_ref, w_ref, part_ref):
        total = dot_nt(d_ref[0], w_ref[0])
        for group in range(1, 4):
            total = total + dot_nt(d_ref[group], w_ref[group])
        part_ref[...] = total.astype(BF16)

    return call_rows(
        kernel,
        array((1024, 1024), BF16),
        rows_spec(1024),
        [group_spec(384), fixed_spec((4, 1024, 384))],
        2 * 1024 * 1024 * 1536,
        10 * 2**20,
    )(d_proj, weight)


def entry_back(d_residual, d_own, d_other, entry, gain):
    def kernel(dr_ref, a_ref, b_ref, x_ref, gain_ref, dx_ref, sum_ref):
        clear_first(sum_ref)
        unit_x, scale_x = standard(x_ref[...].astype(F32))
        d_normed = a_ref[...].astype(F32) + b_ref[...].astype(F32)
        back, gain_first, shift_first = standard_back(unit_x, scale_x, gain_ref[...], d_normed)
        dx_ref[...] = (dr_ref[...] + back).astype(BF16)
        add_rows(sum_ref, 0, gain_first)
        add_rows(sum_ref, 1, shift_first)

    return call_rows(
        kernel,
        (array((1024, 1024), BF16), array((8, 1024), F32)),
        (rows_spec(1024), fixed_spec((8, 1024))),
        [rows_spec(1024)] * 4 + [fixed_spec((1, 1024))],
        20 * 2**20,
        15 * 2**20,
    )(d_residual, d_own, d_other, entry, gain)


def contract(left, right):
    return lax.dot_general(left, right, (((0,), (0,)), ((), ())), preferred_element_type=F32)


def layer_forward(projected, entry, weights, small, split_at):
    normed, proj = projected
    w_qkv, w_out, w_up, w_down = weights
    gains, shifts, mid_gain, mid_shift, head_scale = small
    scale_row = jnp.repeat(head_scale.reshape(8), 64)
    head_out, scaled, logs = attention(proj, split_at, scale_row.reshape(4, 1, 128))
    branch = dot(scaled, w_out).astype(BF16)
    branch_other = core_swap(branch)
    residual, ffn_input, gelu, slope, stat = widen(entry, branch, branch_other, gains, shifts, w_up)
    stat_other = core_swap(stat)
    middle, part = narrow(gelu, stat, stat_other, mid_gain, mid_shift, w_down)
    part_other = core_swap(part)
    kept = dict(
        entry=entry, normed=normed, proj=proj, head_out=head_out, scaled=scaled, logs=logs, branch=branch,
        branch_other=branch_other, residual=residual, ffn_input=ffn_input, gelu=gelu, slope=slope, stat=stat,
        stat_other=stat_other, middle=middle, scale_row=scale_row, split_at=split_at,
    )
    return residual, part, part_other, kept


def layer_backward(grad_low, weights, small, kept):
    w_qkv, w_out, w_up, w_down = weights
    gains, shifts, mid_gain, mid_shift, head_scale = small
    middle, ffn_input, normed = kept["middle"], kept["ffn_input"], kept["normed"]
    grad_down = jnp.einsum("pmk,mn->pkn", middle, grad_low, preferred_element_type=F32)
    grad_down = grad_down.astype(BF16)
    stat, stat_other = kept["stat"], kept["stat_other"]
    d_middle, sums, g_mid_gain, g_mid_shift = narrow_back(
        grad_low, kept["gelu"], stat, stat_other, mid_gain, w_down
    )
    sums_other = core_swap(sums)
    d_hidden, part = widen_back(
        d_middle, kept["gelu"], kept["slope"], stat, stat_other, sums, sums_other, mid_gain, w_up
    )
    part_other = core_swap(part)
    grad_up = jnp.einsum("mk,pmn->pkn", ffn_input, d_hidden, preferred_element_type=F32)
    grad_up = grad_up.astype(BF16).reshape(4, 4, 256, 512)
    d_residual, d_branch, d_heads, norm_sums, head_sums = norms_back(
        grad_low, kept["residual"], part, part_other, kept["branch"], kept["branch_other"], gains,
        kept["head_out"], kept["scale_row"].reshape(1, 512), w_out,
    )
    grad_out = contract(kept["scaled"], d_branch)
    grad_out = grad_out.astype(BF16).reshape(4, 128, 1024)
    d_proj = attention_back(kept["proj"], kept["split_at"], d_heads, kept["head_out"], kept["logs"])
    d_part = project_back(d_proj, w_qkv)
    d_part_other = core_swap(d_part)
    grad_qkv = jnp.einsum("mk,pmn->pkn", normed, d_proj, preferred_element_type=F32)
    grad_qkv = grad_qkv.astype(BF16).reshape(4, 4, 256, 384)
    d_x, first_sums = entry_back(d_residual, d_part, d_part_other, kept["entry"], gains[0:1])
    return d_x, (grad_qkv, grad_out, grad_up, grad_down), (first_sums, norm_sums, g_mid_gain, g_mid_shift, head_sums)


MESH = pl.DeviceIdType.MESH
SIZES = ((256, 384), (128, 256), (256, 512), (512, 256))


def partner(place, step):
    return {0: place, 1: place + 1 - 2 * lax.rem(place, 2), 2: lax.rem(place + 2, 4), 3: 3 - place}[step]


def here():
    return lax.axis_index("section"), lax.axis_index("dp"), lax.axis_index("shard")


def greet(core, place, depth):
    barrier = pltpu.get_barrier_semaphore()
    targets = [{"shard": lax.rem(depth + step, 4)} for step in (1, 2, 3)]
    targets += [{"section": 1 - core, "shard": lax.rem(depth + step, 4)} for step in range(4)]
    targets += [{"dp": partner(place, step)} for step in (1, 2, 3)]
    for target in targets:
        pl.semaphore_signal(barrier, inc=1, device_id=target, device_id_type=MESH)
    pl.semaphore_wait(barrier, len(targets))


def send(source, target, send_sem, recv_sem, device):
    copy = pltpu.make_async_remote_copy(
        src_ref=source, dst_ref=target, send_sem=send_sem, recv_sem=recv_sem,
        device_id=device, device_id_type=MESH,
    )
    copy.start()


def await_bytes(view, sem):
    pltpu.make_async_copy(view, view, sem).wait()


def lanes(start, size):
    return pl.ds(pl.multiple_of(start, 128), size)


def raw_views(raw, matrix, half, quarter):
    if matrix == 0:
        return [raw[0].at[:, lanes(third * 1024 + quarter * 256 + half * 128, 128)] for third in range(3)]
    if matrix == 1:
        return [raw[1].at[pl.ds(half * 128, 128), lanes(quarter * 256, 256)]]
    if matrix == 2:
        return [raw[2].at[:, lanes(quarter * 1024 + half * 512, 512)]]
    return [raw[3].at[pl.ds(half * 512, 512), lanes(quarter * 256, 256)]]


def whole_view(whole, matrix, quarter, shard):
    if matrix in (0, 2):
        return whole[matrix].at[quarter, shard]
    return whole[matrix].at[shard, :, lanes(quarter * 256, 256)]


def whole_views(whole, matrix, quarter, shard):
    if matrix == 0:
        return [whole[0].at[quarter, shard, :, pl.ds(third * 128, 128)] for third in range(3)]
    return [whole_view(whole, matrix, quarter, shard)]


def pieces_view(whole, matrix, first, second):
    if matrix in (0, 2):
        return whole[matrix].at[pl.ds(0, first), pl.ds(0, second)]
    return whole[matrix].at[pl.ds(0, first), :, pl.ds(0, 256 * second)]


def gather_kernel(
    items, qkv, out, up, down, gains, shifts, mid_gain, mid_shift, heads,
    entry, cotangent, wq0, wo0, wu0, wd0, wq1, wo1, wu1, wd1, gains2, shifts2, mid_gain2, mid_shift2, heads2,
    item_send, item_recv, item_pass, own_send, own_recv, deep_send, deep_recv, hop_send, hop_recv, small_sems,
):
    core, place, depth = here()
    raw = (qkv, out, up, down)
    wholes = ((wq0, wo0, wu0, wd0), (wq1, wo1, wu1, wd1))
    arrays = (entry, cotangent)
    smalls = ((gains, gains2), (shifts, shifts2), (mid_gain, mid_gain2), (mid_shift, mid_shift2), (heads, heads2))
    greet(core, place, depth)

    for layer in (0, 1):
        @pl.when(core == layer)
        def unused():
            for step in (1, 2, 3):
                send(items.at[partner(place, step)], arrays[layer].at[place], item_send.at[layer, step],
                     item_recv.at[layer, step], {"dp": partner(place, step)})
            pltpu.make_async_copy(items.at[place], arrays[layer].at[place], item_send.at[layer, 0]).start()
            send(items.at[place], arrays[layer].at[place], item_pass.at[layer, 0], item_recv.at[layer, 0],
                 {"section": 1 - layer})
            for index, (source, target) in enumerate(smalls):
                pltpu.make_async_copy(source, target.at[layer], small_sems.at[0, index]).start()
                send(source, target.at[layer], small_sems.at[1, index], small_sems.at[2, index],
                     {"section": 1 - layer})

    units = [(layer, matrix) for layer in (0, 1) for matrix in range(4)]

    def deep(unit):
        layer, matrix = units[unit]

        @pl.when(core == layer)
        def unused():
            for step in (1, 2, 3):
                for half in (0, 1):
                    for source, target in zip(
                        raw_views(raw, matrix, half, place), whole_views(wholes[layer], matrix, place, depth)
                    ):
                        send(source, target, deep_send.at[unit], deep_recv.at[unit, step],
                             {"section": half, "shard": lax.rem(depth + 4 - step, 4)})

    def own(unit):
        layer, matrix = units[unit]

        @pl.when(core == layer)
        def unused():
            for quarter in range(4):
                for source, target in zip(
                    raw_views(raw, matrix, layer, quarter), whole_views(wholes[layer], matrix, quarter, depth)
                ):
                    pltpu.make_async_copy(source, target, own_send.at[unit, 0]).start()
                for source, target in zip(
                    raw_views(raw, matrix, 1 - layer, quarter), whole_views(wholes[layer], matrix, quarter, depth)
                ):
                    send(source, target, own_send.at[unit, 1], own_recv.at[unit], {"section": 1 - layer})

    def route(unit, step):
        return (1, 2) if (unit + step) % 2 == 0 else (2, 1)

    def piece(unit, offset, step):
        layer, matrix = units[unit]
        return whole_view(wholes[layer], matrix, partner(place, offset), lax.rem(depth + step, 4))

    def spread_first(unit):
        for step in (1, 2, 3):
            first, second = route(unit, step)
            await_bytes(piece(unit, 0, step), deep_recv.at[unit, step])
            for offset in (first, second):
                send(piece(unit, 0, step), piece(unit, 0, step), hop_send.at[unit], hop_recv.at[unit, step - 1, offset - 1],
                     {"dp": partner(place, offset)})

    def spread_second(unit):
        for step in (1, 2, 3):
            first, second = route(unit, step)
            await_bytes(piece(unit, first, step), hop_recv.at[unit, step - 1, first - 1])
            send(piece(unit, first, step), piece(unit, first, step), hop_send.at[unit], hop_recv.at[unit, step - 1, 2],
                 {"dp": partner(place, second)})

    deep(0)
    deep(1)
    own(0)
    own(1)
    for unit in range(8):
        if unit + 2 < 8:
            deep(unit + 2)
        spread_first(unit)
        if unit + 2 < 8:
            own(unit + 2)
        if unit >= 1:
            spread_second(unit - 1)
        if unit in (0, 1):
            layer = unit

            @pl.when(core == layer)
            def unused():
                for step in (1, 2, 3):
                    block = arrays[layer].at[partner(place, step)]
                    await_bytes(block, item_recv.at[layer, step])
                    send(block, block, item_pass.at[layer, step], item_recv.at[layer, step], {"section": 1 - layer})

    spread_second(7)

    for layer in (0, 1):
        @pl.when(core == layer)
        def unused():
            for step in range(4):
                await_bytes(items.at[0], item_send.at[layer, step])
                await_bytes(items.at[0], item_pass.at[layer, step])
            for index, (source, target) in enumerate(smalls):
                await_bytes(source, small_sems.at[0, index])
                await_bytes(source, small_sems.at[1, index])

        @pl.when(core != layer)
        def unused_too():
            for step in range(4):
                await_bytes(items.at[0], item_recv.at[layer, step])
            for index, (source, target) in enumerate(smalls):
                await_bytes(source, small_sems.at[2, index])

    for unit, (layer, matrix) in enumerate(units):
        whole = wholes[layer]
        quarters = pieces_view(whole, matrix, 2, 2)

        @pl.when(core == layer)
        def unused():
            await_bytes(quarters, own_send.at[unit, 0])
            await_bytes(quarters, own_send.at[unit, 1])
            await_bytes(pieces_view(whole, matrix, 3, 2), deep_send.at[unit])

        @pl.when(core != layer)
        def unused_too():
            await_bytes(quarters, own_recv.at[unit])

        for step in (1, 2, 3):
            first, second = route(unit, step)
            await_bytes(piece(unit, 0, 0), hop_recv.at[unit, step - 1, second - 1])
            await_bytes(piece(unit, 0, 0), hop_recv.at[unit, step - 1, 2])
        await_bytes(pieces_view(whole, matrix, 3, 3), hop_send.at[unit])


def gather_all(*operands):
    weights = (
        array((4, 4, 256, 384), BF16),
        array((4, 128, 1024), BF16),
        array((4, 4, 256, 512), BF16),
        array((4, 512, 1024), BF16),
    )
    shapes = (array((4, 256, 1024), BF16),) * 2 + weights * 2
    shapes += tuple(array((2,) + operand.shape, F32) for operand in operands[5:])
    anywhere = pl.BlockSpec(memory_space=pl.ANY)
    dma = pltpu.SemaphoreType.DMA
    return pl.pallas_call(
        gather_kernel,
        in_specs=[anywhere] * len(operands),
        out_specs=[anywhere] * len(shapes),
        out_shape=shapes,
        scratch_shapes=[
            dma((2, 4)), dma((2, 4)), dma((2, 4)), dma((8, 2)), dma((8,)),
            dma((8,)), dma((8, 4)), dma((8,)), dma((8, 3, 3)), dma((3, 5)),
        ],
        compiler_params=pltpu.CompilerParams(collective_id=0, has_side_effects=True),
    )(*operands)


ORDER = tuple((layer, matrix) for layer in (1, 0) for matrix in (3, 2, 1, 0))


def add_up_into(target, *terms):
    rows = target.shape[0]

    def step(index, unused):
        span = pl.ds(pl.multiple_of(index * 32, 32), 32)
        total = target[span, :].astype(F32)
        for term in terms:
            total = total + term[span, :].astype(F32)
        target[span, :] = total.astype(BF16)
        return unused

    lax.fori_loop(0, rows // 32, step, 0)


def reduce_kernel(*refs):
    grads = (refs[0:4], refs[4:8])
    smalls = (refs[8:13], refs[13:18])
    ends_in = (refs[18], refs[19])
    shares = refs[20:24]
    ends, small_out = refs[24:26]
    own, first_in, second_in, deep_in = refs[26:30], refs[30:34], refs[34:38], refs[38:42]
    vec, inbox, acc = refs[42:45]
    (load_sem, first_send, first_recv, second_send, second_recv, deep_send, deep_recv, last_send, last_copy,
     last_recv, ends_send, ends_recv, small_send, small_recv) = refs[45:]
    core, place, depth = here()
    greet(core, place, depth)

    for layer in (0, 1):
        @pl.when(core == layer)
        def unused():
            source = ends_in[layer]
            for step in (1, 2, 3):
                send(source.at[partner(place, step)], ends.at[place], ends_send.at[step], ends_recv.at[step],
                     {"dp": partner(place, step)})
            pltpu.make_async_copy(source.at[place], ends.at[place], ends_send.at[0]).start()

    def route(step):
        return (1, 2) if step < 2 else (2, 1)

    def shard_of(step):
        return lax.rem(depth + step, 4)

    def begin(unit):
        layer, matrix = ORDER[unit]
        for step in range(4):
            first, second = route(step)
            for index, offset in enumerate((first, 3)):
                send(whole_view(grads[layer], matrix, partner(place, offset), shard_of(step)),
                     first_in[matrix].at[layer, step, index], first_send.at[unit], first_recv.at[unit],
                     {"dp": partner(place, first)})
            for index, offset in enumerate((0, second)):
                pltpu.make_async_copy(
                    whole_view(grads[layer], matrix, partner(place, offset), shard_of(step)),
                    own[matrix].at[layer, step, index], load_sem.at[unit],
                ).start()

    def second_hop(unit):
        layer, matrix = ORDER[unit]
        await_bytes(own[matrix].at[layer], load_sem.at[unit])
        await_bytes(first_in[matrix].at[layer], first_recv.at[unit])
        for step in range(4):
            first, second = route(step)
            mine = own[matrix].at[layer, step, 1]
            add_up_into(mine, first_in[matrix].at[layer, step, 1])
            send(mine, second_in[matrix].at[layer, step], second_send.at[unit], second_recv.at[unit],
                 {"dp": partner(place, second)})

    def deep_hop(unit):
        layer, matrix = ORDER[unit]
        await_bytes(second_in[matrix].at[layer], second_recv.at[unit])
        for step in (1, 2, 3, 0):
            mine = own[matrix].at[layer, step, 0]
            add_up_into(mine, first_in[matrix].at[layer, step, 0], second_in[matrix].at[layer, step])
            if step:
                send(mine, deep_in[matrix].at[layer, step - 1], deep_send.at[unit], deep_recv.at[unit],
                     {"shard": shard_of(step)})

    def finish(unit):
        layer, matrix = ORDER[unit]
        await_bytes(deep_in[matrix].at[layer], deep_recv.at[unit])
        mine = own[matrix].at[layer, 0, 0]
        add_up_into(mine, *[deep_in[matrix].at[layer, index] for index in range(3)])
        sources = [mine]
        if matrix == 0:
            sources = [mine.at[:, pl.ds(third * 128, 128)] for third in range(3)]
        for half in (0, 1):
            @pl.when(core == half)
            def unused():
                for source, target in zip(sources, raw_views(shares, matrix, half, place)):
                    if half == layer:
                        pltpu.make_async_copy(source, target, last_copy.at[unit]).start()
                        for offset in (1, 2):
                            send(source, target, last_send.at[unit, 0], last_recv.at[unit, half, offset],
                                 {"dp": partner(place, offset)})
                    else:
                        send(source, target, last_send.at[unit, 0], last_recv.at[unit, half, 0], {"section": layer})

    def forward(unit):
        layer, matrix = ORDER[unit]
        half = 1 - layer

        @pl.when(core == layer)
        def unused():
            views = raw_views(shares, matrix, half, place)
            await_bytes(own[matrix].at[layer, 0, 0], last_recv.at[unit, half, 0])
            for view in views:
                for offset in (1, 2):
                    send(view, view, last_send.at[unit, 1], last_recv.at[unit, half, offset],
                         {"dp": partner(place, offset)})

    def corner(unit):
        layer, matrix = ORDER[unit]

        @pl.when(core == layer)
        def unused():
            for half in (layer, 1 - layer):
                first, second = (1, 2) if half == 0 else (2, 1)
                await_bytes(own[matrix].at[layer, 0, 0], last_recv.at[unit, half, first])
                for view in raw_views(shares, matrix, half, partner(place, first)):
                    send(view, view, last_send.at[unit, 2], last_recv.at[unit, half, 3], {"dp": partner(place, second)})

    def clean(unit):
        layer, matrix = ORDER[unit]
        sample = own[matrix].at[layer, 0, 0]
        await_bytes(first_in[matrix].at[layer], first_send.at[unit])
        await_bytes(second_in[matrix].at[layer], second_send.at[unit])
        await_bytes(deep_in[matrix].at[layer], deep_send.at[unit])

        @pl.when(core == layer)
        def unused():
            await_bytes(sample, last_copy.at[unit])
            for row in range(3):
                await_bytes(own[matrix].at[layer, 0], last_send.at[unit, row])
            for half in (0, 1):
                first, second = (1, 2) if half == 0 else (2, 1)
                await_bytes(sample, last_recv.at[unit, half, second])
                await_bytes(sample, last_recv.at[unit, half, 3])

        @pl.when(core != layer)
        def unused_too():
            await_bytes(sample, last_send.at[unit, 0])

    vec[...] = jnp.zeros_like(vec)
    column = pl.ds(pl.multiple_of(core * 512, 512), 512)
    for layer in (0, 1):
        entry_sums, norm_sums, mid_gain, mid_shift, heads = smalls[layer]

        @pl.when(core == layer)
        def unused():
            vec[layer, 0:1, :] = entry_sums[0:1, :]
            vec[layer, 1:3, :] = norm_sums[0:2, :]
            vec[layer, 3:4, :] = entry_sums[1:2, :]
            vec[layer, 4:6, :] = norm_sums[2:4, :]

        vec[layer, 6:10, column] = mid_gain[...]
        vec[layer, 10:14, column] = mid_shift[...]
        vec[layer, 14:15, column] = heads[0:1, :]

    exchanges = (
        {"section": 1 - core},
        {"dp": partner(place, 1)},
        {"dp": partner(place, 2)},
        {"shard": partner(depth, 1)},
        {"shard": partner(depth, 2)},
    )

    def small_step(index):
        if index:
            source = acc.at[index - 1]
            send(source, inbox.at[index], small_send.at[index], small_recv.at[index], exchanges[index])
        else:
            for half in (0, 1):
                @pl.when(core == half)
                def unused():
                    send(vec.at[1 - half], inbox.at[0], small_send.at[0], small_recv.at[0], exchanges[0])

    def small_take(index):
        await_bytes(inbox.at[index], small_recv.at[index])
        if index:
            acc[index] = acc[index - 1] + inbox[index]
        else:
            for half in (0, 1):
                @pl.when(core == half)
                def unused():
                    acc[0] = vec[half] + inbox[0]

    begin(0)
    begin(1)
    small_step(0)
    for turn in range(12):
        if turn + 2 < 8:
            begin(turn + 2)
        if turn < 8:
            second_hop(turn)
        if 0 <= turn - 1 < 8:
            deep_hop(turn - 1)
        if 0 <= turn - 2 < 8:
            finish(turn - 2)
        if 0 <= turn - 3 < 8:
            forward(turn - 3)
        if 0 <= turn - 4 < 8:
            corner(turn - 4)
        if turn < 5:
            small_take(turn)
            if turn < 4:
                small_step(turn + 1)
    small_out[...] = acc[4]
    for unit in range(8):
        clean(unit)
    for index in range(5):
        await_bytes(inbox.at[index], small_send.at[index])
    for step in range(4):
        await_bytes(ends.at[0], ends_send.at[step])
    for step in (1, 2, 3):
        await_bytes(ends.at[0], ends_recv.at[step])


def reduce_all(grads, smalls, ends):
    anywhere = pl.BlockSpec(memory_space=pl.ANY)
    local = pl.BlockSpec(memory_space=pltpu.VMEM)
    dma = pltpu.SemaphoreType.DMA
    operands = (*grads[0], *grads[1], *smalls[0], *smalls[1], *ends)
    return pl.pallas_call(
        reduce_kernel,
        in_specs=[anywhere] * 8 + [local] * 10 + [anywhere] * 2,
        out_specs=[anywhere] * 5 + [local],
        out_shape=(
            array((256, 3072), BF16),
            array((256, 1024), BF16),
            array((256, 4096), BF16),
            array((1024, 1024), BF16),
            array((4, 256, 1024), BF16),
            array((16, 1024), F32),
        ),
        scratch_shapes=[pltpu.VMEM((2, 4, 2) + size, BF16) for size in SIZES]
        + [pltpu.VMEM((2, 4, 2) + size, BF16) for size in SIZES]
        + [pltpu.VMEM((2, 4) + size, BF16) for size in SIZES]
        + [pltpu.VMEM((2, 3) + size, BF16) for size in SIZES]
        + [pltpu.VMEM((2, 16, 1024), F32), pltpu.VMEM((5, 16, 1024), F32), pltpu.VMEM((5, 16, 1024), F32)]
        + [dma((8,))] * 7
        + [dma((8, 3)), dma((8,)), dma((8, 2, 4)), dma((4,)), dma((4,)), dma((5,)), dma((5,))],
        compiler_params=pltpu.CompilerParams(
            collective_id=1, has_side_effects=True, vmem_limit_bytes=VMEM_BYTES
        ),
    )(*operands)


def local(
    boundary,
    first_len,
    qkv_weight,
    out_weight,
    up_weight,
    down_weight,
    norm_gain,
    norm_shift,
    mid_gain,
    mid_shift,
    head_scale,
):
    core = lax.axis_index("section")
    split_at = pick(first_len, lax.axis_index("dp"))
    (x, cotangent, wq0, wo0, wu0, wd0, wq1, wo1, wu1, wd1, gains, shifts, mid_gains, mid_shifts, heads) = gather_all(
        boundary[0, :, 0], qkv_weight[0], out_weight[0], up_weight[0], down_weight[0],
        norm_gain[0], norm_shift[0], mid_gain, mid_shift, head_scale,
    )
    x, cotangent = x.reshape(1024, 1024), cotangent.reshape(1024, 1024)
    weights = [
        (wq.reshape(4, 1024, 384), wo.reshape(512, 1024), wu.reshape(4, 1024, 512), wd)
        for wq, wo, wu, wd in ((wq0, wo0, wu0, wd0), (wq1, wo1, wu1, wd1))
    ]

    def own_half(value):
        return lax.dynamic_index_in_dim(value, core, 2, keepdims=False)

    mid_gains = own_half(mid_gains.reshape(2, 4, 2, 512))
    mid_shifts = own_half(mid_shifts.reshape(2, 4, 2, 512))
    heads = own_half(heads.reshape(2, 4, 2, 2))
    smalls = [
        (gains[layer], shifts[layer], mid_gains[layer], mid_shifts[layer], heads[layer]) for layer in (0, 1)
    ]
    projected = project(x, gains[0, 0:1], shifts[0, 0:1], weights[0][0])
    residual, part, part_other, kept_first = layer_forward(projected, x, weights[0], smalls[0], split_at)
    between, normed, proj = project_next(
        residual, part, part_other, gains[1, 0:1], shifts[1, 0:1], weights[1][0]
    )
    residual, part, part_other, kept_second = layer_forward(
        (normed, proj), between, weights[1], smalls[1], split_at
    )
    output = (residual + (part.astype(F32) + part_other.astype(F32))).astype(BF16)
    d_between, big_second, small_second = layer_backward(cotangent, weights[1], smalls[1], kept_second)
    d_x, big_first, small_first = layer_backward(d_between, weights[0], smalls[0], kept_first)
    *shares, ends, totals = reduce_all(
        (big_first, big_second),
        (small_first, small_second),
        (d_x.reshape(4, 256, 1024), output.reshape(4, 256, 1024)),
    )
    head_sums = jnp.sum(totals[14].reshape(2, 4, 2, 64), axis=3).transpose(1, 0, 2).reshape(1, 16)
    return (
        ends[None, :, None],
        *[share.astype(F32)[None] for share in shares],
        totals[0:3][None],
        totals[3:6][None],
        totals[6:10].reshape(1, 4096),
        totals[10:14].reshape(1, 4096),
        head_sums,
    )


def fits(mesh, boundary, mid_gain, head_scale):
    sizes = (mesh.shape["section"], mesh.shape["dp"], mesh.shape["shard"])
    return (
        sizes == (2, 4, 4)
        and boundary == (2, 4, 4, 1024, 1024)
        and mid_gain == (2, 4096)
        and head_scale == (2, 16)
    )


def solution(mesh):
    placed = (
        P("section", None, "shard", "dp", None),
        P(None, "shard"),
        P("section", "shard", None),
        P("section", "shard", None),
        P("section", "shard", None),
        P("section", "shard", None),
        P("section", None, None),
        P("section", None, None),
        P("section", None),
        P("section", None),
        P("section", None),
    )
    results = (
        P("section", None, "shard", "dp", None),
        P("section", "shard", None),
        P("section", "shard", None),
        P("section", "shard", None),
        P("section", "shard", None),
        P("section", None, None),
        P("section", None, None),
        P("section", None),
        P("section", None),
        P("section", None),
    )

    def whole(*arrays):
        fast = fits(mesh, arrays[0].shape, arrays[8].shape, arrays[10].shape)
        body = local if fast else general
        return jax.shard_map(
            body, mesh=mesh, in_specs=placed, out_specs=results, check_vma=False
        )(*arrays)

    return whole
```

```python
import math
from typing import NamedTuple

import jax
import jax.numpy as jnp
from jax import lax
from jax.experimental import pallas as pl
from jax.experimental.pallas import tpu as pltpu
from jax.sharding import PartitionSpec as P

EPSILON = 1e-05


def shifted(value, axis, steps):
    count = lax.axis_size(axis)
    first, last = (max(0, -steps), min(count, count - steps))
    return lax.ppermute(value, axis, [(source, source + steps) for source in range(first, last)])


def normalize(values_in, gain, shift):
    centre = values_in - jnp.mean(values_in, axis=-1, keepdims=True)
    spread = jnp.mean(centre * centre, axis=-1, keepdims=True)
    return centre * lax.rsqrt(spread + EPSILON) * gain + shift


def middle_norm(hidden, mid_gain, mid_shift):
    return normalize(jax.nn.gelu(hidden, approximate=False), mid_gain, mid_shift)


def contract_rows(left, right):
    return lax.dot_general(
        left, right, (((0,), (0,)), ((), ())), preferred_element_type=jnp.float32
    )


def contract_cols(left, right):
    return lax.dot_general(
        left, right, (((1,), (1,)), ((), ())), preferred_element_type=jnp.float32
    )


def visible(query_place, key_place, split_at):
    same_doc = (query_place[:, None] < split_at) == (key_place[None, :] < split_at)
    return same_doc & (key_place[None, :] <= query_place[:, None])


def forward_parts(stream_in, weights, small, split_at, head_count):
    weight_qkv, weight_out, weight_up, weight_down = weights
    gains, shifts, mid_gain, mid_shift, head_scale = small
    row_count, model_width = stream_in.shape
    head_dim = model_width // head_count
    factor = 1.0 / math.sqrt(head_dim)
    normed = normalize(stream_in, gains[0], shifts[0]).astype(jnp.bfloat16)
    projected = jnp.dot(normed, weight_qkv, preferred_element_type=jnp.float32).astype(jnp.bfloat16)
    queries = projected[:, :model_width].reshape(row_count, head_count, head_dim)
    key_rows = projected[:, model_width : 2 * model_width].reshape(row_count, head_count, head_dim)
    value_rows = projected[:, 2 * model_width :].reshape(row_count, head_count, head_dim)
    keys_all, values_all = (
        lax.all_gather(key_rows, "dp", axis=0, tiled=True),
        lax.all_gather(value_rows, "dp", axis=0, tiled=True),
    )
    seq_len = keys_all.shape[0]
    own_place = lax.axis_index("dp") * row_count + jnp.arange(row_count, dtype=jnp.int32)
    all_place = jnp.arange(seq_len, dtype=jnp.int32)
    allowed = visible(own_place, all_place, split_at)
    scores = (
        jnp.einsum("qhd,khd->hqk", queries, keys_all, preferred_element_type=jnp.float32) * factor
    )
    scores = jnp.where(allowed[None], scores, -1e30)
    row_max = jnp.max(scores, axis=-1, keepdims=True)
    log_total = row_max + jnp.log(jnp.sum(jnp.exp(scores - row_max), axis=-1, keepdims=True))
    attend = jnp.exp(scores - log_total)
    attend_low = attend.astype(jnp.bfloat16)
    head_out = jnp.einsum(
        "hqk,khd->qhd", attend_low, values_all, preferred_element_type=jnp.float32
    )
    scaled = (
        (head_out * head_scale[None, :, None]).astype(jnp.bfloat16).reshape(row_count, model_width)
    )
    branch = jnp.dot(scaled, weight_out, preferred_element_type=jnp.float32)
    residual = stream_in + normalize(branch, gains[1], shifts[1])
    ffn_input = normalize(residual, gains[2], shifts[2]).astype(jnp.bfloat16)
    hidden = jnp.dot(ffn_input, weight_up, preferred_element_type=jnp.float32)
    middle = middle_norm(hidden, mid_gain, mid_shift).astype(jnp.bfloat16)
    return dict(
        normed=normed,
        queries=queries,
        key_rows=key_rows,
        value_rows=value_rows,
        keys_all=keys_all,
        values_all=values_all,
        own_place=own_place,
        all_place=all_place,
        attend=attend,
        attend_low=attend_low,
        log_total=log_total,
        head_out=head_out,
        scaled=scaled,
        branch=branch,
        residual=residual,
        ffn_input=ffn_input,
        hidden=hidden,
        middle=middle,
        factor=factor,
    )


def backward_parts(stream_in, grad_in, weights, small, split_at, head_count):
    weight_qkv, weight_out, weight_up, weight_down = weights
    gains, shifts, mid_gain, mid_shift, head_scale = small
    parts = forward_parts(stream_in, weights, small, split_at, head_count)
    row_count, model_width = stream_in.shape
    head_dim = model_width // head_count
    factor = parts["factor"]
    grad_down = contract_rows(parts["middle"], grad_in)
    d_middle = contract_cols(grad_in, weight_down)
    unused, pull_middle = jax.vjp(middle_norm, parts["hidden"], mid_gain, mid_shift)
    d_hidden, grad_mid_gain, grad_mid_shift = pull_middle(d_middle)
    d_hidden = d_hidden.astype(jnp.bfloat16)
    grad_up = contract_rows(parts["ffn_input"], d_hidden)
    d_ffn_input = contract_cols(d_hidden, weight_up)
    unused, pull_third = jax.vjp(normalize, parts["residual"], gains[2], shifts[2])
    d_residual, gain_third, shift_third = pull_third(d_ffn_input)
    d_residual = d_residual + grad_in.astype(jnp.float32)
    unused, pull_second = jax.vjp(normalize, parts["branch"], gains[1], shifts[1])
    d_branch, gain_second, shift_second = pull_second(d_residual)
    d_branch = d_branch.astype(jnp.bfloat16)
    grad_out = contract_rows(parts["scaled"], d_branch)
    d_scaled = contract_cols(d_branch, weight_out).reshape(row_count, head_count, head_dim)
    grad_head_scale = jnp.sum(d_scaled * parts["head_out"], axis=(0, 2))
    d_heads = (d_scaled * head_scale[None, :, None]).astype(jnp.bfloat16)
    attend = parts["attend"]
    d_attend = jnp.einsum(
        "qhd,khd->hqk", d_heads, parts["values_all"], preferred_element_type=jnp.float32
    )
    row_dot = jnp.sum(attend * d_attend, axis=-1, keepdims=True)
    d_scores = (attend * (d_attend - row_dot)).astype(jnp.bfloat16)
    d_query = (
        jnp.einsum("hqk,khd->qhd", d_scores, parts["keys_all"], preferred_element_type=jnp.float32)
        * factor
    ).astype(jnp.bfloat16)
    full_keys = (
        jnp.einsum("hqk,qhd->khd", d_scores, parts["queries"], preferred_element_type=jnp.float32)
        * factor
    )
    full_values = jnp.einsum(
        "hqk,qhd->khd", parts["attend_low"], d_heads, preferred_element_type=jnp.float32
    )
    d_keys, d_values = (
        lax.psum_scatter(full_keys, "dp", scatter_dimension=0, tiled=True),
        lax.psum_scatter(full_values, "dp", scatter_dimension=0, tiled=True),
    )
    d_projected = jnp.concatenate(
        [
            d_query.reshape(row_count, model_width),
            d_keys.astype(jnp.bfloat16).reshape(row_count, model_width),
            d_values.astype(jnp.bfloat16).reshape(row_count, model_width),
        ],
        axis=1,
    )
    grad_qkv = contract_rows(parts["normed"], d_projected)
    d_normed = contract_cols(d_projected, weight_qkv)
    unused, pull_first = jax.vjp(normalize, stream_in, gains[0], shifts[0])
    d_entry, gain_first, shift_first = pull_first(d_normed)
    d_entry = d_entry + d_residual
    big_grads = (grad_qkv, grad_out, grad_up, grad_down)
    small_grads = (
        jnp.stack([gain_first, gain_second, gain_third]),
        jnp.stack([shift_first, shift_second, shift_third]),
        grad_mid_gain,
        grad_mid_shift,
        grad_head_scale,
    )
    return (d_entry, big_grads, small_grads)


def add_up(first_term, second_term):
    return first_term + second_term


def general(
    boundary,
    first_len,
    qkv_weight,
    out_weight,
    up_weight,
    down_weight,
    norm_gain,
    norm_shift,
    mid_gain,
    mid_shift,
    head_scale,
):
    section_index = lax.axis_index("section")
    gathered = (
        lax.all_gather(qkv_weight, "shard", axis=1, tiled=True),
        lax.all_gather(out_weight, "shard", axis=1, tiled=True),
        lax.all_gather(up_weight, "shard", axis=1, tiled=True),
        lax.all_gather(down_weight, "shard", axis=1, tiled=True),
    )
    weights = tuple((piece[0] for piece in gathered))
    small = (norm_gain[0], norm_shift[0], mid_gain[0], mid_shift[0], head_scale[0])
    head_count = head_scale.shape[1]
    micro = boundary.shape[1]
    row_count = boundary.shape[3]
    model_width = boundary.shape[4]
    local_ends = boundary[0, :, 0]
    splits = first_len[:, 0]

    def forward_tick(step_index, carry):
        incoming, kept, ends = carry
        index = step_index - section_index
        active = (index >= 0) & (index < micro)
        slot = jnp.clip(index, 0, micro - 1)
        entry = jnp.where(section_index == 0, local_ends[slot], incoming)
        parts = forward_parts(entry.astype(jnp.float32), weights, small, splits[slot], head_count)
        result = (
            parts["residual"]
            + jnp.dot(parts["middle"], weights[3], preferred_element_type=jnp.float32)
        ).astype(jnp.bfloat16)
        kept = kept.at[slot].set(jnp.where(active, entry, kept[slot]))
        ends = ends.at[slot].set(jnp.where(active, result, ends[slot]))
        incoming = shifted(result, "section", 1)
        return (incoming, kept, ends)

    blank = jnp.zeros((row_count, model_width), jnp.bfloat16)
    stack_blank = jnp.zeros((micro, row_count, model_width), jnp.bfloat16)
    unused, kept, ends = lax.fori_loop(
        0, micro + 1, forward_tick, (blank, stack_blank, stack_blank)
    )

    def backward_tick(step_index, carry):
        incoming, ends, big_sums, small_sums = carry
        index = micro - step_index - section_index
        active = (index >= 0) & (index < micro)
        slot = jnp.clip(index, 0, micro - 1)
        grad_in = jnp.where(section_index == 1, local_ends[slot], incoming)
        grad_in = jnp.where(active, grad_in, jnp.zeros_like(grad_in))
        d_entry, big_grads, small_grads = backward_parts(
            kept[slot].astype(jnp.float32), grad_in, weights, small, splits[slot], head_count
        )
        d_low = d_entry.astype(jnp.bfloat16)
        ends = ends.at[slot].set(jnp.where(active & (section_index == 0), d_low, ends[slot]))
        big_sums = jax.tree.map(add_up, big_sums, big_grads)
        small_sums = jax.tree.map(add_up, small_sums, small_grads)
        incoming = shifted(d_low, "section", -1)
        return (incoming, ends, big_sums, small_sums)

    big_zero = tuple((jnp.zeros(item.shape, jnp.float32) for item in weights))
    small_zero = tuple((jnp.zeros(item.shape, jnp.float32) for item in small))
    unused, ends, big_sums, small_sums = lax.fori_loop(
        0, micro + 1, backward_tick, (blank, ends, big_zero, small_zero)
    )
    shares = (
        lax.psum_scatter(big_sums[0][None], "shard", scatter_dimension=1, tiled=True),
        lax.psum_scatter(big_sums[1][None], "shard", scatter_dimension=1, tiled=True),
        lax.psum_scatter(big_sums[2][None], "shard", scatter_dimension=1, tiled=True),
        lax.psum_scatter(big_sums[3][None], "shard", scatter_dimension=1, tiled=True),
    )
    shares = lax.psum((shares[0], shares[1], shares[2], shares[3]), "dp")
    totals = lax.psum(
        (small_sums[0], small_sums[1], small_sums[2], small_sums[3], small_sums[4]), ("dp", "shard")
    )
    return (
        ends[None, :, None],
        shares[0],
        shares[1],
        shares[2],
        shares[3],
        totals[0][None],
        totals[1][None],
        totals[2][None],
        totals[3][None],
        totals[4][None],
    )


def pick(value, index):
    return lax.dynamic_index_in_dim(value, index, 0, keepdims=False)


BF16 = jnp.bfloat16
F32 = jnp.float32
TILE = 256
VMEM_BYTES = 56 * 2**20
SECTION, DP, SHARD = "section", "dp", "shard"


def rows_spec(columns):
    return pl.BlockSpec((TILE, columns), lambda step: (step, 0))


def group_spec(columns):
    return pl.BlockSpec((4, TILE, columns), lambda step: (0, step, 0))


def array(shape, dtype):
    return jax.ShapeDtypeStruct(shape, dtype)


def dot(left, right):
    return jnp.dot(left, right, preferred_element_type=F32)


def dot_nt(left, right):
    return lax.dot_general(left, right, (((1,), (1,)), ((), ())), preferred_element_type=F32)


def standard(values_in):
    centre = values_in - jnp.mean(values_in, axis=-1, keepdims=True)
    spread_of = jnp.mean(centre * centre, axis=-1, keepdims=True)
    scale = lax.rsqrt(spread_of + EPSILON)
    return centre * scale, scale


def standard_back(unit_values, scale, gain, grad):
    inner = grad * gain
    first = jnp.mean(inner, axis=-1, keepdims=True)
    second = jnp.mean(inner * unit_values, axis=-1, keepdims=True)
    back = scale * (inner - first - unit_values * second)
    return back, jnp.sum(grad * unit_values, axis=0, keepdims=True), jnp.sum(grad, axis=0, keepdims=True)


def lane_masks(rows):
    lanes = lax.broadcasted_iota(jnp.int32, (rows, 128), 1)
    return lanes < 64


def fill_bias(bias_ref, split_at):
    for block in range(4):
        keys = lax.broadcasted_iota(jnp.int32, (256, 1024), 0) + block * 256
        queries = lax.broadcasted_iota(jnp.int32, (256, 1024), 1)
        allowed = ((queries < split_at) == (keys < split_at)) & (keys <= queries)
        bias_ref[pl.ds(block * 256, 256), :] = jnp.where(allowed, 0.0, -1e30)


def two_columns(first, second):
    return jnp.where(lane_masks(first.shape[0]), first, second)


def mid_stats(own, other):
    mean_own, mean_other = own[:, 0:1], other[:, 0:1]
    gap = mean_own - mean_other
    spread_of = 0.5 * (own[:, 64:65] + other[:, 64:65]) + 0.25 * gap * gap
    return 0.5 * (mean_own + mean_other), lax.rsqrt(spread_of + EPSILON)


def attend(q_ref, k_ref, v_ref, scale_row, out_ref, scaled_ref, log_ref, bias_ref, turned_ref):
    turned_ref[...] = v_ref[0].astype(F32).T.astype(BF16)
    low_lanes = lane_masks(256)
    for block in range(4):
        seen = (block + 1) * 256
        span = pl.ds(block * 256, 256)
        q = q_ref[0, span, :] * 0.125
        keys = k_ref[0, pl.ds(0, seen), :]
        halves_out = []
        for half in range(2):
            q_half = jnp.where(low_lanes if half == 0 else ~low_lanes, q, 0.0).astype(BF16)
            scores = dot_nt(keys, q_half) + bias_ref[pl.ds(0, seen), span]
            top = jnp.max(scores, axis=0, keepdims=True)
            powers = jnp.exp(scores - top)
            total = jnp.sum(powers, axis=0, keepdims=True)
            log_ref[0, half : half + 1, span] = top + jnp.log(total)
            mixed = dot(turned_ref[half * 64 : half * 64 + 64, :seen], powers.astype(BF16))
            halves_out.append(mixed * (1.0 / total))
        head_out = jnp.concatenate(halves_out, axis=0).T
        out_ref[span, :] = head_out.astype(BF16)
        scaled_ref[span, :] = (head_out * scale_row).astype(BF16)


def attend_back(q_ref, k_ref, v_ref, grad_ref, out_ref, log_ref, back_ref, bias_ref, turned_ref, dk_ref, dv_ref):
    turned_ref[...] = k_ref[0].astype(F32).T.astype(BF16)
    dk_ref[...] = jnp.zeros_like(dk_ref)
    dv_ref[...] = jnp.zeros_like(dv_ref)
    low_lanes = lane_masks(256)
    for block in range(4):
        seen = (block + 1) * 256
        span = pl.ds(block * 256, 256)
        q = q_ref[0, span, :] * 0.125
        grad = grad_ref[span, :]
        product = (grad.astype(F32) * out_ref[span, :].astype(F32)).T
        keys = k_ref[0, pl.ds(0, seen), :]
        values = v_ref[0, pl.ds(0, seen), :]
        dq_halves, lows, d_scores_all, q_halves, grad_halves = [], [], [], [], []
        for half in range(2):
            mask = low_lanes if half == 0 else ~low_lanes
            q_half = jnp.where(mask, q, 0.0).astype(BF16)
            grad_half = jnp.where(mask, grad, 0.0).astype(BF16)
            row_dot = jnp.sum(product[half * 64 : half * 64 + 64, :], axis=0, keepdims=True)
            scores = dot_nt(keys, q_half) + bias_ref[pl.ds(0, seen), span]
            attend = jnp.exp(scores - log_ref[0, half : half + 1, span])
            d_attend = dot_nt(values, grad_half)
            d_scores = (attend * (d_attend - row_dot)).astype(BF16)
            dq_halves.append(dot(turned_ref[half * 64 : half * 64 + 64, :seen], d_scores))
            lows.append(attend.astype(BF16))
            d_scores_all.append(d_scores)
            q_halves.append(q_half)
            grad_halves.append(grad_half)
        dv_ref[pl.ds(0, seen), :] += dot(jnp.concatenate(lows, axis=1), jnp.concatenate(grad_halves, axis=0))
        dk_ref[pl.ds(0, seen), :] += dot(jnp.concatenate(d_scores_all, axis=1), jnp.concatenate(q_halves, axis=0))
        back_ref[0, span, 0:128] = (jnp.concatenate(dq_halves, axis=0).T * 0.125).astype(BF16)
    back_ref[0, :, 128:256] = dk_ref[...].astype(BF16)
    back_ref[0, :, 256:384] = dv_ref[...].astype(BF16)


MESH = pl.DeviceIdType.MESH
SIZES = ((256, 384), (128, 256), (256, 512), (512, 256))


def partner(place, step):
    return {0: place, 1: place + 1 - 2 * lax.rem(place, 2), 2: lax.rem(place + 2, 4), 3: 3 - place}[step]


def here():
    return lax.axis_index("section"), lax.axis_index("dp"), lax.axis_index("shard")


def greet(core, place, depth):
    barrier = pltpu.get_barrier_semaphore()
    targets = [{SHARD: lax.rem(depth + step, 4)} for step in (1, 2, 3)]
    targets += [{SECTION: 1 - core, SHARD: lax.rem(depth + step, 4)} for step in range(4)]
    targets += [{DP: partner(place, step)} for step in (1, 2, 3)]
    for target in targets:
        pl.semaphore_signal(barrier, inc=1, device_id=target, device_id_type=MESH)
    pl.semaphore_wait(barrier, len(targets))


def send(source, target, send_sem, recv_sem, device):
    copy = pltpu.make_async_remote_copy(
        src_ref=source, dst_ref=target, send_sem=send_sem, recv_sem=recv_sem,
        device_id=device, device_id_type=MESH,
    )
    copy.start()


def await_bytes(view, sem):
    pltpu.make_async_copy(view, view, sem).wait()


def lanes(start, size):
    return pl.ds(pl.multiple_of(start, 128), size)


def raw_views(raw, matrix, half, quarter):
    if matrix == 0:
        return [raw[0].at[:, lanes(third * 1024 + quarter * 256 + half * 128, 128)] for third in range(3)]
    if matrix == 1:
        return [raw[1].at[pl.ds(half * 128, 128), lanes(quarter * 256, 256)]]
    if matrix == 2:
        return [raw[2].at[:, lanes(quarter * 1024 + half * 512, 512)]]
    return [raw[3].at[pl.ds(half * 512, 512), lanes(quarter * 256, 256)]]


def whole_view(whole, matrix, quarter, shard):
    if matrix in (0, 2):
        return whole[matrix].at[quarter, shard]
    return whole[matrix].at[shard, :, lanes(quarter * 256, 256)]


def whole_views(whole, matrix, quarter, shard):
    if matrix == 0:
        return [whole[0].at[quarter, shard, :, pl.ds(third * 128, 128)] for third in range(3)]
    return [whole_view(whole, matrix, quarter, shard)]


def pieces_view(whole, matrix, first, second):
    if matrix in (0, 2):
        return whole[matrix].at[pl.ds(0, first), pl.ds(0, second)]
    return whole[matrix].at[pl.ds(0, first), :, pl.ds(0, 256 * second)]


class Saved(NamedTuple):
    entry: object
    normed: object
    proj: object
    head_out: object
    scaled: object
    logs: object
    branch: object
    branch_other: object
    residual: object
    ffn_input: object
    gelu: object
    slope: object
    stat: object
    stat_other: object
    middle: object


def whole_spec(shape):
    return pl.BlockSpec(shape, lambda step: (0,) * len(shape), pipeline_mode=pl.Buffered(1))


def block_spec(rows, columns):
    return pl.BlockSpec((1, rows, columns), lambda step: (step, 0, 0))


def grad_spec(columns):
    return pl.BlockSpec((1, 4, 256, columns), lambda step: (step, 0, 0, 0))


def column_spec(columns):
    return pl.BlockSpec((1024, columns), lambda step: (0, step))


def third_spec(third):
    return pl.BlockSpec((1, 1024, 128), lambda group: (group, 0, third))


def stage(body, ins, outs, hooks=()):
    def hooked(*refs):
        body(*refs)
        for step, action in hooks:
            pl.when(pl.program_id(0) == step)(action)

    pltpu.emit_pipeline(
        hooked, grid=(4,), in_specs=[spec for unused, spec in ins], out_specs=[spec for unused, spec in outs]
    )(*[ref for ref, unused in ins], *[ref for ref, unused in outs])


def after(*actions):
    def run():
        for action, *arguments in actions:
            action(*arguments)

    return run


def block_rows(index):
    return pl.ds(pl.multiple_of(index * 256, 256), 256)


def forward_kernel(*refs):
    refs = list(refs)

    def take(count):
        found = refs[:count]
        del refs[:count]
        return found

    (split_ref,) = take(1)
    items, *raw = take(5)
    small_in = take(5)
    cotangent, part_out = take(2)
    wholes = (take(4), take(4))
    saved = [Saved(*take(15)) for unused in (0, 1)]
    small_out = take(5)
    smalls = take(5)
    gains, shifts, mid_gain, mid_shift, head_row = smalls
    bias, turned = take(2)
    swaps = [(*take(2),) for unused in range(3)]
    stats = [(*take(2),) for unused in (0, 1)]
    (item_send, item_recv, item_pass, own_send, own_recv, deep_send, deep_recv, hop_send, hop_recv, small_sems,
     swap_send, swap_recv, keep_sem, small_keep) = refs
    core, place, depth = here()
    arrays = (saved[0].entry, cotangent)
    greet(core, place, depth)

    for layer in (0, 1):
        @pl.when(core == layer)
        def unused():
            for step in (1, 2, 3):
                send(items.at[partner(place, step)], arrays[layer].at[block_rows(place)], item_send.at[layer, step],
                     item_recv.at[layer, step], {DP: partner(place, step)})
            pltpu.make_async_copy(items.at[place], arrays[layer].at[block_rows(place)], item_send.at[layer, 0]).start()
            send(items.at[place], arrays[layer].at[block_rows(place)], item_pass.at[layer, 0], item_recv.at[layer, 0],
                 {SECTION: 1 - layer})
            for index, (source, target) in enumerate(zip(small_in, smalls)):
                pltpu.make_async_copy(source, target.at[layer], small_sems.at[0, index]).start()
                send(source, target.at[layer], small_sems.at[1, index], small_sems.at[2, index],
                     {SECTION: 1 - layer})

    units = [(layer, matrix) for layer in (0, 1) for matrix in range(4)]

    def deep(unit):
        layer, matrix = units[unit]

        @pl.when(core == layer)
        def unused():
            for step in (1, 2, 3):
                for half in (0, 1):
                    for source, target in zip(
                        raw_views(raw, matrix, half, place), whole_views(wholes[layer], matrix, place, depth)
                    ):
                        send(source, target, deep_send.at[unit], deep_recv.at[unit, step],
                             {SECTION: half, SHARD: lax.rem(depth + 4 - step, 4)})

    def own(unit):
        layer, matrix = units[unit]

        @pl.when(core == layer)
        def unused():
            for quarter in range(4):
                for source, target in zip(
                    raw_views(raw, matrix, layer, quarter), whole_views(wholes[layer], matrix, quarter, depth)
                ):
                    pltpu.make_async_copy(source, target, own_send.at[unit, 0]).start()
                for source, target in zip(
                    raw_views(raw, matrix, 1 - layer, quarter), whole_views(wholes[layer], matrix, quarter, depth)
                ):
                    send(source, target, own_send.at[unit, 1], own_recv.at[unit], {SECTION: 1 - layer})

    def route(unit, step):
        return (1, 2) if (unit + step) % 2 == 0 else (2, 1)

    def piece(unit, offset, step):
        layer, matrix = units[unit]
        return whole_view(wholes[layer], matrix, partner(place, offset), lax.rem(depth + step, 4))

    def first_hop(unit):
        for step in (1, 2, 3):
            first, second = route(unit, step)
            await_bytes(piece(unit, 0, step), deep_recv.at[unit, step])
            for offset in (first, second):
                send(piece(unit, 0, step), piece(unit, 0, step), hop_send.at[unit], hop_recv.at[unit, step - 1, offset - 1],
                     {DP: partner(place, offset)})

    def second_hop(unit):
        for step in (1, 2, 3):
            first, second = route(unit, step)
            await_bytes(piece(unit, first, step), hop_recv.at[unit, step - 1, first - 1])
            send(piece(unit, first, step), piece(unit, first, step), hop_send.at[unit], hop_recv.at[unit, step - 1, 2],
                 {DP: partner(place, second)})

    def ready(unit):
        layer, matrix = units[unit]
        quarters = pieces_view(wholes[layer], matrix, 2, 2)

        @pl.when(core == layer)
        def unused():
            await_bytes(quarters, own_send.at[unit, 0])

        @pl.when(core != layer)
        def unused_too():
            await_bytes(quarters, own_recv.at[unit])

        for step in (1, 2, 3):
            first, second = route(unit, step)
            await_bytes(piece(unit, 0, 0), hop_recv.at[unit, step - 1, second - 1])
            await_bytes(piece(unit, 0, 0), hop_recv.at[unit, step - 1, 2])

    def pass_on(layer):
        @pl.when(core == layer)
        def unused():
            for step in (1, 2, 3):
                block = arrays[layer].at[block_rows(partner(place, step))]
                await_bytes(block, item_recv.at[layer, step])
                send(block, block, item_pass.at[layer, step], item_recv.at[layer, step], {SECTION: 1 - layer})

    def passed(layer):
        @pl.when(core == layer)
        def unused():
            await_bytes(items.at[0], item_send.at[layer, 0])

        @pl.when(core != layer)
        def unused_too():
            for step in range(4):
                await_bytes(items.at[0], item_recv.at[layer, step])

    def take_smalls():
        for index, (source, target) in enumerate(zip(small_in, smalls)):
            for layer in (0, 1):
                @pl.when(core == layer)
                def unused():
                    await_bytes(source, small_sems.at[0, index])

                @pl.when(core != layer)
                def unused_too():
                    await_bytes(source, small_sems.at[2, index])

    def keep(index, source, target):
        pltpu.make_async_copy(source, target, keep_sem.at[index]).start()

    def kept(index, source):
        await_bytes(source, keep_sem.at[index])

    def swap_tile(index, pair, value):
        own_ref, other_ref = pair
        span = block_rows(pl.program_id(0))
        own_ref[span, :] = value
        send(own_ref.at[span], other_ref.at[span], swap_send.at[index], swap_recv.at[index], {SECTION: 1 - core})

    def swapped(index, pair):
        await_bytes(pair[0], swap_send.at[index])
        await_bytes(pair[1], swap_recv.at[index])

    def mid_row(ref, layer, group):
        return ref[layer, :, lanes(group * 1024 + core * 512, 512)]

    def project_rows(layer, x, normed_ref, proj_ref, w_ref):
        unit_x, unused = standard(x)
        normed = (unit_x * gains[layer, 0:1, :] + shifts[layer, 0:1, :]).astype(BF16)
        normed_ref[...] = normed
        for group in range(4):
            proj_ref[group] = dot(normed, w_ref[group].reshape(1024, 384)).astype(BF16)

    def project_stage(layer, hooks):
        own_half = saved[layer]
        weight = (wholes[layer][0], whole_spec((4, 4, 256, 384)))
        made = [(own_half.normed, rows_spec(1024)), (own_half.proj, group_spec(384))]

        def body_first(x_ref, w_ref, normed_ref, proj_ref):
            project_rows(layer, x_ref[...].astype(F32), normed_ref, proj_ref, w_ref)

        def body_next(res_ref, a_ref, b_ref, w_ref, normed_ref, proj_ref, entry_ref):
            entry = (res_ref[...] + (a_ref[...].astype(F32) + b_ref[...].astype(F32))).astype(BF16)
            entry_ref[...] = entry
            project_rows(layer, entry.astype(F32), normed_ref, proj_ref, w_ref)

        if layer == 0:
            stage(body_first, [(own_half.entry, rows_spec(1024)), weight], made, hooks)
        else:
            stage(
                body_next,
                [(saved[0].residual, rows_spec(1024)), (swaps[1][0], rows_spec(1024)), (swaps[1][1], rows_spec(1024)), weight],
                [*made, (own_half.entry, rows_spec(1024))],
                hooks,
            )

    def attention_stage(layer, hooks):
        own_half = saved[layer]

        def body(q_ref, k_ref, v_ref, out_ref, scaled_ref, log_ref):
            scale_row = head_row[layer, :, lanes(pl.program_id(0) * 256 + core * 128, 128)]
            attend(q_ref, k_ref, v_ref, scale_row, out_ref, scaled_ref, log_ref, bias, turned)

        stage(
            body,
            [(own_half.proj, third_spec(0)), (own_half.proj, third_spec(1)), (own_half.proj, third_spec(2))],
            [(own_half.head_out, column_spec(128)), (own_half.scaled, column_spec(128)),
             (own_half.logs, pl.BlockSpec((1, 2, 1024), lambda group: (group, 0, 0)))],
            hooks,
        )

    def out_stage(layer, hooks):
        def body(scaled_ref, w_ref):
            swap_tile(layer * 2, swaps[layer * 2], dot(scaled_ref[...], w_ref[...].reshape(512, 1024)).astype(BF16))

        stage(body, [(saved[layer].scaled, rows_spec(512)), (wholes[layer][1], whole_spec((4, 128, 1024)))], [], hooks)

    def widen_stage(layer, hooks):
        own_half = saved[layer]

        def body(x_ref, a_ref, b_ref, w_ref, res_ref, ffn_ref, gelu_ref, slope_ref):
            branch = a_ref[...].astype(F32) + b_ref[...].astype(F32)
            unit_b, unused = standard(branch)
            residual = x_ref[...].astype(F32) + unit_b * gains[layer, 1:2, :] + shifts[layer, 1:2, :]
            res_ref[...] = residual
            unit_r, unused = standard(residual)
            ffn_input = (unit_r * gains[layer, 2:3, :] + shifts[layer, 2:3, :]).astype(BF16)
            ffn_ref[...] = ffn_input
            first, second = [], []
            for group in range(4):
                hidden = dot(ffn_input, w_ref[group].reshape(1024, 512))
                half = 0.5 + 0.5 * lax.erf(hidden * math.sqrt(0.5))
                gelu = hidden * half
                bell = jnp.exp(-0.5 * hidden * hidden) * (1.0 / math.sqrt(2.0 * math.pi))
                gelu_ref[group] = gelu.astype(BF16)
                slope_ref[group] = (half + hidden * bell).astype(BF16)
                mean = jnp.mean(gelu, axis=-1, keepdims=True)
                centre = gelu - mean
                first.append(mean)
                second.append(jnp.mean(centre * centre, axis=-1, keepdims=True))
            mean = 0.25 * (first[0] + first[1] + first[2] + first[3])
            spread_of = sum(0.25 * (s + (m - mean) * (m - mean)) for m, s in zip(first, second))
            swap_tile(3 + layer, stats[layer], two_columns(mean, spread_of))

        branch_own, branch_other = swaps[layer * 2]
        stage(
            body,
            [(own_half.entry, rows_spec(1024)), (branch_own, rows_spec(1024)), (branch_other, rows_spec(1024)),
             (wholes[layer][2], whole_spec((4, 4, 256, 512)))],
            [(own_half.residual, rows_spec(1024)), (own_half.ffn_input, rows_spec(1024)), (own_half.gelu, group_spec(512)),
             (own_half.slope, group_spec(512))],
            hooks,
        )

    def narrow_stage(layer, hooks):
        own_half = saved[layer]

        def rows(g_ref, own_ref, other_ref, w_ref, mid_ref):
            mean, scale = mid_stats(own_ref[...], other_ref[...])
            total = jnp.zeros((TILE, 1024), F32)
            for group in range(4):
                unit_m = (g_ref[group].astype(F32) - mean) * scale
                middle = (unit_m * mid_row(mid_gain, layer, group) + mid_row(mid_shift, layer, group)).astype(BF16)
                mid_ref[group] = middle
                total = total + dot(middle, w_ref[group])
            return total.astype(BF16)

        def body_first(*tiles):
            swap_tile(1, swaps[1], rows(*tiles))

        def body_last(*tiles):
            tiles[-1][...] = rows(*tiles[:-1])

        ins = [(own_half.gelu, group_spec(512)), (stats[layer][0], rows_spec(128)), (stats[layer][1], rows_spec(128)),
               (wholes[layer][3], whole_spec((4, 512, 1024)))]
        outs = [(own_half.middle, group_spec(512))]
        if layer == 0:
            stage(body_first, ins, outs, hooks)
        else:
            stage(body_last, ins, [*outs, (part_out, rows_spec(1024))], hooks)

    def layer_forward(layer, hooks):
        own_half = saved[layer]
        base = layer * 4
        ready(base)
        if layer == 0:
            passed(0)
            take_smalls()
        else:
            swapped(1, swaps[1])
        project_stage(layer, hooks[0])
        attention_stage(layer, hooks[1])
        ready(base + 1)
        out_stage(layer, hooks[2])
        ready(base + 2)
        swapped(layer * 2, swaps[layer * 2])
        for index, (source, target) in enumerate(zip(swaps[layer * 2], (own_half.branch, own_half.branch_other))):
            keep(layer * 4 + index, source, target)
        widen_stage(layer, hooks[3])
        ready(base + 3)
        swapped(3 + layer, stats[layer])
        for index, (source, target) in enumerate(zip(stats[layer], (own_half.stat, own_half.stat_other))):
            keep(layer * 4 + 2 + index, source, target)
        narrow_stage(layer, hooks[4])

    deep(0)
    deep(1)
    own(0)
    own(1)
    deep(2)
    fill_bias(bias, split_ref[0])
    first_hop(0)
    pass_on(0)
    first_hop(1)
    own(2)
    deep(3)
    second_hop(0)
    first_hop(2)
    own(3)
    second_hop(1)
    layer_forward(0, (
        ((2, after((deep, 4), (second_hop, 2))),),
        ((1, after((first_hop, 3), (own, 4))), (3, after((deep, 5), (pass_on, 1)))),
        (),
        ((0, after((second_hop, 3), (own, 5))), (2, after((first_hop, 4), (deep, 6)))),
        ((1, after((second_hop, 4), (own, 6))), (3, after((first_hop, 5), (deep, 7), (second_hop, 5)))),
    ))
    first_hop(6)
    own(7)
    layer_forward(1, (
        ((2, after((second_hop, 6),)),),
        ((1, after((first_hop, 7),)), (3, after((second_hop, 7),))),
        (),
        (),
        (),
    ))

    for index, (source, target) in enumerate(zip(smalls, small_out)):
        pltpu.make_async_copy(source, target, small_keep.at[index]).start()
    for layer in (0, 1):
        for index, (source, unused_target) in enumerate(zip((*swaps[layer * 2], *stats[layer]), range(4))):
            kept(layer * 4 + index, source)

        @pl.when(core == layer)
        def unused():
            for step in (1, 2, 3):
                await_bytes(items.at[0], item_send.at[layer, step])
            for step in range(4):
                await_bytes(items.at[0], item_pass.at[layer, step])
            for index, source in enumerate(small_in):
                await_bytes(source, small_sems.at[1, index])

    passed(1)
    for unit, (layer, matrix) in enumerate(units):
        whole = wholes[layer]

        @pl.when(core == layer)
        def unused():
            await_bytes(pieces_view(whole, matrix, 2, 2), own_send.at[unit, 1])
            await_bytes(pieces_view(whole, matrix, 3, 2), deep_send.at[unit])

        await_bytes(pieces_view(whole, matrix, 3, 3), hop_send.at[unit])
    for index, source in enumerate(smalls):
        await_bytes(source, small_keep.at[index])


def forward_all(split_at, items, weights, smalls):
    anywhere = pl.BlockSpec(memory_space=pl.ANY)
    dma = pltpu.SemaphoreType.DMA
    rows = array((1024, 1024), BF16)
    gathered = [
        array((4, 4, 256, 384), BF16),
        array((4, 128, 1024), BF16),
        array((4, 4, 256, 512), BF16),
        array((4, 512, 1024), BF16),
    ]
    wide, stat, heads = array((4, 1024, 512), BF16), array((1024, 128), F32), array((1024, 512), BF16)
    saved = [
        rows, rows, array((4, 1024, 384), BF16), heads, heads, array((4, 2, 1024), F32), rows, rows,
        array((1024, 1024), F32), rows, wide, wide, stat, stat, wide,
    ]
    small_shapes = [(2,) + operand.shape for operand in smalls]
    shapes = [rows, rows, *gathered * 2, *saved * 2, *[array(shape, F32) for shape in small_shapes]]
    found = pl.pallas_call(
        forward_kernel,
        in_specs=[pl.BlockSpec(memory_space=pltpu.SMEM)] + [anywhere] * (5 + 5),
        out_specs=[anywhere] * len(shapes),
        out_shape=shapes,
        scratch_shapes=[pltpu.VMEM(shape, F32) for shape in small_shapes]
        + [pltpu.VMEM((1024, 1024), F32), pltpu.VMEM((128, 1024), BF16)]
        + [pltpu.VMEM((1024, 1024), BF16)] * 6
        + [pltpu.VMEM((1024, 128), F32)] * 4
        + [
            dma((2, 4)), dma((2, 4)), dma((2, 4)), dma((8, 2)), dma((8,)),
            dma((8,)), dma((8, 4)), dma((8,)), dma((8, 3, 3)), dma((3, 5)),
            dma((5,)), dma((5,)), dma((8,)), dma((5,)),
        ],
        compiler_params=pltpu.CompilerParams(
            collective_id=0, has_side_effects=True, vmem_limit_bytes=VMEM_BYTES
        ),
    )(split_at, items, *weights, *smalls)
    cotangent, part = found[0:2]
    wholes = (found[2:6], found[6:10])
    kept = (Saved(*found[10:25]), Saved(*found[25:40]))
    return cotangent, part, wholes, kept, found[40:]


ORDER = tuple((layer, matrix) for layer in (1, 0) for matrix in (3, 2, 1, 0))

class Made(NamedTuple):
    d_middle: object
    d_hidden: object
    d_residual: object
    d_branch: object
    d_heads: object
    d_proj: object
    d_entry: object


def add_up_into(target, *terms):
    rows = target.shape[0]

    def step(index, unused):
        span = pl.ds(pl.multiple_of(index * 32, 32), 32)
        total = target[span, :].astype(F32)
        for term in terms:
            total = total + term[span, :].astype(F32)
        target[span, :] = total.astype(BF16)
        return unused

    lax.fori_loop(0, rows // 32, step, 0)


def backward_kernel(*refs):
    refs = list(refs)

    def take(count):
        found = refs[:count]
        del refs[:count]
        return found

    split_ref, cotangent, part_last = take(3)
    saved = [Saved(*take(15)) for unused in (0, 1)]
    weights = [take(4), take(4)]
    gains, mid_gain, head_row = take(3)
    shares = take(4)
    (ends, small_out) = take(2)
    grads = (take(4), take(4))
    made = [Made(*take(7)) for unused in (0, 1)]
    output, part_other = take(2)
    own, first_in, second_in, deep_in = take(4), take(4), take(4), take(4)
    vec, inbox, acc, bias, turned, dk_acc, dv_acc = take(7)
    swaps = [(*take(2),) for unused in (0, 1)]
    sums = [(*take(2),) for unused in (0, 1)]
    (load_sem, first_send, first_recv, second_send, second_recv, deep_send, deep_recv, last_send, last_copy,
     last_recv, ends_send, ends_recv, small_send, small_recv, swap_send, swap_recv, credit) = refs
    core, place, depth = here()
    greet(core, place, depth)

    def send_ends(owner, source):
        @pl.when(core == owner)
        def unused():
            for step in (1, 2, 3):
                send(source.at[block_rows(partner(place, step))], ends.at[place], ends_send.at[step], ends_recv.at[step],
                     {DP: partner(place, step)})
            pltpu.make_async_copy(source.at[block_rows(place)], ends.at[place], ends_send.at[0]).start()

    def route(step):
        return (1, 2) if step < 2 else (2, 1)

    def shard_of(step):
        return lax.rem(depth + step, 4)

    def begin(unit):
        layer, matrix = ORDER[unit]
        if unit >= 4:
            pl.semaphore_wait(credit.at[matrix], 2)
        for step in range(4):
            first, second = route(step)
            for index, offset in enumerate((first, 3)):
                send(whole_view(grads[layer], matrix, partner(place, offset), shard_of(step)),
                     first_in[matrix].at[step, index], first_send.at[unit], first_recv.at[unit],
                     {DP: partner(place, first)})
            for index, offset in enumerate((0, second)):
                pltpu.make_async_copy(
                    whole_view(grads[layer], matrix, partner(place, offset), shard_of(step)),
                    own[matrix].at[step, index], load_sem.at[unit],
                ).start()

    def second_hop(unit):
        layer, matrix = ORDER[unit]
        await_bytes(own[matrix], load_sem.at[unit])
        await_bytes(first_in[matrix], first_recv.at[unit])
        for step in range(4):
            first, second = route(step)
            mine = own[matrix].at[step, 1]
            add_up_into(mine, first_in[matrix].at[step, 1])
            send(mine, second_in[matrix].at[step], second_send.at[unit], second_recv.at[unit],
                 {DP: partner(place, second)})

    def deep_hop(unit):
        layer, matrix = ORDER[unit]
        await_bytes(second_in[matrix], second_recv.at[unit])
        for step in (1, 2, 3, 0):
            mine = own[matrix].at[step, 0]
            add_up_into(mine, first_in[matrix].at[step, 0], second_in[matrix].at[step])
            if step:
                send(mine, deep_in[matrix].at[layer, step - 1], deep_send.at[unit], deep_recv.at[unit],
                     {SHARD: shard_of(step)})
        if unit < 4:
            for step in (1, 2):
                pl.semaphore_signal(
                    credit.at[matrix], inc=1, device_id={DP: partner(place, step)}, device_id_type=MESH
                )

    def finish(unit):
        layer, matrix = ORDER[unit]
        await_bytes(deep_in[matrix].at[layer], deep_recv.at[unit])
        mine = own[matrix].at[0, 0]
        add_up_into(mine, *[deep_in[matrix].at[layer, index] for index in range(3)])
        sources = [mine]
        if matrix == 0:
            sources = [mine.at[:, pl.ds(third * 128, 128)] for third in range(3)]
        for half in (0, 1):
            @pl.when(core == half)
            def unused():
                for source, target in zip(sources, raw_views(shares, matrix, half, place)):
                    if half == layer:
                        pltpu.make_async_copy(source, target, last_copy.at[unit]).start()
                        for offset in (1, 2):
                            send(source, target, last_send.at[unit, 0], last_recv.at[unit, half, offset],
                                 {DP: partner(place, offset)})
                    else:
                        send(source, target, last_send.at[unit, 0], last_recv.at[unit, half, 0], {SECTION: layer})

    def forward(unit):
        layer, matrix = ORDER[unit]
        half = 1 - layer

        @pl.when(core == layer)
        def unused():
            views = raw_views(shares, matrix, half, place)
            await_bytes(own[matrix].at[0, 0], last_recv.at[unit, half, 0])
            for view in views:
                for offset in (1, 2):
                    send(view, view, last_send.at[unit, 1], last_recv.at[unit, half, offset],
                         {DP: partner(place, offset)})

    def corner(unit):
        layer, matrix = ORDER[unit]

        @pl.when(core == layer)
        def unused():
            for half in (layer, 1 - layer):
                first, second = (1, 2) if half == 0 else (2, 1)
                await_bytes(own[matrix].at[0, 0], last_recv.at[unit, half, first])
                for view in raw_views(shares, matrix, half, partner(place, first)):
                    send(view, view, last_send.at[unit, 2], last_recv.at[unit, half, 3], {DP: partner(place, second)})

    def free_own(unit):
        layer, matrix = ORDER[unit]

        @pl.when(core == layer)
        def unused():
            await_bytes(own[matrix].at[0], last_send.at[unit, 0])
            await_bytes(own[matrix].at[0, 0], last_copy.at[unit])

        @pl.when(core != layer)
        def unused_too():
            await_bytes(own[matrix].at[0, 0], last_send.at[unit, 0])

    def free_hops(unit):
        layer, matrix = ORDER[unit]
        await_bytes(second_in[matrix], second_send.at[unit])
        await_bytes(deep_in[matrix].at[layer], deep_send.at[unit])
        free_own(unit)

    def clean(unit):
        layer, matrix = ORDER[unit]
        await_bytes(first_in[matrix], first_send.at[unit])
        if unit >= 4:
            free_hops(unit)

        @pl.when(core == layer)
        def unused():
            for row in (1, 2):
                await_bytes(own[matrix].at[0], last_send.at[unit, row])
            for half in (0, 1):
                first, second = (1, 2) if half == 0 else (2, 1)
                await_bytes(own[matrix].at[0, 0], last_recv.at[unit, half, second])
                await_bytes(own[matrix].at[0, 0], last_recv.at[unit, half, 3])

    column = pl.ds(pl.multiple_of(core * 512, 512), 512)
    exchanges = (
        {SECTION: 1 - core},
        {DP: partner(place, 1)},
        {DP: partner(place, 2)},
        {SHARD: partner(depth, 1)},
        {SHARD: partner(depth, 2)},
    )

    def small_step(index):
        if index:
            send(acc.at[index - 1], inbox.at[index], small_send.at[index], small_recv.at[index], exchanges[index])
        else:
            for layer in (0, 1):
                @pl.when(core != layer)
                def unused():
                    vec[layer, 0:6, :] = jnp.zeros((6, 1024), F32)

            for half in (0, 1):
                @pl.when(core == half)
                def unused_too():
                    send(vec.at[1 - half], inbox.at[0], small_send.at[0], small_recv.at[0], exchanges[0])

    def small_take(index):
        await_bytes(inbox.at[index], small_recv.at[index])
        if index:
            acc[index] = acc[index - 1] + inbox[index]
        else:
            for half in (0, 1):
                @pl.when(core == half)
                def unused():
                    acc[0] = vec[half] + inbox[0]

    def swap_tile(index, pair, value):
        own_ref, other_ref = pair
        span = block_rows(pl.program_id(0))
        own_ref[span, :] = value
        send(own_ref.at[span], other_ref.at[span], swap_send.at[index], swap_recv.at[index], {SECTION: 1 - core})

    def swapped(index, pair):
        await_bytes(pair[0], swap_send.at[index])
        await_bytes(pair[1], swap_recv.at[index])

    def mid_row(layer, group):
        return mid_gain[layer, :, lanes(group * 1024 + core * 512, 512)]

    def add_vec(layer, row, value, span=slice(None)):
        vec[layer, row : row + 1, span] += value

    def weight_grad(left, left_spec, right, right_spec, target, target_spec):
        def body(left_ref, right_ref, out_ref):
            a = left_ref[...].reshape(left_ref.shape[-2:])
            b = right_ref[...].reshape(right_ref.shape[-2:])
            value = lax.dot_general(a, b, (((0,), (0,)), ((), ())), preferred_element_type=F32)
            out_ref[...] = value.astype(BF16).reshape(out_ref.shape)

        stage(body, [(left, left_spec), (right, right_spec)], [(target, target_spec)])

    def narrow_stage(layer, grad):
        own_half, make = saved[layer], made[layer]

        def body(c_ref, g_ref, own_ref, other_ref, w_ref, dm_ref):
            mean, scale = mid_stats(own_ref[...], other_ref[...])
            grad_low = c_ref[...]
            first = jnp.zeros((TILE, 1), F32)
            second = jnp.zeros((TILE, 1), F32)
            for group in range(4):
                d_middle = dot_nt(grad_low, w_ref[group])
                dm_ref[group] = d_middle.astype(BF16)
                unit_m = (g_ref[group].astype(F32) - mean) * scale
                product = d_middle * unit_m
                add_vec(layer, 6 + group, jnp.sum(product, axis=0, keepdims=True), column)
                add_vec(layer, 10 + group, jnp.sum(d_middle, axis=0, keepdims=True), column)
                row_gain = mid_row(layer, group)
                first = first + jnp.sum(d_middle * row_gain, axis=-1, keepdims=True)
                second = second + jnp.sum(product * row_gain, axis=-1, keepdims=True)
            swap_tile(layer * 3, sums[layer], two_columns(first, second))

        stage(
            body,
            [(grad, rows_spec(1024)), (own_half.gelu, group_spec(512)), (own_half.stat, rows_spec(128)),
             (own_half.stat_other, rows_spec(128)), (weights[layer][3], whole_spec((4, 512, 1024)))],
            [(make.d_middle, group_spec(512))],
        )

    def widen_stage(layer):
        own_half, make = saved[layer], made[layer]

        def body(dm_ref, g_ref, s_ref, own_ref, other_ref, a_ref, b_ref, w_ref, dh_ref):
            mean, scale = mid_stats(own_ref[...], other_ref[...])
            both = (a_ref[...] + b_ref[...]) * (1.0 / 4096)
            first, second = both[:, 0:1], both[:, 64:65]
            total = jnp.zeros((TILE, 1024), F32)
            for group in range(4):
                unit_m = (g_ref[group].astype(F32) - mean) * scale
                inner = dm_ref[group].astype(F32) * mid_row(layer, group)
                d_gelu = scale * (inner - first - unit_m * second)
                d_hidden = (d_gelu * s_ref[group].astype(F32)).astype(BF16)
                dh_ref[group] = d_hidden
                total = total + dot_nt(d_hidden, w_ref[group].reshape(1024, 512))
            swap_tile(layer * 3 + 1, swaps[0], total.astype(BF16))

        stage(
            body,
            [(make.d_middle, group_spec(512)), (own_half.gelu, group_spec(512)), (own_half.slope, group_spec(512)),
             (own_half.stat, rows_spec(128)), (own_half.stat_other, rows_spec(128)), (sums[layer][0], rows_spec(128)),
             (sums[layer][1], rows_spec(128)), (weights[layer][2], whole_spec((4, 4, 256, 512)))],
            [(make.d_hidden, group_spec(512))],
        )

    def norms_stage(layer, grad):
        own_half, make = saved[layer], made[layer]
        scale_row = jnp.concatenate(
            [head_row[layer, :, lanes(group * 256 + core * 128, 128)] for group in range(4)], axis=1
        )

        def body(c_ref, res_ref, da_ref, db_ref, ba_ref, bb_ref, ho_ref, w_ref, dr_ref, dbr_ref, dh_ref):
            unit_r, scale_r = standard(res_ref[...])
            d_ffn = da_ref[...].astype(F32) + db_ref[...].astype(F32)
            back, gain_third, shift_third = standard_back(unit_r, scale_r, gains[layer, 2:3, :], d_ffn)
            d_residual = c_ref[...].astype(F32) + back
            dr_ref[...] = d_residual
            unit_b, scale_b = standard(ba_ref[...].astype(F32) + bb_ref[...].astype(F32))
            back, gain_second, shift_second = standard_back(unit_b, scale_b, gains[layer, 1:2, :], d_residual)
            d_branch = back.astype(BF16)
            dbr_ref[...] = d_branch
            d_scaled = dot_nt(d_branch, w_ref[...].reshape(512, 1024))
            dh_ref[...] = (d_scaled * scale_row).astype(BF16)
            add_vec(layer, 14, jnp.sum(d_scaled * ho_ref[...].astype(F32), axis=0, keepdims=True), column)
            for row, value in ((1, gain_second), (2, gain_third), (4, shift_second), (5, shift_third)):
                add_vec(layer, row, value)

        stage(
            body,
            [(grad, rows_spec(1024)), (own_half.residual, rows_spec(1024)), (swaps[0][0], rows_spec(1024)),
             (swaps[0][1], rows_spec(1024)), (own_half.branch, rows_spec(1024)),
             (own_half.branch_other, rows_spec(1024)), (own_half.head_out, rows_spec(512)),
             (weights[layer][1], whole_spec((4, 128, 1024)))],
            [(make.d_residual, rows_spec(1024)), (make.d_branch, rows_spec(1024)), (make.d_heads, rows_spec(512))],
        )

    def attention_stage(layer):
        own_half, make = saved[layer], made[layer]

        def body(q_ref, k_ref, v_ref, grad_ref, out_ref, log_ref, back_ref):
            attend_back(q_ref, k_ref, v_ref, grad_ref, out_ref, log_ref, back_ref, bias, turned, dk_acc, dv_acc)

        stage(
            body,
            [(own_half.proj, third_spec(0)), (own_half.proj, third_spec(1)), (own_half.proj, third_spec(2)),
             (make.d_heads, column_spec(128)), (own_half.head_out, column_spec(128)),
             (own_half.logs, pl.BlockSpec((1, 2, 1024), lambda group: (group, 0, 0)))],
            [(make.d_proj, block_spec(1024, 384))],
        )

    def project_stage(layer):
        make = made[layer]

        def body(d_ref, w_ref):
            total = dot_nt(d_ref[0], w_ref[0].reshape(1024, 384))
            for group in range(1, 4):
                total = total + dot_nt(d_ref[group], w_ref[group].reshape(1024, 384))
            swap_tile(layer * 3 + 2, swaps[1], total.astype(BF16))

        stage(
            body, [(make.d_proj, group_spec(384)), (weights[layer][0], whole_spec((4, 4, 256, 384)))], []
        )

    def entry_stage(layer):
        own_half, make = saved[layer], made[layer]

        def body(dr_ref, a_ref, b_ref, x_ref, dx_ref):
            unit_x, scale_x = standard(x_ref[...].astype(F32))
            d_normed = a_ref[...].astype(F32) + b_ref[...].astype(F32)
            back, gain_first, shift_first = standard_back(unit_x, scale_x, gains[layer, 0:1, :], d_normed)
            dx_ref[...] = (dr_ref[...] + back).astype(BF16)
            add_vec(layer, 0, gain_first)
            add_vec(layer, 3, shift_first)

        stage(
            body,
            [(make.d_residual, rows_spec(1024)), (swaps[1][0], rows_spec(1024)),
             (swaps[1][1], rows_spec(1024)), (own_half.entry, rows_spec(1024))],
            [(make.d_entry, rows_spec(1024))],
        )

    def layer_back(layer, grad, events):
        own_half, make = saved[layer], made[layer]
        base = 0 if layer == 1 else 4
        weight_grad(own_half.middle, block_spec(1024, 512), grad, whole_spec((1024, 1024)),
                    grads[layer][3], block_spec(512, 1024))
        events[0]()
        begin(base)
        narrow_stage(layer, grad)
        events[1]()
        swapped(layer * 3, sums[layer])
        widen_stage(layer)
        events[2]()
        weight_grad(own_half.ffn_input, whole_spec((1024, 1024)), make.d_hidden, block_spec(1024, 512),
                    grads[layer][2], grad_spec(512))
        begin(base + 1)
        swapped(layer * 3 + 1, swaps[0])
        norms_stage(layer, grad)
        events[3]()
        weight_grad(own_half.scaled, column_spec(128), make.d_branch, whole_spec((1024, 1024)),
                    grads[layer][1], block_spec(128, 1024))
        begin(base + 2)
        attention_stage(layer)
        events[4]()
        project_stage(layer)
        events[5]()
        weight_grad(own_half.normed, whole_spec((1024, 1024)), make.d_proj, block_spec(1024, 384),
                    grads[layer][0], grad_spec(384))
        begin(base + 3)
        swapped(layer * 3 + 2, swaps[1])
        entry_stage(layer)
        events[6]()

    def output_stage():
        swapped(6, (part_last, part_other))

        def body(res_ref, a_ref, b_ref, out_ref):
            out_ref[...] = (res_ref[...] + (a_ref[...].astype(F32) + b_ref[...].astype(F32))).astype(BF16)

        stage(
            body,
            [(saved[1].residual, rows_spec(1024)), (part_last, rows_spec(1024)), (part_other, rows_spec(1024))],
            [(output, rows_spec(1024))],
        )
        send_ends(1, output)

    def prepare():
        vec[...] = jnp.zeros_like(vec)
        fill_bias(bias, split_ref[0])

    send(part_last, part_other, swap_send.at[6], swap_recv.at[6], {SECTION: 1 - core})
    layer_back(1, cotangent, (
        after((prepare,)),
        after(),
        after((second_hop, 0), (output_stage,)),
        after((deep_hop, 0),),
        after((second_hop, 1), (finish, 0), (second_hop, 2)),
        after((deep_hop, 1), (forward, 0)),
        after((deep_hop, 2), (finish, 1), (corner, 0), (second_hop, 3)),
    ))
    layer_back(0, made[1].d_entry, (
        after((forward, 1), (finish, 2), (deep_hop, 3), (free_hops, 0)),
        after((corner, 1), (forward, 2)),
        after((second_hop, 4), (finish, 3), (free_hops, 1), (corner, 2)),
        after((deep_hop, 4), (forward, 3), (free_hops, 2)),
        after((second_hop, 5), (finish, 4), (corner, 3), (second_hop, 6)),
        after((deep_hop, 5), (forward, 4), (free_hops, 3)),
        after((deep_hop, 6),),
    ))
    send_ends(0, made[0].d_entry)
    small_step(0)
    second_hop(7)
    finish(5)
    finish(6)
    corner(4)
    small_take(0)
    small_step(1)
    deep_hop(7)
    forward(5)
    forward(6)
    small_take(1)
    small_step(2)
    finish(7)
    corner(5)
    corner(6)
    small_take(2)
    small_step(3)
    forward(7)
    small_take(3)
    small_step(4)
    corner(7)
    small_take(4)
    small_out[...] = acc[4]
    for unit in range(8):
        clean(unit)
    for index in range(5):
        await_bytes(inbox.at[index], small_send.at[index])
    for step in range(4):
        await_bytes(ends.at[0], ends_send.at[step])
    for step in (1, 2, 3):
        await_bytes(ends.at[0], ends_recv.at[step])


def backward_all(split_at, cotangent, part, kept, weights, params):
    anywhere = pl.BlockSpec(memory_space=pl.ANY)
    local = pl.BlockSpec(memory_space=pltpu.VMEM)
    dma = pltpu.SemaphoreType.DMA
    operands = [split_at, cotangent, part, *kept[0], *kept[1], *weights[0], *weights[1], *params]
    rows = array((1024, 1024), BF16)
    grad_shapes = [
        array((4, 4, 256, 384), BF16),
        array((4, 128, 1024), BF16),
        array((4, 4, 256, 512), BF16),
        array((4, 512, 1024), BF16),
    ]
    wide = array((4, 1024, 512), BF16)
    made = [
        wide, wide, array((1024, 1024), F32), rows, array((1024, 512), BF16), array((4, 1024, 384), BF16), rows,
    ]
    shapes = [
        array((256, 3072), BF16),
        array((256, 1024), BF16),
        array((256, 4096), BF16),
        array((1024, 1024), BF16),
        array((4, 256, 1024), BF16),
        array((16, 1024), F32),
        *grad_shapes * 2,
        *made * 2,
        rows,
        rows,
    ]
    return pl.pallas_call(
        backward_kernel,
        in_specs=[pl.BlockSpec(memory_space=pltpu.SMEM)] + [anywhere] * (2 + 30 + 8) + [local] * 3,
        out_specs=[anywhere] * 5 + [local] + [anywhere] * (len(shapes) - 6),
        out_shape=shapes,
        scratch_shapes=[pltpu.VMEM((4, 2) + size, BF16) for size in SIZES]
        + [pltpu.VMEM((4, 2) + size, BF16) for size in SIZES]
        + [pltpu.VMEM((4,) + size, BF16) for size in SIZES]
        + [pltpu.VMEM((2, 3) + size, BF16) for size in SIZES]
        + [pltpu.VMEM((2, 16, 1024), F32), pltpu.VMEM((5, 16, 1024), F32), pltpu.VMEM((5, 16, 1024), F32)]
        + [pltpu.VMEM((1024, 1024), F32), pltpu.VMEM((128, 1024), BF16)]
        + [pltpu.VMEM((1024, 128), F32), pltpu.VMEM((1024, 128), F32)]
        + [pltpu.VMEM((1024, 1024), BF16)] * 4
        + [pltpu.VMEM((1024, 128), F32)] * 4
        + [dma((8,))] * 7
        + [dma((8, 3)), dma((8,)), dma((8, 2, 4)), dma((4,)), dma((4,)), dma((5,)), dma((5,)), dma((7,)), dma((7,))]
        + [pltpu.SemaphoreType.REGULAR((4,))],
        compiler_params=pltpu.CompilerParams(
            collective_id=1, has_side_effects=True, vmem_limit_bytes=62 * 2**20
        ),
    )(*operands)[:6]


def local(
    boundary,
    first_len,
    qkv_weight,
    out_weight,
    up_weight,
    down_weight,
    norm_gain,
    norm_shift,
    mid_gain,
    mid_shift,
    head_scale,
):
    split_at = pick(first_len, lax.axis_index("dp"))
    cotangent, part, weights, kept, smalls = forward_all(
        split_at,
        boundary[0, :, 0],
        (qkv_weight[0], out_weight[0], up_weight[0], down_weight[0]),
        (norm_gain[0], norm_shift[0], mid_gain, mid_shift, jnp.repeat(head_scale, 64, axis=1)),
    )
    params = (smalls[0], smalls[2], smalls[4])
    *shares, ends, totals = backward_all(split_at, cotangent, part, kept, weights, params)
    head_sums = jnp.sum(totals[14].reshape(2, 4, 2, 64), axis=3).transpose(1, 0, 2).reshape(1, 16)
    return (
        ends[None, :, None],
        *[share.astype(F32)[None] for share in shares],
        totals[0:3][None],
        totals[3:6][None],
        totals[6:10].reshape(1, 4096),
        totals[10:14].reshape(1, 4096),
        head_sums,
    )


def fits(mesh, boundary, mid_gain, head_scale):
    sizes = (mesh.shape["section"], mesh.shape["dp"], mesh.shape["shard"])
    return (
        sizes == (2, 4, 4)
        and boundary == (2, 4, 4, 1024, 1024)
        and mid_gain == (2, 4096)
        and head_scale == (2, 16)
    )


def solution(mesh):
    placed = (
        P("section", None, "shard", "dp", None),
        P(None, "shard"),
        P("section", "shard", None),
        P("section", "shard", None),
        P("section", "shard", None),
        P("section", "shard", None),
        P("section", None, None),
        P("section", None, None),
        P("section", None),
        P("section", None),
        P("section", None),
    )
    results = (
        P("section", None, "shard", "dp", None),
        P("section", "shard", None),
        P("section", "shard", None),
        P("section", "shard", None),
        P("section", "shard", None),
        P("section", None, None),
        P("section", None, None),
        P("section", None),
        P("section", None),
        P("section", None),
    )

    def whole(*arrays):
        fast = fits(mesh, arrays[0].shape, arrays[8].shape, arrays[10].shape)
        body = local if fast else general
        return jax.shard_map(
            body, mesh=mesh, in_specs=placed, out_specs=results, check_vma=False
        )(*arrays)

    return whole
```

```python
import functools
import math
from typing import NamedTuple

import jax
import jax.numpy as jnp
from jax import lax
from jax.experimental import pallas as pl
from jax.experimental.pallas import tpu as pltpu
from jax.sharding import PartitionSpec as P

EPSILON = 1e-05


def shifted(value, axis, steps):
    count = lax.axis_size(axis)
    first, last = (max(0, -steps), min(count, count - steps))
    return lax.ppermute(value, axis, [(source, source + steps) for source in range(first, last)])


def normalize(values_in, gain, shift):
    centre = values_in - jnp.mean(values_in, axis=-1, keepdims=True)
    spread = jnp.mean(centre * centre, axis=-1, keepdims=True)
    return centre * lax.rsqrt(spread + EPSILON) * gain + shift


def middle_norm(hidden, mid_gain, mid_shift):
    return normalize(jax.nn.gelu(hidden, approximate=False), mid_gain, mid_shift)


def contract_rows(left, right):
    return lax.dot_general(
        left, right, (((0,), (0,)), ((), ())), preferred_element_type=jnp.float32
    )


def contract_cols(left, right):
    return lax.dot_general(
        left, right, (((1,), (1,)), ((), ())), preferred_element_type=jnp.float32
    )


def visible(query_place, key_place, split_at):
    same_doc = (query_place[:, None] < split_at) == (key_place[None, :] < split_at)
    return same_doc & (key_place[None, :] <= query_place[:, None])


def forward_parts(stream_in, weights, small, split_at, head_count):
    weight_qkv, weight_out, weight_up, weight_down = weights
    gains, shifts, mid_gain, mid_shift, head_scale = small
    row_count, model_width = stream_in.shape
    head_dim = model_width // head_count
    factor = 1.0 / math.sqrt(head_dim)
    normed = normalize(stream_in, gains[0], shifts[0]).astype(jnp.bfloat16)
    projected = jnp.dot(normed, weight_qkv, preferred_element_type=jnp.float32).astype(jnp.bfloat16)
    queries = projected[:, :model_width].reshape(row_count, head_count, head_dim)
    key_rows = projected[:, model_width : 2 * model_width].reshape(row_count, head_count, head_dim)
    value_rows = projected[:, 2 * model_width :].reshape(row_count, head_count, head_dim)
    keys_all, values_all = (
        lax.all_gather(key_rows, "dp", axis=0, tiled=True),
        lax.all_gather(value_rows, "dp", axis=0, tiled=True),
    )
    seq_len = keys_all.shape[0]
    own_place = lax.axis_index("dp") * row_count + jnp.arange(row_count, dtype=jnp.int32)
    all_place = jnp.arange(seq_len, dtype=jnp.int32)
    allowed = visible(own_place, all_place, split_at)
    scores = (
        jnp.einsum("qhd,khd->hqk", queries, keys_all, preferred_element_type=jnp.float32) * factor
    )
    scores = jnp.where(allowed[None], scores, -1e30)
    row_max = jnp.max(scores, axis=-1, keepdims=True)
    log_total = row_max + jnp.log(jnp.sum(jnp.exp(scores - row_max), axis=-1, keepdims=True))
    attend = jnp.exp(scores - log_total)
    attend_low = attend.astype(jnp.bfloat16)
    head_out = jnp.einsum(
        "hqk,khd->qhd", attend_low, values_all, preferred_element_type=jnp.float32
    )
    scaled = (
        (head_out * head_scale[None, :, None]).astype(jnp.bfloat16).reshape(row_count, model_width)
    )
    branch = jnp.dot(scaled, weight_out, preferred_element_type=jnp.float32)
    residual = stream_in + normalize(branch, gains[1], shifts[1])
    ffn_input = normalize(residual, gains[2], shifts[2]).astype(jnp.bfloat16)
    hidden = jnp.dot(ffn_input, weight_up, preferred_element_type=jnp.float32)
    middle = middle_norm(hidden, mid_gain, mid_shift).astype(jnp.bfloat16)
    return dict(
        normed=normed,
        queries=queries,
        key_rows=key_rows,
        value_rows=value_rows,
        keys_all=keys_all,
        values_all=values_all,
        own_place=own_place,
        all_place=all_place,
        attend=attend,
        attend_low=attend_low,
        log_total=log_total,
        head_out=head_out,
        scaled=scaled,
        branch=branch,
        residual=residual,
        ffn_input=ffn_input,
        hidden=hidden,
        middle=middle,
        factor=factor,
    )


def backward_parts(stream_in, grad_in, weights, small, split_at, head_count):
    weight_qkv, weight_out, weight_up, weight_down = weights
    gains, shifts, mid_gain, mid_shift, head_scale = small
    parts = forward_parts(stream_in, weights, small, split_at, head_count)
    row_count, model_width = stream_in.shape
    head_dim = model_width // head_count
    factor = parts["factor"]
    grad_down = contract_rows(parts["middle"], grad_in)
    d_middle = contract_cols(grad_in, weight_down)
    unused, pull_middle = jax.vjp(middle_norm, parts["hidden"], mid_gain, mid_shift)
    d_hidden, grad_mid_gain, grad_mid_shift = pull_middle(d_middle)
    d_hidden = d_hidden.astype(jnp.bfloat16)
    grad_up = contract_rows(parts["ffn_input"], d_hidden)
    d_ffn_input = contract_cols(d_hidden, weight_up)
    unused, pull_third = jax.vjp(normalize, parts["residual"], gains[2], shifts[2])
    d_residual, gain_third, shift_third = pull_third(d_ffn_input)
    d_residual = d_residual + grad_in.astype(jnp.float32)
    unused, pull_second = jax.vjp(normalize, parts["branch"], gains[1], shifts[1])
    d_branch, gain_second, shift_second = pull_second(d_residual)
    d_branch = d_branch.astype(jnp.bfloat16)
    grad_out = contract_rows(parts["scaled"], d_branch)
    d_scaled = contract_cols(d_branch, weight_out).reshape(row_count, head_count, head_dim)
    grad_head_scale = jnp.sum(d_scaled * parts["head_out"], axis=(0, 2))
    d_heads = (d_scaled * head_scale[None, :, None]).astype(jnp.bfloat16)
    attend = parts["attend"]
    d_attend = jnp.einsum(
        "qhd,khd->hqk", d_heads, parts["values_all"], preferred_element_type=jnp.float32
    )
    row_dot = jnp.sum(attend * d_attend, axis=-1, keepdims=True)
    d_scores = (attend * (d_attend - row_dot)).astype(jnp.bfloat16)
    d_query = (
        jnp.einsum("hqk,khd->qhd", d_scores, parts["keys_all"], preferred_element_type=jnp.float32)
        * factor
    ).astype(jnp.bfloat16)
    full_keys = (
        jnp.einsum("hqk,qhd->khd", d_scores, parts["queries"], preferred_element_type=jnp.float32)
        * factor
    )
    full_values = jnp.einsum(
        "hqk,qhd->khd", parts["attend_low"], d_heads, preferred_element_type=jnp.float32
    )
    d_keys, d_values = (
        lax.psum_scatter(full_keys, "dp", scatter_dimension=0, tiled=True),
        lax.psum_scatter(full_values, "dp", scatter_dimension=0, tiled=True),
    )
    d_projected = jnp.concatenate(
        [
            d_query.reshape(row_count, model_width),
            d_keys.astype(jnp.bfloat16).reshape(row_count, model_width),
            d_values.astype(jnp.bfloat16).reshape(row_count, model_width),
        ],
        axis=1,
    )
    grad_qkv = contract_rows(parts["normed"], d_projected)
    d_normed = contract_cols(d_projected, weight_qkv)
    unused, pull_first = jax.vjp(normalize, stream_in, gains[0], shifts[0])
    d_entry, gain_first, shift_first = pull_first(d_normed)
    d_entry = d_entry + d_residual
    big_grads = (grad_qkv, grad_out, grad_up, grad_down)
    small_grads = (
        jnp.stack([gain_first, gain_second, gain_third]),
        jnp.stack([shift_first, shift_second, shift_third]),
        grad_mid_gain,
        grad_mid_shift,
        grad_head_scale,
    )
    return (d_entry, big_grads, small_grads)


def add_up(first_term, second_term):
    return first_term + second_term


def general(
    boundary,
    first_len,
    qkv_weight,
    out_weight,
    up_weight,
    down_weight,
    norm_gain,
    norm_shift,
    mid_gain,
    mid_shift,
    head_scale,
):
    section_index = lax.axis_index("section")
    gathered = (
        lax.all_gather(qkv_weight, "shard", axis=1, tiled=True),
        lax.all_gather(out_weight, "shard", axis=1, tiled=True),
        lax.all_gather(up_weight, "shard", axis=1, tiled=True),
        lax.all_gather(down_weight, "shard", axis=1, tiled=True),
    )
    weights = tuple((piece[0] for piece in gathered))
    small = (norm_gain[0], norm_shift[0], mid_gain[0], mid_shift[0], head_scale[0])
    head_count = head_scale.shape[1]
    micro = boundary.shape[1]
    row_count = boundary.shape[3]
    model_width = boundary.shape[4]
    local_ends = boundary[0, :, 0]
    splits = first_len[:, 0]

    def forward_tick(step_index, carry):
        incoming, kept, ends = carry
        index = step_index - section_index
        active = (index >= 0) & (index < micro)
        slot = jnp.clip(index, 0, micro - 1)
        entry = jnp.where(section_index == 0, local_ends[slot], incoming)
        parts = forward_parts(entry.astype(jnp.float32), weights, small, splits[slot], head_count)
        result = (
            parts["residual"]
            + jnp.dot(parts["middle"], weights[3], preferred_element_type=jnp.float32)
        ).astype(jnp.bfloat16)
        kept = kept.at[slot].set(jnp.where(active, entry, kept[slot]))
        ends = ends.at[slot].set(jnp.where(active, result, ends[slot]))
        incoming = shifted(result, "section", 1)
        return (incoming, kept, ends)

    blank = jnp.zeros((row_count, model_width), jnp.bfloat16)
    stack_blank = jnp.zeros((micro, row_count, model_width), jnp.bfloat16)
    unused, kept, ends = lax.fori_loop(
        0, micro + 1, forward_tick, (blank, stack_blank, stack_blank)
    )

    def backward_tick(step_index, carry):
        incoming, ends, big_sums, small_sums = carry
        index = micro - step_index - section_index
        active = (index >= 0) & (index < micro)
        slot = jnp.clip(index, 0, micro - 1)
        grad_in = jnp.where(section_index == 1, local_ends[slot], incoming)
        grad_in = jnp.where(active, grad_in, jnp.zeros_like(grad_in))
        d_entry, big_grads, small_grads = backward_parts(
            kept[slot].astype(jnp.float32), grad_in, weights, small, splits[slot], head_count
        )
        d_low = d_entry.astype(jnp.bfloat16)
        ends = ends.at[slot].set(jnp.where(active & (section_index == 0), d_low, ends[slot]))
        big_sums = jax.tree.map(add_up, big_sums, big_grads)
        small_sums = jax.tree.map(add_up, small_sums, small_grads)
        incoming = shifted(d_low, "section", -1)
        return (incoming, ends, big_sums, small_sums)

    big_zero = tuple((jnp.zeros(item.shape, jnp.float32) for item in weights))
    small_zero = tuple((jnp.zeros(item.shape, jnp.float32) for item in small))
    unused, ends, big_sums, small_sums = lax.fori_loop(
        0, micro + 1, backward_tick, (blank, ends, big_zero, small_zero)
    )
    shares = (
        lax.psum_scatter(big_sums[0][None], "shard", scatter_dimension=1, tiled=True),
        lax.psum_scatter(big_sums[1][None], "shard", scatter_dimension=1, tiled=True),
        lax.psum_scatter(big_sums[2][None], "shard", scatter_dimension=1, tiled=True),
        lax.psum_scatter(big_sums[3][None], "shard", scatter_dimension=1, tiled=True),
    )
    shares = lax.psum((shares[0], shares[1], shares[2], shares[3]), "dp")
    totals = lax.psum(
        (small_sums[0], small_sums[1], small_sums[2], small_sums[3], small_sums[4]), ("dp", "shard")
    )
    return (
        ends[None, :, None],
        shares[0],
        shares[1],
        shares[2],
        shares[3],
        totals[0][None],
        totals[1][None],
        totals[2][None],
        totals[3][None],
        totals[4][None],
    )


def pick(value, index):
    return lax.dynamic_index_in_dim(value, index, 0, keepdims=False)


BF16 = jnp.bfloat16
F32 = jnp.float32
TILE = 256
SECTION, DP, SHARD = "section", "dp", "shard"


def rows_spec(columns):
    return pl.BlockSpec((TILE, columns), lambda step: (step, 0))


def group_spec(columns):
    return pl.BlockSpec((4, TILE, columns), lambda step: (0, step, 0))


def array(shape, dtype):
    return jax.ShapeDtypeStruct(shape, dtype)


def dot(left, right):
    return jnp.dot(left, right, preferred_element_type=F32)


def dot_nt(left, right):
    return lax.dot_general(left, right, (((1,), (1,)), ((), ())), preferred_element_type=F32)


def standard(values_in):
    centre = values_in - jnp.mean(values_in, axis=-1, keepdims=True)
    spread_of = jnp.mean(centre * centre, axis=-1, keepdims=True)
    scale = lax.rsqrt(spread_of + EPSILON)
    return centre * scale, scale


def standard_back(unit_values, scale, gain, grad):
    inner = grad * gain
    first = jnp.mean(inner, axis=-1, keepdims=True)
    second = jnp.mean(inner * unit_values, axis=-1, keepdims=True)
    back = scale * (inner - first - unit_values * second)
    return back, jnp.sum(grad * unit_values, axis=0, keepdims=True), jnp.sum(grad, axis=0, keepdims=True)


def lane_masks(rows):
    lanes = lax.broadcasted_iota(jnp.int32, (rows, 128), 1)
    return lanes < 64


def two_columns(first, second):
    return jnp.where(lane_masks(first.shape[0]), first, second)


def mid_stats(own, other):
    mean_own, mean_other = own[:, 0:1], other[:, 0:1]
    gap = mean_own - mean_other
    spread_of = 0.5 * (own[:, 64:65] + other[:, 64:65]) + 0.25 * gap * gap
    return 0.5 * (mean_own + mean_other), lax.rsqrt(spread_of + EPSILON)


def fill_triangle(triangle_ref):
    keys = lax.broadcasted_iota(jnp.int32, (256, 256), 0)
    queries = lax.broadcasted_iota(jnp.int32, (256, 256), 1)
    triangle_ref[...] = jnp.where(keys <= queries, 0.0, -1e30)


def own_lanes(rows, half):
    lane = lax.broadcasted_iota(jnp.int32, (rows, 128), 1)
    return (lane < 64 if half == 0 else lane >= 64), lane == 64 * (1 - half)


def walled_keys(keys, split_at, half):
    mine, spare = own_lanes(1024, half)
    row = lax.broadcasted_iota(jnp.int32, (1024, 128), 0)
    return jnp.where(mine, keys, jnp.where(spare & (row < split_at), -1e30, 0.0).astype(BF16))


def walled_queries(queries, split_at, half, start):
    mine, spare = own_lanes(256, half)
    row = lax.broadcasted_iota(jnp.int32, (256, 128), 0) + start
    return jnp.where(mine, queries, jnp.where(spare & (row >= split_at), 1.0, 0.0).astype(BF16))


def score_parts(keys_ref, queries, block, triangle_ref):
    parts = []
    for part in range(2 * (block + 1)):
        scores = dot_nt(keys_ref[part * 128 : part * 128 + 128, :], queries)
        if part >= 2 * block:
            scores = scores + triangle_ref[(part - 2 * block) * 128 : (part - 2 * block) * 128 + 128, :]
        parts.append(scores)
    return parts


def run_lagged(first, second):
    tasks = [(block, half) for block in (3, 2, 1, 0) for half in (0, 1)]
    before = None
    for task in tasks:
        held = first(*task)
        if before is not None:
            second(*before)
        before = (*task, held)
    second(*before)


def attend(q_ref, k_ref, v_ref, scale_row, out_ref, scaled_ref, log_ref, split_at, triangle_ref, turned_ref, keys_ref):
    turned_ref[...] = v_ref[0].astype(F32).T.astype(BF16)
    for half in range(2):
        keys_ref[half] = walled_keys(k_ref[0], split_at, half)
    found = {}

    def score(block, half):
        queries = (q_ref[0, pl.ds(block * 256, 256), :] * 0.125).astype(BF16)
        parts = score_parts(keys_ref.at[half], walled_queries(queries, split_at, half, block * 256), block, triangle_ref)
        tops = functools.reduce(jnp.maximum, [jnp.max(part.reshape(16, 8, 256), axis=0) for part in parts])
        return parts, jnp.max(tops, axis=0, keepdims=True)

    def mix(block, half, held):
        parts, top = held
        span = pl.ds(block * 256, 256)
        powers = [jnp.exp(part - top) for part in parts]
        total = functools.reduce(jnp.add, [jnp.sum(power.reshape(16, 8, 256), axis=0) for power in powers])
        total = jnp.sum(total, axis=0, keepdims=True)
        low = jnp.concatenate([power.astype(BF16) for power in powers], axis=0)
        mixed = dot(turned_ref[half * 64 : half * 64 + 64, : (block + 1) * 256], low)
        log_ref[0, half : half + 1, span] = top + jnp.log(total)
        found[half] = mixed * (1.0 / total)
        if half == 1:
            head_out = jnp.concatenate([found[0], found[1]], axis=0).T
            out_ref[span, :] = head_out.astype(BF16)
            scaled_ref[span, :] = (head_out * scale_row).astype(BF16)

    run_lagged(score, mix)


def attend_back(
    q_ref, k_ref, v_ref, grad_ref, out_ref, log_ref, back_ref, split_at, triangle_ref, turned_ref, keys_ref, dk_ref, dv_ref
):
    turned_ref[...] = k_ref[0].astype(F32).T.astype(BF16)
    for half in range(2):
        keys_ref[half] = walled_keys(k_ref[0], split_at, half)
    products, found = {}, {}

    def score(block, half):
        span = pl.ds(block * 256, 256)
        mine, unused = own_lanes(256, half)
        queries = (q_ref[0, span, :] * 0.125).astype(BF16)
        grad = grad_ref[span, :]
        own_grad = jnp.where(mine, grad, 0.0).astype(BF16)
        if half == 0:
            products[block] = (grad.astype(F32) * out_ref[span, :].astype(F32)).T
        row_dot = jnp.sum(products[block][half * 64 : half * 64 + 64, :], axis=0, keepdims=True)
        parts = score_parts(keys_ref.at[half], walled_queries(queries, split_at, half, block * 256), block, triangle_ref)
        lows, grads = [], []
        for part, scores in enumerate(parts):
            attend_part = jnp.exp(scores - log_ref[0, half : half + 1, span])
            d_attend = dot_nt(v_ref[0, part * 128 : part * 128 + 128, :], own_grad)
            lows.append(attend_part.astype(BF16))
            grads.append((attend_part * (d_attend - row_dot)).astype(BF16))
        own_queries = jnp.where(mine, queries, 0.0).astype(BF16)
        return jnp.concatenate(lows, axis=0), jnp.concatenate(grads, axis=0), own_queries, own_grad

    def mix(block, half, held):
        low, d_scores, own_queries, own_grad = held
        seen = pl.ds(0, (block + 1) * 256)
        found[half] = dot(turned_ref[half * 64 : half * 64 + 64, : (block + 1) * 256], d_scores)
        if (block, half) == (3, 0):
            dv_ref[...] = dot(low, own_grad)
            dk_ref[...] = dot(d_scores, own_queries)
        else:
            dv_ref[seen, :] += dot(low, own_grad)
            dk_ref[seen, :] += dot(d_scores, own_queries)
        if half == 1:
            d_query = jnp.concatenate([found[0], found[1]], axis=0).T * 0.125
            back_ref[0, pl.ds(block * 256, 256), 0:128] = d_query.astype(BF16)

    run_lagged(score, mix)
    back_ref[0, :, 128:256] = dk_ref[...].astype(BF16)
    back_ref[0, :, 256:384] = dv_ref[...].astype(BF16)


MESH = pl.DeviceIdType.MESH
SIZES = ((256, 384), (128, 256), (256, 512), (512, 256))


def partner(place, step):
    return {0: place, 1: place + 1 - 2 * lax.rem(place, 2), 2: lax.rem(place + 2, 4), 3: 3 - place}[step]


def here():
    return lax.axis_index("section"), lax.axis_index("dp"), lax.axis_index("shard")


def greet(core, place, depth):
    barrier = pltpu.get_barrier_semaphore()
    targets = [{SHARD: lax.rem(depth + step, 4)} for step in (1, 2, 3)]
    targets += [{SECTION: 1 - core, SHARD: lax.rem(depth + step, 4)} for step in range(4)]
    targets += [{DP: partner(place, step)} for step in (1, 2, 3)]
    for target in targets:
        pl.semaphore_signal(barrier, inc=1, device_id=target, device_id_type=MESH)
    pl.semaphore_wait(barrier, len(targets))


def send(source, target, send_sem, recv_sem, device):
    copy = pltpu.make_async_remote_copy(
        src_ref=source, dst_ref=target, send_sem=send_sem, recv_sem=recv_sem,
        device_id=device, device_id_type=MESH,
    )
    copy.start()


def await_bytes(view, sem):
    pltpu.make_async_copy(view, view, sem).wait()


def lanes(start, size):
    return pl.ds(pl.multiple_of(start, 128), size)


def raw_views(raw, matrix, half, quarter):
    if matrix == 0:
        return [raw[0].at[:, lanes(third * 1024 + quarter * 256 + half * 128, 128)] for third in range(3)]
    if matrix == 1:
        return [raw[1].at[pl.ds(half * 128, 128), lanes(quarter * 256, 256)]]
    if matrix == 2:
        return [raw[2].at[:, lanes(quarter * 1024 + half * 512, 512)]]
    return [raw[3].at[pl.ds(half * 512, 512), lanes(quarter * 256, 256)]]


def whole_view(whole, matrix, quarter, shard):
    if matrix in (0, 2):
        return whole[matrix].at[quarter, shard]
    return whole[matrix].at[shard, :, lanes(quarter * 256, 256)]


def whole_views(whole, matrix, quarter, shard):
    if matrix == 0:
        return [whole[0].at[quarter, shard, :, pl.ds(third * 128, 128)] for third in range(3)]
    return [whole_view(whole, matrix, quarter, shard)]


def pieces_view(whole, matrix, first, second):
    if matrix in (0, 2):
        return whole[matrix].at[pl.ds(0, first), pl.ds(0, second)]
    return whole[matrix].at[pl.ds(0, first), :, pl.ds(0, 256 * second)]


class Saved(NamedTuple):
    entry: object
    normed: object
    proj: object
    head_out: object
    scaled: object
    logs: object
    branch: object
    branch_other: object
    residual: object
    ffn_input: object
    gelu: object
    slope: object
    middle: object


def whole_spec(shape):
    return pl.BlockSpec(shape, lambda step: (0,) * len(shape), pipeline_mode=pl.Buffered(1))


def block_spec(rows, columns):
    return pl.BlockSpec((1, rows, columns), lambda step: (step, 0, 0))


def grad_spec(columns):
    return pl.BlockSpec((1, 4, 256, columns), lambda step: (step, 0, 0, 0))


def column_spec(columns):
    return pl.BlockSpec((1024, columns), lambda step: (0, step))


def third_spec(third):
    return pl.BlockSpec((1, 1024, 128), lambda group: (group, 0, third))


def stage(body, ins, outs, hooks=()):
    def hooked(*refs):
        body(*refs)
        for step, action in hooks:
            pl.when(pl.program_id(0) == step)(action)

    pltpu.emit_pipeline(
        hooked, grid=(4,), in_specs=[spec for unused, spec in ins], out_specs=[spec for unused, spec in outs]
    )(*[ref for ref, unused in ins], *[ref for ref, unused in outs])


def after(*actions):
    def run():
        for action, *arguments in actions:
            action(*arguments)

    return run


def block_rows(index):
    return pl.ds(pl.multiple_of(index * 256, 256), 256)


def forward_part(items, raw, small_in, cotangent, wholes, saved, smalls, split_ref, attention_refs, swaps, stats, sems):
    gains, shifts, mid_gain, mid_shift, head_row = smalls
    triangle, turned, walled = attention_refs
    (item_send, item_recv, item_pass, own_send, own_recv, deep_send, deep_recv, hop_send, hop_recv, small_sems,
     swap_send, swap_recv, keep_sem) = sems
    core, place, depth = here()
    arrays = (saved[0].entry, cotangent)
    greet(core, place, depth)

    def items_out(layer):
        @pl.when(core == layer)
        def unused():
            for step in (1, 2, 3):
                send(items.at[partner(place, step)], arrays[layer].at[block_rows(place)], item_send.at[layer, step],
                     item_recv.at[layer, step], {DP: partner(place, step)})
            pltpu.make_async_copy(items.at[place], arrays[layer].at[block_rows(place)], item_send.at[layer, 0]).start()
            send(items.at[place], arrays[layer].at[block_rows(place)], item_pass.at[layer, 0], item_recv.at[layer, 0],
                 {SECTION: 1 - layer})

    def smalls_out():
        for layer in (0, 1):
            @pl.when(core == layer)
            def unused():
                for index, (source, target) in enumerate(zip(small_in, smalls)):
                    pltpu.make_async_copy(source, target.at[layer], small_sems.at[0, index]).start()
                    send(source, target.at[layer], small_sems.at[1, index], small_sems.at[2, index],
                         {SECTION: 1 - layer})

    units = [(layer, matrix) for layer in (0, 1) for matrix in range(4)]

    def deep(unit):
        layer, matrix = units[unit]

        @pl.when(core == layer)
        def unused():
            for step in (1, 2, 3):
                for half in (0, 1):
                    for source, target in zip(
                        raw_views(raw, matrix, half, place), whole_views(wholes[layer], matrix, place, depth)
                    ):
                        send(source, target, deep_send.at[unit], deep_recv.at[unit, step],
                             {SECTION: half, SHARD: lax.rem(depth + 4 - step, 4)})

    def own(unit):
        layer, matrix = units[unit]

        @pl.when(core == layer)
        def unused():
            for quarter in range(4):
                for source, target in zip(
                    raw_views(raw, matrix, layer, quarter), whole_views(wholes[layer], matrix, quarter, depth)
                ):
                    pltpu.make_async_copy(source, target, own_send.at[unit, 0]).start()
                for source, target in zip(
                    raw_views(raw, matrix, 1 - layer, quarter), whole_views(wholes[layer], matrix, quarter, depth)
                ):
                    send(source, target, own_send.at[unit, 1], own_recv.at[unit], {SECTION: 1 - layer})

    def route(unit, step):
        return (1, 2) if (unit + step) % 2 == 0 else (2, 1)

    def piece(unit, offset, step):
        layer, matrix = units[unit]
        return whole_view(wholes[layer], matrix, partner(place, offset), lax.rem(depth + step, 4))

    def first_hop(unit):
        for step in (1, 2, 3):
            first, second = route(unit, step)
            await_bytes(piece(unit, 0, step), deep_recv.at[unit, step])
            for offset in (first, second):
                send(piece(unit, 0, step), piece(unit, 0, step), hop_send.at[unit], hop_recv.at[unit, step - 1, offset - 1],
                     {DP: partner(place, offset)})

    def second_hop(unit):
        for step in (1, 2, 3):
            first, second = route(unit, step)
            await_bytes(piece(unit, first, step), hop_recv.at[unit, step - 1, first - 1])
            send(piece(unit, first, step), piece(unit, first, step), hop_send.at[unit], hop_recv.at[unit, step - 1, 2],
                 {DP: partner(place, second)})

    def ready(unit):
        layer, matrix = units[unit]
        quarters = pieces_view(wholes[layer], matrix, 2, 2)

        @pl.when(core == layer)
        def unused():
            await_bytes(quarters, own_send.at[unit, 0])

        @pl.when(core != layer)
        def unused_too():
            await_bytes(quarters, own_recv.at[unit])

        for step in (1, 2, 3):
            first, second = route(unit, step)
            await_bytes(piece(unit, 0, 0), hop_recv.at[unit, step - 1, second - 1])
            await_bytes(piece(unit, 0, 0), hop_recv.at[unit, step - 1, 2])

    def pass_on(layer):
        @pl.when(core == layer)
        def unused():
            for step in (1, 2, 3):
                block = arrays[layer].at[block_rows(partner(place, step))]
                await_bytes(block, item_recv.at[layer, step])
                send(block, block, item_pass.at[layer, step], item_recv.at[layer, step], {SECTION: 1 - layer})

    def passed(layer):
        @pl.when(core == layer)
        def unused():
            await_bytes(items.at[0], item_send.at[layer, 0])

        @pl.when(core != layer)
        def unused_too():
            for step in range(4):
                await_bytes(items.at[0], item_recv.at[layer, step])

    def take_smalls():
        for index, (source, target) in enumerate(zip(small_in, smalls)):
            for layer in (0, 1):
                @pl.when(core == layer)
                def unused():
                    await_bytes(source, small_sems.at[0, index])

                @pl.when(core != layer)
                def unused_too():
                    await_bytes(source, small_sems.at[2, index])

    def keep(index, source, target):
        pltpu.make_async_copy(source, target, keep_sem.at[index]).start()

    def kept(index, source):
        await_bytes(source, keep_sem.at[index])

    def swap_tile(index, pair, value):
        own_ref, other_ref = pair
        span = block_rows(pl.program_id(0))
        own_ref[span, :] = value
        send(own_ref.at[span], other_ref.at[span], swap_send.at[index], swap_recv.at[index], {SECTION: 1 - core})

    def swapped(index, pair):
        await_bytes(pair[0], swap_send.at[index])
        await_bytes(pair[1], swap_recv.at[index])

    def mid_row(ref, layer, group):
        return ref[layer, :, lanes(group * 1024 + core * 512, 512)]

    def project_rows(layer, x, normed_ref, proj_ref, w_ref):
        unit_x, unused = standard(x)
        normed = (unit_x * gains[layer, 0:1, :] + shifts[layer, 0:1, :]).astype(BF16)
        normed_ref[...] = normed
        for group in range(4):
            proj_ref[group] = dot(normed, w_ref[group].reshape(1024, 384)).astype(BF16)

    def project_stage(layer, hooks):
        own_half = saved[layer]
        weight = (wholes[layer][0], whole_spec((4, 4, 256, 384)))
        made = [(own_half.normed, rows_spec(1024)), (own_half.proj, group_spec(384))]

        def body_first(x_ref, w_ref, normed_ref, proj_ref):
            project_rows(layer, x_ref[...].astype(F32), normed_ref, proj_ref, w_ref)

        def body_next(res_ref, a_ref, b_ref, w_ref, normed_ref, proj_ref, entry_ref):
            entry = (res_ref[...] + (a_ref[...].astype(F32) + b_ref[...].astype(F32))).astype(BF16)
            entry_ref[...] = entry
            project_rows(layer, entry.astype(F32), normed_ref, proj_ref, w_ref)

        if layer == 0:
            stage(body_first, [(own_half.entry, rows_spec(1024)), weight], made, hooks)
        else:
            stage(
                body_next,
                [(saved[0].residual, rows_spec(1024)), (swaps[1][0], rows_spec(1024)), (swaps[1][1], rows_spec(1024)), weight],
                [*made, (own_half.entry, rows_spec(1024))],
                hooks,
            )

    def attention_stage(layer, hooks):
        own_half = saved[layer]

        def body(q_ref, k_ref, v_ref, out_ref, scaled_ref, log_ref):
            scale_row = head_row[layer, :, lanes(pl.program_id(0) * 256 + core * 128, 128)]
            attend(
                q_ref, k_ref, v_ref, scale_row, out_ref, scaled_ref, log_ref, split_ref[0], triangle, turned, walled
            )

        stage(
            body,
            [(own_half.proj, third_spec(0)), (own_half.proj, third_spec(1)), (own_half.proj, third_spec(2))],
            [(own_half.head_out, column_spec(128)), (own_half.scaled, column_spec(128)),
             (own_half.logs, pl.BlockSpec((1, 2, 1024), lambda group: (group, 0, 0)))],
            hooks,
        )

    def out_stage(layer, hooks):
        def body(scaled_ref, w_ref):
            swap_tile(layer * 2, swaps[layer * 2], dot(scaled_ref[...], w_ref[...].reshape(512, 1024)).astype(BF16))

        stage(body, [(saved[layer].scaled, rows_spec(512)), (wholes[layer][1], whole_spec((4, 128, 1024)))], [], hooks)

    def widen_stage(layer, hooks):
        own_half = saved[layer]

        def body(x_ref, a_ref, b_ref, w_ref, res_ref, ffn_ref, gelu_ref, slope_ref):
            branch = a_ref[...].astype(F32) + b_ref[...].astype(F32)
            unit_b, unused = standard(branch)
            residual = x_ref[...].astype(F32) + unit_b * gains[layer, 1:2, :] + shifts[layer, 1:2, :]
            res_ref[...] = residual
            unit_r, unused = standard(residual)
            ffn_input = (unit_r * gains[layer, 2:3, :] + shifts[layer, 2:3, :]).astype(BF16)
            ffn_ref[...] = ffn_input
            first, second = [], []
            for group in range(4):
                hidden = dot(ffn_input, w_ref[group].reshape(1024, 512))
                half = 0.5 + 0.5 * lax.erf(hidden * math.sqrt(0.5))
                gelu = hidden * half
                bell = jnp.exp(-0.5 * hidden * hidden) * (1.0 / math.sqrt(2.0 * math.pi))
                gelu_ref[group] = gelu.astype(BF16)
                slope_ref[group] = (half + hidden * bell).astype(BF16)
                mean = jnp.mean(gelu, axis=-1, keepdims=True)
                centre = gelu - mean
                first.append(mean)
                second.append(jnp.mean(centre * centre, axis=-1, keepdims=True))
            mean = 0.25 * (first[0] + first[1] + first[2] + first[3])
            spread_of = sum(0.25 * (s + (m - mean) * (m - mean)) for m, s in zip(first, second))
            swap_tile(3 + layer, stats[layer], two_columns(mean, spread_of))

        branch_own, branch_other = swaps[layer * 2]
        stage(
            body,
            [(own_half.entry, rows_spec(1024)), (branch_own, rows_spec(1024)), (branch_other, rows_spec(1024)),
             (wholes[layer][2], whole_spec((4, 4, 256, 512)))],
            [(own_half.residual, rows_spec(1024)), (own_half.ffn_input, rows_spec(1024)), (own_half.gelu, group_spec(512)),
             (own_half.slope, group_spec(512))],
            hooks,
        )

    def middle_rows(layer, gelu, mean, scale, group):
        unit_m = (gelu.astype(F32) - mean) * scale
        return (unit_m * mid_row(mid_gain, layer, group) + mid_row(mid_shift, layer, group)).astype(BF16)

    def narrow_stage(layer, hooks):
        own_half = saved[layer]

        def body(g_ref, own_ref, other_ref, w_ref, mid_ref):
            mean, scale = mid_stats(own_ref[...], other_ref[...])
            total = jnp.zeros((TILE, 1024), F32)
            for group in range(4):
                middle = middle_rows(layer, g_ref[group], mean, scale, group)
                mid_ref[group] = middle
                total = total + dot(middle, w_ref[group])
            swap_tile(1, swaps[1], total.astype(BF16))

        stage(
            body,
            [(own_half.gelu, group_spec(512)), (stats[layer][0], rows_spec(128)), (stats[layer][1], rows_spec(128)),
             (wholes[layer][3], whole_spec((4, 512, 1024)))],
            [(own_half.middle, group_spec(512))],
            hooks,
        )

    def middle_stage(layer, hooks):
        own_half = saved[layer]

        def body(g_ref, own_ref, other_ref, mid_ref):
            mean, scale = mid_stats(own_ref[...], other_ref[...])
            for group in range(4):
                mid_ref[group] = middle_rows(layer, g_ref[group], mean, scale, group)

        stage(
            body,
            [(own_half.gelu, group_spec(512)), (stats[layer][0], rows_spec(128)), (stats[layer][1], rows_spec(128))],
            [(own_half.middle, group_spec(512))],
            hooks,
        )

    def layer_forward(layer, hooks, gaps):
        own_half = saved[layer]
        base = layer * 4
        gaps[0]()
        ready(base)
        if layer == 0:
            passed(0)
            take_smalls()
        else:
            swapped(1, swaps[1])
        project_stage(layer, hooks[0])
        attention_stage(layer, hooks[1])
        gaps[1]()
        ready(base + 1)
        out_stage(layer, hooks[2])
        gaps[2]()
        ready(base + 2)
        swapped(layer * 2, swaps[layer * 2])
        for index, (source, target) in enumerate(zip(swaps[layer * 2], (own_half.branch, own_half.branch_other))):
            keep(layer * 2 + index, source, target)
        widen_stage(layer, hooks[3])
        gaps[3]()
        swapped(3 + layer, stats[layer])
        if layer == 0:
            ready(base + 3)
            narrow_stage(layer, hooks[4])
        else:
            middle_stage(layer, hooks[4])

    deep(0)
    items_out(0)
    smalls_out()
    own(0)
    deep(1)
    own(1)
    fill_triangle(triangle)
    first_hop(0)
    deep(2)
    pass_on(0)
    first_hop(1)
    second_hop(0)
    own(2)
    deep(3)
    second_hop(1)
    own(3)
    items_out(1)
    layer_forward(0, ((), ((1, after((first_hop, 2), (deep, 4))),), (), (), ()), (
        after(),
        after((pass_on, 1), (own, 4)),
        after((second_hop, 2), (first_hop, 3), (deep, 5), (own, 5)),
        after((second_hop, 3), (first_hop, 4), (deep, 6), (own, 6)),
    ))
    layer_forward(1, (((1, after((second_hop, 5), (first_hop, 6))),), (), (), (), ()), (
        after((second_hop, 4), (first_hop, 5), (deep, 7), (own, 7)),
        after(),
        after((second_hop, 6), (first_hop, 7)),
        after((second_hop, 7),),
    ))

    for layer in (0, 1):
        for index, source in enumerate(swaps[layer * 2]):
            kept(layer * 2 + index, source)
    passed(1)

    def clean_up():
        for layer in (0, 1):
            @pl.when(core == layer)
            def unused():
                for step in (1, 2, 3):
                    await_bytes(items.at[0], item_send.at[layer, step])
                for step in range(4):
                    await_bytes(items.at[0], item_pass.at[layer, step])
                for index, source in enumerate(small_in):
                    await_bytes(source, small_sems.at[1, index])

        for unit, (layer, matrix) in enumerate(units):
            whole = wholes[layer]

            @pl.when(core == layer)
            def unused_too():
                await_bytes(pieces_view(whole, matrix, 2, 2), own_send.at[unit, 1])
                await_bytes(pieces_view(whole, matrix, 3, 2), deep_send.at[unit])

            await_bytes(pieces_view(whole, matrix, 3, 3), hop_send.at[unit])

    return after((ready, 7)), clean_up


ORDER = tuple((layer, matrix) for layer in (1, 0) for matrix in (3, 2, 1, 0))

class Made(NamedTuple):
    d_middle: object
    d_hidden: object
    d_residual: object
    d_branch: object
    d_heads: object
    d_proj: object
    d_entry: object


def add_up_into(target, *terms):
    rows = target.shape[0]

    def step(index, unused):
        span = pl.ds(pl.multiple_of(index * 32, 32), 32)
        total = target[span, :].astype(F32)
        for term in terms:
            total = total + term[span, :].astype(F32)
        target[span, :] = total.astype(BF16)
        return unused

    lax.fori_loop(0, rows // 32, step, 0)


def whole_kernel(*refs):
    refs = list(refs)

    def take(count):
        found = refs[:count]
        del refs[:count]
        return found

    (split_ref,) = take(1)
    items, *raw = take(5)
    small_in = take(5)
    shares = take(4)
    (ends, small_out) = take(2)
    cotangent, output = take(2)
    weights = (take(4), take(4))
    saved = [Saved(*take(13)) for unused in (0, 1)]
    grads = (take(4), take(4))
    made = [Made(*take(7)) for unused in (0, 1)]
    smalls = take(5)
    attention_refs = take(3)
    swaps = [(*take(2),) for unused in range(3)]
    stats = [(*take(2),) for unused in (0, 1)]
    sums = [(*take(2),) for unused in (0, 1)]
    own, first_in, second_in, deep_in = take(4), take(4), take(4), take(4)
    vec, inbox, acc, dk_acc, dv_acc = take(5)
    forward_sems = take(13)
    (load_sem, first_send, first_recv, second_send, second_recv, deep_send, deep_recv, last_send, last_copy,
     last_recv, ends_send, ends_recv, small_send, small_recv, swap_send, swap_recv, credit) = refs
    gains, unused_shifts, mid_gain, unused_mid_shift, head_row = smalls
    triangle, turned, walled = attention_refs
    core, place, depth = here()
    last_ready, clean_up = forward_part(
        items, raw, small_in, cotangent, weights, saved, smalls, split_ref, attention_refs, swaps, stats, forward_sems
    )

    def send_ends(owner, source):
        @pl.when(core == owner)
        def unused():
            for step in (1, 2, 3):
                send(source.at[block_rows(partner(place, step))], ends.at[place], ends_send.at[step], ends_recv.at[step],
                     {DP: partner(place, step)})
            pltpu.make_async_copy(source.at[block_rows(place)], ends.at[place], ends_send.at[0]).start()

    def route(step):
        return (1, 2) if step < 2 else (2, 1)

    def shard_of(step):
        return lax.rem(depth + step, 4)

    def begin(unit):
        layer, matrix = ORDER[unit]
        if unit >= 4:
            pl.semaphore_wait(credit.at[matrix], 2)
        for step in range(4):
            first, second = route(step)
            for index, offset in enumerate((first, 3)):
                send(whole_view(grads[layer], matrix, partner(place, offset), shard_of(step)),
                     first_in[matrix].at[step, index], first_send.at[unit], first_recv.at[unit],
                     {DP: partner(place, first)})
            for index, offset in enumerate((0, second)):
                pltpu.make_async_copy(
                    whole_view(grads[layer], matrix, partner(place, offset), shard_of(step)),
                    own[matrix].at[step, index], load_sem.at[unit],
                ).start()

    def second_hop(unit):
        layer, matrix = ORDER[unit]
        await_bytes(own[matrix], load_sem.at[unit])
        await_bytes(first_in[matrix], first_recv.at[unit])
        for step in range(4):
            first, second = route(step)
            mine = own[matrix].at[step, 1]
            add_up_into(mine, first_in[matrix].at[step, 1])
            send(mine, second_in[matrix].at[step], second_send.at[unit], second_recv.at[unit],
                 {DP: partner(place, second)})

    def deep_hop(unit):
        layer, matrix = ORDER[unit]
        await_bytes(second_in[matrix], second_recv.at[unit])
        for step in (1, 2, 3, 0):
            mine = own[matrix].at[step, 0]
            add_up_into(mine, first_in[matrix].at[step, 0], second_in[matrix].at[step])
            if step:
                send(mine, deep_in[matrix].at[layer, step - 1], deep_send.at[unit], deep_recv.at[unit],
                     {SHARD: shard_of(step)})
        if unit < 4:
            for step in (1, 2):
                pl.semaphore_signal(
                    credit.at[matrix], inc=1, device_id={DP: partner(place, step)}, device_id_type=MESH
                )

    def finish(unit):
        layer, matrix = ORDER[unit]
        await_bytes(deep_in[matrix].at[layer], deep_recv.at[unit])
        mine = own[matrix].at[0, 0]
        add_up_into(mine, *[deep_in[matrix].at[layer, index] for index in range(3)])
        sources = [mine]
        if matrix == 0:
            sources = [mine.at[:, pl.ds(third * 128, 128)] for third in range(3)]
        for half in (0, 1):
            @pl.when(core == half)
            def unused():
                for source, target in zip(sources, raw_views(shares, matrix, half, place)):
                    if half == layer:
                        pltpu.make_async_copy(source, target, last_copy.at[unit]).start()
                        for offset in (1, 2):
                            send(source, target, last_send.at[unit, 0], last_recv.at[unit, half, offset],
                                 {DP: partner(place, offset)})
                    else:
                        send(source, target, last_send.at[unit, 0], last_recv.at[unit, half, 0], {SECTION: layer})

    def forward(unit):
        layer, matrix = ORDER[unit]
        half = 1 - layer

        @pl.when(core == layer)
        def unused():
            views = raw_views(shares, matrix, half, place)
            await_bytes(own[matrix].at[0, 0], last_recv.at[unit, half, 0])
            for view in views:
                for offset in (1, 2):
                    send(view, view, last_send.at[unit, 1], last_recv.at[unit, half, offset],
                         {DP: partner(place, offset)})

    def corner(unit):
        layer, matrix = ORDER[unit]

        @pl.when(core == layer)
        def unused():
            for half in (layer, 1 - layer):
                first, second = (1, 2) if half == 0 else (2, 1)
                await_bytes(own[matrix].at[0, 0], last_recv.at[unit, half, first])
                for view in raw_views(shares, matrix, half, partner(place, first)):
                    send(view, view, last_send.at[unit, 2], last_recv.at[unit, half, 3], {DP: partner(place, second)})

    def free_own(unit):
        layer, matrix = ORDER[unit]

        @pl.when(core == layer)
        def unused():
            await_bytes(own[matrix].at[0], last_send.at[unit, 0])
            await_bytes(own[matrix].at[0, 0], last_copy.at[unit])

        @pl.when(core != layer)
        def unused_too():
            await_bytes(own[matrix].at[0, 0], last_send.at[unit, 0])

    def free_hops(unit):
        layer, matrix = ORDER[unit]
        await_bytes(second_in[matrix], second_send.at[unit])
        await_bytes(deep_in[matrix].at[layer], deep_send.at[unit])
        free_own(unit)

    def clean(unit):
        layer, matrix = ORDER[unit]
        await_bytes(first_in[matrix], first_send.at[unit])
        if unit >= 4:
            free_hops(unit)

        @pl.when(core == layer)
        def unused():
            for row in (1, 2):
                await_bytes(own[matrix].at[0], last_send.at[unit, row])
            for half in (0, 1):
                first, second = (1, 2) if half == 0 else (2, 1)
                await_bytes(own[matrix].at[0, 0], last_recv.at[unit, half, second])
                await_bytes(own[matrix].at[0, 0], last_recv.at[unit, half, 3])

    column = pl.ds(pl.multiple_of(core * 512, 512), 512)
    exchanges = (
        {SECTION: 1 - core},
        {DP: partner(place, 1)},
        {DP: partner(place, 2)},
        {SHARD: partner(depth, 1)},
        {SHARD: partner(depth, 2)},
    )

    def small_step(index):
        if index:
            send(acc.at[index - 1], inbox.at[index], small_send.at[index], small_recv.at[index], exchanges[index])
        else:
            for layer in (0, 1):
                @pl.when(core != layer)
                def unused():
                    vec[layer, 0:6, :] = jnp.zeros((6, 1024), F32)

            for half in (0, 1):
                @pl.when(core == half)
                def unused_too():
                    send(vec.at[1 - half], inbox.at[0], small_send.at[0], small_recv.at[0], exchanges[0])

    def small_take(index):
        await_bytes(inbox.at[index], small_recv.at[index])
        if index:
            acc[index] = acc[index - 1] + inbox[index]
        else:
            for half in (0, 1):
                @pl.when(core == half)
                def unused():
                    acc[0] = vec[half] + inbox[0]

    def swap_tile(index, pair, value):
        own_ref, other_ref = pair
        span = block_rows(pl.program_id(0))
        own_ref[span, :] = value
        send(own_ref.at[span], other_ref.at[span], swap_send.at[index], swap_recv.at[index], {SECTION: 1 - core})

    def swapped(index, pair):
        await_bytes(pair[0], swap_send.at[index])
        await_bytes(pair[1], swap_recv.at[index])

    def mid_row(layer, group):
        return mid_gain[layer, :, lanes(group * 1024 + core * 512, 512)]

    def add_vec(layer, row, value, span=slice(None)):
        vec[layer, row : row + 1, span] += value

    def weight_grad(left, left_spec, right, right_spec, target, target_spec):
        def body(left_ref, right_ref, out_ref):
            a = left_ref[...].reshape(left_ref.shape[-2:])
            b = right_ref[...].reshape(right_ref.shape[-2:])
            value = lax.dot_general(a, b, (((0,), (0,)), ((), ())), preferred_element_type=F32)
            out_ref[...] = value.astype(BF16).reshape(out_ref.shape)

        stage(body, [(left, left_spec), (right, right_spec)], [(target, target_spec)])

    def narrow_stage(layer, grad):
        own_half, make = saved[layer], made[layer]

        def body(c_ref, g_ref, own_ref, other_ref, w_ref, dm_ref):
            mean, scale = mid_stats(own_ref[...], other_ref[...])
            grad_low = c_ref[...]
            first = jnp.zeros((TILE, 1), F32)
            second = jnp.zeros((TILE, 1), F32)
            for group in range(4):
                d_middle = dot_nt(grad_low, w_ref[group])
                dm_ref[group] = d_middle.astype(BF16)
                unit_m = (g_ref[group].astype(F32) - mean) * scale
                product = d_middle * unit_m
                add_vec(layer, 6 + group, jnp.sum(product, axis=0, keepdims=True), column)
                add_vec(layer, 10 + group, jnp.sum(d_middle, axis=0, keepdims=True), column)
                row_gain = mid_row(layer, group)
                first = first + jnp.sum(d_middle * row_gain, axis=-1, keepdims=True)
                second = second + jnp.sum(product * row_gain, axis=-1, keepdims=True)
            swap_tile(layer * 3, sums[layer], two_columns(first, second))

        stage(
            body,
            [(grad, rows_spec(1024)), (own_half.gelu, group_spec(512)), (stats[layer][0], rows_spec(128)),
             (stats[layer][1], rows_spec(128)), (weights[layer][3], whole_spec((4, 512, 1024)))],
            [(make.d_middle, group_spec(512))],
        )

    def widen_stage(layer):
        own_half, make = saved[layer], made[layer]

        def body(dm_ref, g_ref, s_ref, own_ref, other_ref, a_ref, b_ref, w_ref, dh_ref):
            mean, scale = mid_stats(own_ref[...], other_ref[...])
            both = (a_ref[...] + b_ref[...]) * (1.0 / 4096)
            first, second = both[:, 0:1], both[:, 64:65]
            total = jnp.zeros((TILE, 1024), F32)
            for group in range(4):
                unit_m = (g_ref[group].astype(F32) - mean) * scale
                inner = dm_ref[group].astype(F32) * mid_row(layer, group)
                d_gelu = scale * (inner - first - unit_m * second)
                d_hidden = (d_gelu * s_ref[group].astype(F32)).astype(BF16)
                dh_ref[group] = d_hidden
                total = total + dot_nt(d_hidden, w_ref[group].reshape(1024, 512))
            swap_tile(layer * 3 + 1, swaps[0], total.astype(BF16))

        stage(
            body,
            [(make.d_middle, group_spec(512)), (own_half.gelu, group_spec(512)), (own_half.slope, group_spec(512)),
             (stats[layer][0], rows_spec(128)), (stats[layer][1], rows_spec(128)), (sums[layer][0], rows_spec(128)),
             (sums[layer][1], rows_spec(128)), (weights[layer][2], whole_spec((4, 4, 256, 512)))],
            [(make.d_hidden, group_spec(512))],
        )

    def norms_stage(layer, grad):
        own_half, make = saved[layer], made[layer]
        scale_row = jnp.concatenate(
            [head_row[layer, :, lanes(group * 256 + core * 128, 128)] for group in range(4)], axis=1
        )

        def body(c_ref, res_ref, da_ref, db_ref, ba_ref, bb_ref, ho_ref, w_ref, dr_ref, dbr_ref, dh_ref):
            unit_r, scale_r = standard(res_ref[...])
            d_ffn = da_ref[...].astype(F32) + db_ref[...].astype(F32)
            back, gain_third, shift_third = standard_back(unit_r, scale_r, gains[layer, 2:3, :], d_ffn)
            d_residual = c_ref[...].astype(F32) + back
            dr_ref[...] = d_residual
            unit_b, scale_b = standard(ba_ref[...].astype(F32) + bb_ref[...].astype(F32))
            back, gain_second, shift_second = standard_back(unit_b, scale_b, gains[layer, 1:2, :], d_residual)
            d_branch = back.astype(BF16)
            dbr_ref[...] = d_branch
            d_scaled = dot_nt(d_branch, w_ref[...].reshape(512, 1024))
            dh_ref[...] = (d_scaled * scale_row).astype(BF16)
            add_vec(layer, 14, jnp.sum(d_scaled * ho_ref[...].astype(F32), axis=0, keepdims=True), column)
            for row, value in ((1, gain_second), (2, gain_third), (4, shift_second), (5, shift_third)):
                add_vec(layer, row, value)

        stage(
            body,
            [(grad, rows_spec(1024)), (own_half.residual, rows_spec(1024)), (swaps[0][0], rows_spec(1024)),
             (swaps[0][1], rows_spec(1024)), (own_half.branch, rows_spec(1024)),
             (own_half.branch_other, rows_spec(1024)), (own_half.head_out, rows_spec(512)),
             (weights[layer][1], whole_spec((4, 128, 1024)))],
            [(make.d_residual, rows_spec(1024)), (make.d_branch, rows_spec(1024)), (make.d_heads, rows_spec(512))],
        )

    def attention_stage(layer):
        own_half, make = saved[layer], made[layer]

        def body(q_ref, k_ref, v_ref, grad_ref, out_ref, log_ref, back_ref):
            attend_back(
                q_ref, k_ref, v_ref, grad_ref, out_ref, log_ref, back_ref, split_ref[0], triangle, turned, walled, dk_acc, dv_acc
            )

        stage(
            body,
            [(own_half.proj, third_spec(0)), (own_half.proj, third_spec(1)), (own_half.proj, third_spec(2)),
             (make.d_heads, column_spec(128)), (own_half.head_out, column_spec(128)),
             (own_half.logs, pl.BlockSpec((1, 2, 1024), lambda group: (group, 0, 0)))],
            [(make.d_proj, block_spec(1024, 384))],
        )

    def project_stage(layer):
        make = made[layer]

        def body(d_ref, w_ref):
            total = dot_nt(d_ref[0], w_ref[0].reshape(1024, 384))
            for group in range(1, 4):
                total = total + dot_nt(d_ref[group], w_ref[group].reshape(1024, 384))
            swap_tile(layer * 3 + 2, swaps[1], total.astype(BF16))

        stage(
            body, [(make.d_proj, group_spec(384)), (weights[layer][0], whole_spec((4, 4, 256, 384)))], []
        )

    def entry_stage(layer):
        own_half, make = saved[layer], made[layer]

        def body(dr_ref, a_ref, b_ref, x_ref, dx_ref):
            unit_x, scale_x = standard(x_ref[...].astype(F32))
            d_normed = a_ref[...].astype(F32) + b_ref[...].astype(F32)
            back, gain_first, shift_first = standard_back(unit_x, scale_x, gains[layer, 0:1, :], d_normed)
            dx_ref[...] = (dr_ref[...] + back).astype(BF16)
            add_vec(layer, 0, gain_first)
            add_vec(layer, 3, shift_first)

        stage(
            body,
            [(make.d_residual, rows_spec(1024)), (swaps[1][0], rows_spec(1024)),
             (swaps[1][1], rows_spec(1024)), (own_half.entry, rows_spec(1024))],
            [(make.d_entry, rows_spec(1024))],
        )

    def layer_back(layer, grad, events):
        own_half, make = saved[layer], made[layer]
        base = 0 if layer == 1 else 4
        weight_grad(own_half.middle, block_spec(1024, 512), grad, whole_spec((1024, 1024)),
                    grads[layer][3], block_spec(512, 1024))
        events[0]()
        begin(base)
        if layer == 1:
            last_ready()
        narrow_stage(layer, grad)
        events[1]()
        swapped(layer * 3, sums[layer])
        widen_stage(layer)
        events[2]()
        weight_grad(own_half.ffn_input, whole_spec((1024, 1024)), make.d_hidden, block_spec(1024, 512),
                    grads[layer][2], grad_spec(512))
        begin(base + 1)
        swapped(layer * 3 + 1, swaps[0])
        norms_stage(layer, grad)
        events[3]()
        weight_grad(own_half.scaled, column_spec(128), make.d_branch, whole_spec((1024, 1024)),
                    grads[layer][1], block_spec(128, 1024))
        begin(base + 2)
        attention_stage(layer)
        events[4]()
        project_stage(layer)
        events[5]()
        weight_grad(own_half.normed, whole_spec((1024, 1024)), make.d_proj, block_spec(1024, 384),
                    grads[layer][0], grad_spec(384))
        begin(base + 3)
        swapped(layer * 3 + 2, swaps[1])
        entry_stage(layer)
        events[6]()

    def last_stage():
        def body(mid_ref, w_ref):
            total = dot(mid_ref[0], w_ref[0])
            for group in range(1, 4):
                total = total + dot(mid_ref[group], w_ref[group])
            swap_tile(6, swaps[2], total.astype(BF16))

        stage(body, [(saved[1].middle, group_spec(512)), (weights[1][3], whole_spec((4, 512, 1024)))], [])

    def output_stage():
        swapped(6, swaps[2])

        def body(res_ref, a_ref, b_ref, out_ref):
            out_ref[...] = (res_ref[...] + (a_ref[...].astype(F32) + b_ref[...].astype(F32))).astype(BF16)

        stage(
            body,
            [(saved[1].residual, rows_spec(1024)), (swaps[2][0], rows_spec(1024)), (swaps[2][1], rows_spec(1024))],
            [(output, rows_spec(1024))],
        )
        send_ends(1, output)

    def prepare():
        vec[...] = jnp.zeros_like(vec)

    layer_back(1, cotangent, (
        after((prepare,)),
        after(),
        after((second_hop, 0), (last_stage,)),
        after((deep_hop, 0), (output_stage,)),
        after((second_hop, 1), (finish, 0), (second_hop, 2)),
        after((deep_hop, 1), (forward, 0)),
        after((deep_hop, 2), (finish, 1), (corner, 0), (second_hop, 3)),
    ))
    layer_back(0, made[1].d_entry, (
        after((forward, 1), (finish, 2), (deep_hop, 3), (free_hops, 0)),
        after((corner, 1), (forward, 2)),
        after((second_hop, 4), (finish, 3), (free_hops, 1), (corner, 2)),
        after((deep_hop, 4), (forward, 3), (free_hops, 2)),
        after((second_hop, 5), (finish, 4), (corner, 3), (second_hop, 6)),
        after((deep_hop, 5), (forward, 4), (free_hops, 3)),
        after((deep_hop, 6),),
    ))
    send_ends(0, made[0].d_entry)
    small_step(0)
    second_hop(7)
    finish(5)
    finish(6)
    corner(4)
    small_take(0)
    small_step(1)
    deep_hop(7)
    forward(5)
    forward(6)
    small_take(1)
    small_step(2)
    finish(7)
    corner(5)
    corner(6)
    small_take(2)
    small_step(3)
    forward(7)
    small_take(3)
    small_step(4)
    corner(7)
    small_take(4)
    small_out[...] = acc[4]
    clean_up()
    for unit in range(8):
        clean(unit)
    for index in range(5):
        await_bytes(inbox.at[index], small_send.at[index])
    for step in range(4):
        await_bytes(ends.at[0], ends_send.at[step])
    for step in (1, 2, 3):
        await_bytes(ends.at[0], ends_recv.at[step])


def both_layers(split_at, items, weights, smalls):
    anywhere = pl.BlockSpec(memory_space=pl.ANY)
    local_space = pl.BlockSpec(memory_space=pltpu.VMEM)
    dma = pltpu.SemaphoreType.DMA
    rows, rows_wide = array((1024, 1024), BF16), array((1024, 1024), F32)
    weight_shapes = [
        array((4, 4, 256, 384), BF16),
        array((4, 128, 1024), BF16),
        array((4, 4, 256, 512), BF16),
        array((4, 512, 1024), BF16),
    ]
    wide, heads, proj = array((4, 1024, 512), BF16), array((1024, 512), BF16), array((4, 1024, 384), BF16)
    saved = [rows, rows, proj, heads, heads, array((4, 2, 1024), F32), rows, rows, rows_wide, rows, wide, wide, wide]
    made = [wide, wide, rows_wide, rows, heads, proj, rows]
    small_shapes = [(2,) + operand.shape for operand in smalls]
    shapes = [
        array((256, 3072), BF16),
        array((256, 1024), BF16),
        array((256, 4096), BF16),
        array((1024, 1024), BF16),
        array((4, 256, 1024), BF16),
        array((16, 1024), F32),
        rows,
        rows,
        *weight_shapes * 2,
        *saved * 2,
        *weight_shapes * 2,
        *made * 2,
    ]
    return pl.pallas_call(
        whole_kernel,
        in_specs=[pl.BlockSpec(memory_space=pltpu.SMEM)] + [anywhere] * 10,
        out_specs=[anywhere] * 5 + [local_space] + [anywhere] * (len(shapes) - 6),
        out_shape=shapes,
        scratch_shapes=[pltpu.VMEM(shape, F32) for shape in small_shapes]
        + [pltpu.VMEM((256, 256), F32), pltpu.VMEM((128, 1024), BF16), pltpu.VMEM((2, 1024, 128), BF16)]
        + [pltpu.VMEM((1024, 1024), BF16)] * 6
        + [pltpu.VMEM((1024, 128), F32)] * 8
        + [pltpu.VMEM((4, 2) + size, BF16) for size in SIZES]
        + [pltpu.VMEM((4, 2) + size, BF16) for size in SIZES]
        + [pltpu.VMEM((4,) + size, BF16) for size in SIZES]
        + [pltpu.VMEM((2, 3) + size, BF16) for size in SIZES]
        + [pltpu.VMEM((2, 16, 1024), F32), pltpu.VMEM((5, 16, 1024), F32), pltpu.VMEM((5, 16, 1024), F32)]
        + [pltpu.VMEM((1024, 128), F32), pltpu.VMEM((1024, 128), F32)]
        + [
            dma((2, 4)), dma((2, 4)), dma((2, 4)), dma((8, 2)), dma((8,)),
            dma((8,)), dma((8, 4)), dma((8,)), dma((8, 3, 3)), dma((3, 5)),
            dma((5,)), dma((5,)), dma((4,)),
        ]
        + [dma((8,))] * 7
        + [dma((8, 3)), dma((8,)), dma((8, 2, 4)), dma((4,)), dma((4,)), dma((5,)), dma((5,)), dma((7,)), dma((7,))]
        + [pltpu.SemaphoreType.REGULAR((4,))],
        compiler_params=pltpu.CompilerParams(
            collective_id=0, has_side_effects=True, vmem_limit_bytes=62 * 2**20
        ),
    )(split_at, items, *weights, *smalls)[:6]


def local(
    boundary,
    first_len,
    qkv_weight,
    out_weight,
    up_weight,
    down_weight,
    norm_gain,
    norm_shift,
    mid_gain,
    mid_shift,
    head_scale,
):
    split_at = pick(first_len, lax.axis_index("dp"))
    *shares, ends, totals = both_layers(
        split_at,
        boundary[0, :, 0],
        (qkv_weight[0], out_weight[0], up_weight[0], down_weight[0]),
        (norm_gain[0], norm_shift[0], mid_gain, mid_shift, jnp.repeat(head_scale, 64, axis=1)),
    )
    head_sums = jnp.sum(totals[14].reshape(2, 4, 2, 64), axis=3).transpose(1, 0, 2).reshape(1, 16)
    return (
        ends[None, :, None],
        *[share.astype(F32)[None] for share in shares],
        totals[0:3][None],
        totals[3:6][None],
        totals[6:10].reshape(1, 4096),
        totals[10:14].reshape(1, 4096),
        head_sums,
    )


def fits(mesh, boundary, mid_gain, head_scale):
    sizes = (mesh.shape["section"], mesh.shape["dp"], mesh.shape["shard"])
    return (
        sizes == (2, 4, 4)
        and boundary == (2, 4, 4, 1024, 1024)
        and mid_gain == (2, 4096)
        and head_scale == (2, 16)
    )


def solution(mesh):
    placed = (
        P("section", None, "shard", "dp", None),
        P(None, "shard"),
        P("section", "shard", None),
        P("section", "shard", None),
        P("section", "shard", None),
        P("section", "shard", None),
        P("section", None, None),
        P("section", None, None),
        P("section", None),
        P("section", None),
        P("section", None),
    )
    results = (
        P("section", None, "shard", "dp", None),
        P("section", "shard", None),
        P("section", "shard", None),
        P("section", "shard", None),
        P("section", "shard", None),
        P("section", None, None),
        P("section", None, None),
        P("section", None),
        P("section", None),
        P("section", None),
    )

    def whole(*arrays):
        fast = fits(mesh, arrays[0].shape, arrays[8].shape, arrays[10].shape)
        body = local if fast else general
        return jax.shard_map(
            body, mesh=mesh, in_specs=placed, out_specs=results, check_vma=False
        )(*arrays)

    return whole
```

```python
import functools
import math
from typing import NamedTuple

import jax
import jax.numpy as jnp
from jax import lax
from jax.experimental import pallas as pl
from jax.experimental.pallas import tpu as pltpu
from jax.sharding import PartitionSpec as P

EPSILON = 1e-05


def shifted(value, axis, steps):
    count = lax.axis_size(axis)
    first, last = (max(0, -steps), min(count, count - steps))
    return lax.ppermute(value, axis, [(source, source + steps) for source in range(first, last)])


def normalize(values_in, gain, shift):
    centre = values_in - jnp.mean(values_in, axis=-1, keepdims=True)
    spread = jnp.mean(centre * centre, axis=-1, keepdims=True)
    return centre * lax.rsqrt(spread + EPSILON) * gain + shift


def middle_norm(hidden, mid_gain, mid_shift):
    return normalize(jax.nn.gelu(hidden, approximate=False), mid_gain, mid_shift)


def contract_rows(left, right):
    return lax.dot_general(
        left, right, (((0,), (0,)), ((), ())), preferred_element_type=jnp.float32
    )


def contract_cols(left, right):
    return lax.dot_general(
        left, right, (((1,), (1,)), ((), ())), preferred_element_type=jnp.float32
    )


def visible(query_place, key_place, split_at):
    same_doc = (query_place[:, None] < split_at) == (key_place[None, :] < split_at)
    return same_doc & (key_place[None, :] <= query_place[:, None])


def forward_parts(stream_in, weights, small, split_at, head_count):
    weight_qkv, weight_out, weight_up, weight_down = weights
    gains, shifts, mid_gain, mid_shift, head_scale = small
    row_count, model_width = stream_in.shape
    head_dim = model_width // head_count
    factor = 1.0 / math.sqrt(head_dim)
    normed = normalize(stream_in, gains[0], shifts[0]).astype(jnp.bfloat16)
    projected = jnp.dot(normed, weight_qkv, preferred_element_type=jnp.float32).astype(jnp.bfloat16)
    queries = projected[:, :model_width].reshape(row_count, head_count, head_dim)
    key_rows = projected[:, model_width : 2 * model_width].reshape(row_count, head_count, head_dim)
    value_rows = projected[:, 2 * model_width :].reshape(row_count, head_count, head_dim)
    keys_all, values_all = (
        lax.all_gather(key_rows, "dp", axis=0, tiled=True),
        lax.all_gather(value_rows, "dp", axis=0, tiled=True),
    )
    seq_len = keys_all.shape[0]
    own_place = lax.axis_index("dp") * row_count + jnp.arange(row_count, dtype=jnp.int32)
    all_place = jnp.arange(seq_len, dtype=jnp.int32)
    allowed = visible(own_place, all_place, split_at)
    scores = (
        jnp.einsum("qhd,khd->hqk", queries, keys_all, preferred_element_type=jnp.float32) * factor
    )
    scores = jnp.where(allowed[None], scores, -1e30)
    row_max = jnp.max(scores, axis=-1, keepdims=True)
    log_total = row_max + jnp.log(jnp.sum(jnp.exp(scores - row_max), axis=-1, keepdims=True))
    attend = jnp.exp(scores - log_total)
    attend_low = attend.astype(jnp.bfloat16)
    head_out = jnp.einsum(
        "hqk,khd->qhd", attend_low, values_all, preferred_element_type=jnp.float32
    )
    scaled = (
        (head_out * head_scale[None, :, None]).astype(jnp.bfloat16).reshape(row_count, model_width)
    )
    branch = jnp.dot(scaled, weight_out, preferred_element_type=jnp.float32)
    residual = stream_in + normalize(branch, gains[1], shifts[1])
    ffn_input = normalize(residual, gains[2], shifts[2]).astype(jnp.bfloat16)
    hidden = jnp.dot(ffn_input, weight_up, preferred_element_type=jnp.float32)
    middle = middle_norm(hidden, mid_gain, mid_shift).astype(jnp.bfloat16)
    return dict(
        normed=normed,
        queries=queries,
        key_rows=key_rows,
        value_rows=value_rows,
        keys_all=keys_all,
        values_all=values_all,
        own_place=own_place,
        all_place=all_place,
        attend=attend,
        attend_low=attend_low,
        log_total=log_total,
        head_out=head_out,
        scaled=scaled,
        branch=branch,
        residual=residual,
        ffn_input=ffn_input,
        hidden=hidden,
        middle=middle,
        factor=factor,
    )


def backward_parts(stream_in, grad_in, weights, small, split_at, head_count):
    weight_qkv, weight_out, weight_up, weight_down = weights
    gains, shifts, mid_gain, mid_shift, head_scale = small
    parts = forward_parts(stream_in, weights, small, split_at, head_count)
    row_count, model_width = stream_in.shape
    head_dim = model_width // head_count
    factor = parts["factor"]
    grad_down = contract_rows(parts["middle"], grad_in)
    d_middle = contract_cols(grad_in, weight_down)
    unused, pull_middle = jax.vjp(middle_norm, parts["hidden"], mid_gain, mid_shift)
    d_hidden, grad_mid_gain, grad_mid_shift = pull_middle(d_middle)
    d_hidden = d_hidden.astype(jnp.bfloat16)
    grad_up = contract_rows(parts["ffn_input"], d_hidden)
    d_ffn_input = contract_cols(d_hidden, weight_up)
    unused, pull_third = jax.vjp(normalize, parts["residual"], gains[2], shifts[2])
    d_residual, gain_third, shift_third = pull_third(d_ffn_input)
    d_residual = d_residual + grad_in.astype(jnp.float32)
    unused, pull_second = jax.vjp(normalize, parts["branch"], gains[1], shifts[1])
    d_branch, gain_second, shift_second = pull_second(d_residual)
    d_branch = d_branch.astype(jnp.bfloat16)
    grad_out = contract_rows(parts["scaled"], d_branch)
    d_scaled = contract_cols(d_branch, weight_out).reshape(row_count, head_count, head_dim)
    grad_head_scale = jnp.sum(d_scaled * parts["head_out"], axis=(0, 2))
    d_heads = (d_scaled * head_scale[None, :, None]).astype(jnp.bfloat16)
    attend = parts["attend"]
    d_attend = jnp.einsum(
        "qhd,khd->hqk", d_heads, parts["values_all"], preferred_element_type=jnp.float32
    )
    row_dot = jnp.sum(attend * d_attend, axis=-1, keepdims=True)
    d_scores = (attend * (d_attend - row_dot)).astype(jnp.bfloat16)
    d_query = (
        jnp.einsum("hqk,khd->qhd", d_scores, parts["keys_all"], preferred_element_type=jnp.float32)
        * factor
    ).astype(jnp.bfloat16)
    full_keys = (
        jnp.einsum("hqk,qhd->khd", d_scores, parts["queries"], preferred_element_type=jnp.float32)
        * factor
    )
    full_values = jnp.einsum(
        "hqk,qhd->khd", parts["attend_low"], d_heads, preferred_element_type=jnp.float32
    )
    d_keys, d_values = (
        lax.psum_scatter(full_keys, "dp", scatter_dimension=0, tiled=True),
        lax.psum_scatter(full_values, "dp", scatter_dimension=0, tiled=True),
    )
    d_projected = jnp.concatenate(
        [
            d_query.reshape(row_count, model_width),
            d_keys.astype(jnp.bfloat16).reshape(row_count, model_width),
            d_values.astype(jnp.bfloat16).reshape(row_count, model_width),
        ],
        axis=1,
    )
    grad_qkv = contract_rows(parts["normed"], d_projected)
    d_normed = contract_cols(d_projected, weight_qkv)
    unused, pull_first = jax.vjp(normalize, stream_in, gains[0], shifts[0])
    d_entry, gain_first, shift_first = pull_first(d_normed)
    d_entry = d_entry + d_residual
    big_grads = (grad_qkv, grad_out, grad_up, grad_down)
    small_grads = (
        jnp.stack([gain_first, gain_second, gain_third]),
        jnp.stack([shift_first, shift_second, shift_third]),
        grad_mid_gain,
        grad_mid_shift,
        grad_head_scale,
    )
    return (d_entry, big_grads, small_grads)


def add_up(first_term, second_term):
    return first_term + second_term


def general(
    boundary,
    first_len,
    qkv_weight,
    out_weight,
    up_weight,
    down_weight,
    norm_gain,
    norm_shift,
    mid_gain,
    mid_shift,
    head_scale,
):
    section_index = lax.axis_index("section")
    gathered = (
        lax.all_gather(qkv_weight, "shard", axis=1, tiled=True),
        lax.all_gather(out_weight, "shard", axis=1, tiled=True),
        lax.all_gather(up_weight, "shard", axis=1, tiled=True),
        lax.all_gather(down_weight, "shard", axis=1, tiled=True),
    )
    weights = tuple((piece[0] for piece in gathered))
    small = (norm_gain[0], norm_shift[0], mid_gain[0], mid_shift[0], head_scale[0])
    head_count = head_scale.shape[1]
    micro = boundary.shape[1]
    row_count = boundary.shape[3]
    model_width = boundary.shape[4]
    local_ends = boundary[0, :, 0]
    splits = first_len[:, 0]

    def forward_tick(step_index, carry):
        incoming, kept, ends = carry
        index = step_index - section_index
        active = (index >= 0) & (index < micro)
        slot = jnp.clip(index, 0, micro - 1)
        entry = jnp.where(section_index == 0, local_ends[slot], incoming)
        parts = forward_parts(entry.astype(jnp.float32), weights, small, splits[slot], head_count)
        result = (
            parts["residual"]
            + jnp.dot(parts["middle"], weights[3], preferred_element_type=jnp.float32)
        ).astype(jnp.bfloat16)
        kept = kept.at[slot].set(jnp.where(active, entry, kept[slot]))
        ends = ends.at[slot].set(jnp.where(active, result, ends[slot]))
        incoming = shifted(result, "section", 1)
        return (incoming, kept, ends)

    blank = jnp.zeros((row_count, model_width), jnp.bfloat16)
    stack_blank = jnp.zeros((micro, row_count, model_width), jnp.bfloat16)
    unused, kept, ends = lax.fori_loop(
        0, micro + 1, forward_tick, (blank, stack_blank, stack_blank)
    )

    def backward_tick(step_index, carry):
        incoming, ends, big_sums, small_sums = carry
        index = micro - step_index - section_index
        active = (index >= 0) & (index < micro)
        slot = jnp.clip(index, 0, micro - 1)
        grad_in = jnp.where(section_index == 1, local_ends[slot], incoming)
        grad_in = jnp.where(active, grad_in, jnp.zeros_like(grad_in))
        d_entry, big_grads, small_grads = backward_parts(
            kept[slot].astype(jnp.float32), grad_in, weights, small, splits[slot], head_count
        )
        d_low = d_entry.astype(jnp.bfloat16)
        ends = ends.at[slot].set(jnp.where(active & (section_index == 0), d_low, ends[slot]))
        big_sums = jax.tree.map(add_up, big_sums, big_grads)
        small_sums = jax.tree.map(add_up, small_sums, small_grads)
        incoming = shifted(d_low, "section", -1)
        return (incoming, ends, big_sums, small_sums)

    big_zero = tuple((jnp.zeros(item.shape, jnp.float32) for item in weights))
    small_zero = tuple((jnp.zeros(item.shape, jnp.float32) for item in small))
    unused, ends, big_sums, small_sums = lax.fori_loop(
        0, micro + 1, backward_tick, (blank, ends, big_zero, small_zero)
    )
    shares = (
        lax.psum_scatter(big_sums[0][None], "shard", scatter_dimension=1, tiled=True),
        lax.psum_scatter(big_sums[1][None], "shard", scatter_dimension=1, tiled=True),
        lax.psum_scatter(big_sums[2][None], "shard", scatter_dimension=1, tiled=True),
        lax.psum_scatter(big_sums[3][None], "shard", scatter_dimension=1, tiled=True),
    )
    shares = lax.psum((shares[0], shares[1], shares[2], shares[3]), "dp")
    totals = lax.psum(
        (small_sums[0], small_sums[1], small_sums[2], small_sums[3], small_sums[4]), ("dp", "shard")
    )
    return (
        ends[None, :, None],
        shares[0],
        shares[1],
        shares[2],
        shares[3],
        totals[0][None],
        totals[1][None],
        totals[2][None],
        totals[3][None],
        totals[4][None],
    )


BF16 = jnp.bfloat16
F32 = jnp.float32
TILE = 256
SECTION, DP, SHARD = "section", "dp", "shard"


def rows_spec(columns):
    return pl.BlockSpec((TILE, columns), lambda step: (step, 0))


def group_spec(columns):
    return pl.BlockSpec((4, TILE, columns), lambda step: (0, step, 0))


def array(shape, dtype):
    return jax.ShapeDtypeStruct(shape, dtype)


def dot(left, right):
    return jnp.dot(left, right, preferred_element_type=F32)


def dot_nt(left, right):
    return lax.dot_general(left, right, (((1,), (1,)), ((), ())), preferred_element_type=F32)


def standard(values_in):
    centre = values_in - jnp.mean(values_in, axis=-1, keepdims=True)
    spread_of = jnp.mean(centre * centre, axis=-1, keepdims=True)
    scale = lax.rsqrt(spread_of + EPSILON)
    return centre * scale, scale


def standard_back(unit_values, scale, gain, grad):
    inner = grad * gain
    first = jnp.mean(inner, axis=-1, keepdims=True)
    second = jnp.mean(inner * unit_values, axis=-1, keepdims=True)
    back = scale * (inner - first - unit_values * second)
    return back, jnp.sum(grad * unit_values, axis=0, keepdims=True), jnp.sum(grad, axis=0, keepdims=True)


def lane_masks(rows):
    lanes = lax.broadcasted_iota(jnp.int32, (rows, 128), 1)
    return lanes < 64


def two_columns(first, second):
    return jnp.where(lane_masks(first.shape[0]), first, second)


def mid_stats(own, other):
    mean_own, mean_other = own[:, 0:1], other[:, 0:1]
    gap = mean_own - mean_other
    spread_of = 0.5 * (own[:, 64:65] + other[:, 64:65]) + 0.25 * gap * gap
    return 0.5 * (mean_own + mean_other), lax.rsqrt(spread_of + EPSILON)


def fill_triangle(triangle_ref):
    keys = lax.broadcasted_iota(jnp.int32, (256, 256), 0)
    queries = lax.broadcasted_iota(jnp.int32, (256, 256), 1)
    triangle_ref[...] = jnp.where(keys <= queries, 0.0, -1e30)


def own_lanes(rows, half):
    lane = lax.broadcasted_iota(jnp.int32, (rows, 128), 1)
    return (lane < 64 if half == 0 else lane >= 64), lane == 64 * (1 - half)


def walled_keys(keys, split_at, half):
    mine, spare = own_lanes(1024, half)
    row = lax.broadcasted_iota(jnp.int32, (1024, 128), 0)
    return jnp.where(mine, keys, jnp.where(spare & (row < split_at), -1e30, 0.0).astype(BF16))


def walled_queries(queries, split_at, half, start):
    mine, spare = own_lanes(256, half)
    row = lax.broadcasted_iota(jnp.int32, (256, 128), 0) + start
    return jnp.where(mine, queries, jnp.where(spare & (row >= split_at), 1.0, 0.0).astype(BF16))


def score_parts(keys_ref, queries, block, triangle_ref):
    parts = []
    for part in range(2 * (block + 1)):
        scores = dot_nt(keys_ref[part * 128 : part * 128 + 128, :], queries)
        if part >= 2 * block:
            scores = scores + triangle_ref[(part - 2 * block) * 128 : (part - 2 * block) * 128 + 128, :]
        parts.append(scores)
    return parts


def run_lagged(first, second):
    tasks = [(block, half) for block in (3, 2, 1, 0) for half in (0, 1)]
    before = None
    for task in tasks:
        held = first(*task)
        if before is not None:
            second(*before)
        before = (*task, held)
    second(*before)


def attend(q_ref, k_ref, v_ref, scale_row, out_ref, scaled_ref, log_ref, split_at, triangle_ref, turned_ref, keys_ref):
    turned_ref[...] = v_ref[0].astype(F32).T.astype(BF16)
    for half in range(2):
        keys_ref[half] = walled_keys(k_ref[0], split_at, half)
    found = {}

    def score(block, half):
        queries = (q_ref[0, pl.ds(block * 256, 256), :] * 0.125).astype(BF16)
        parts = score_parts(keys_ref.at[half], walled_queries(queries, split_at, half, block * 256), block, triangle_ref)
        tops = functools.reduce(jnp.maximum, [jnp.max(part.reshape(16, 8, 256), axis=0) for part in parts])
        return parts, jnp.max(tops, axis=0, keepdims=True)

    def mix(block, half, held):
        parts, top = held
        span = pl.ds(block * 256, 256)
        powers = [jnp.exp(part - top) for part in parts]
        total = functools.reduce(jnp.add, [jnp.sum(power.reshape(16, 8, 256), axis=0) for power in powers])
        total = jnp.sum(total, axis=0, keepdims=True)
        low = jnp.concatenate([power.astype(BF16) for power in powers], axis=0)
        mixed = dot(turned_ref[half * 64 : half * 64 + 64, : (block + 1) * 256], low)
        log_ref[0, half : half + 1, span] = top + jnp.log(total)
        found[half] = mixed * (1.0 / total)
        if half == 1:
            head_out = jnp.concatenate([found[0], found[1]], axis=0).T
            out_ref[span, :] = head_out.astype(BF16)
            scaled_ref[span, :] = (head_out * scale_row).astype(BF16)

    run_lagged(score, mix)


def attend_back(
    q_ref, k_ref, v_ref, grad_ref, out_ref, log_ref, back_ref, split_at, triangle_ref, turned_ref, keys_ref, dk_ref, dv_ref
):
    turned_ref[...] = k_ref[0].astype(F32).T.astype(BF16)
    for half in range(2):
        keys_ref[half] = walled_keys(k_ref[0], split_at, half)
    products, found = {}, {}

    def score(block, half):
        span = pl.ds(block * 256, 256)
        mine, unused = own_lanes(256, half)
        queries = (q_ref[0, span, :] * 0.125).astype(BF16)
        grad = grad_ref[span, :]
        own_grad = jnp.where(mine, grad, 0.0).astype(BF16)
        if half == 0:
            products[block] = (grad.astype(F32) * out_ref[span, :].astype(F32)).T
        row_dot = jnp.sum(products[block][half * 64 : half * 64 + 64, :], axis=0, keepdims=True)
        parts = score_parts(keys_ref.at[half], walled_queries(queries, split_at, half, block * 256), block, triangle_ref)
        lows, grads = [], []
        for part, scores in enumerate(parts):
            attend_part = jnp.exp(scores - log_ref[0, half : half + 1, span])
            d_attend = dot_nt(v_ref[0, part * 128 : part * 128 + 128, :], own_grad)
            lows.append(attend_part.astype(BF16))
            grads.append((attend_part * (d_attend - row_dot)).astype(BF16))
        own_queries = jnp.where(mine, queries, 0.0).astype(BF16)
        return jnp.concatenate(lows, axis=0), jnp.concatenate(grads, axis=0), own_queries, own_grad

    def mix(block, half, held):
        low, d_scores, own_queries, own_grad = held
        seen = pl.ds(0, (block + 1) * 256)
        found[half] = dot(turned_ref[half * 64 : half * 64 + 64, : (block + 1) * 256], d_scores)
        if (block, half) == (3, 0):
            dv_ref[...] = dot(low, own_grad)
            dk_ref[...] = dot(d_scores, own_queries)
        else:
            dv_ref[seen, :] += dot(low, own_grad)
            dk_ref[seen, :] += dot(d_scores, own_queries)
        if half == 1:
            d_query = jnp.concatenate([found[0], found[1]], axis=0).T * 0.125
            back_ref[0, pl.ds(block * 256, 256), 0:128] = d_query.astype(BF16)

    run_lagged(score, mix)
    back_ref[0, :, 128:256] = dk_ref[...].astype(BF16)
    back_ref[0, :, 256:384] = dv_ref[...].astype(BF16)


MESH = pl.DeviceIdType.MESH
SIZES = ((256, 384), (128, 256), (256, 512), (512, 256))


def partner(place, step):
    return {0: place, 1: place + 1 - 2 * lax.rem(place, 2), 2: lax.rem(place + 2, 4), 3: 3 - place}[step]


def here():
    return lax.axis_index("section"), lax.axis_index("dp"), lax.axis_index("shard")


def greet(core, place, depth):
    barrier = pltpu.get_barrier_semaphore()
    targets = [{SHARD: lax.rem(depth + step, 4)} for step in (1, 2, 3)]
    targets += [{SECTION: 1 - core, SHARD: lax.rem(depth + step, 4)} for step in range(4)]
    targets += [{DP: partner(place, step)} for step in (1, 2, 3)]
    for target in targets:
        pl.semaphore_signal(barrier, inc=1, device_id=target, device_id_type=MESH)
    pl.semaphore_wait(barrier, len(targets))


def send(source, target, send_sem, recv_sem, device):
    copy = pltpu.make_async_remote_copy(
        src_ref=source, dst_ref=target, send_sem=send_sem, recv_sem=recv_sem,
        device_id=device, device_id_type=MESH,
    )
    copy.start()


def await_bytes(view, sem):
    pltpu.make_async_copy(view, view, sem).wait()


def lanes(start, size):
    return pl.ds(pl.multiple_of(start, 128), size)


def raw_views(raw, matrix, half, quarter):
    if matrix == 0:
        return [raw[0].at[:, lanes(third * 1024 + quarter * 256 + half * 128, 128)] for third in range(3)]
    if matrix == 1:
        return [raw[1].at[pl.ds(half * 128, 128), lanes(quarter * 256, 256)]]
    if matrix == 2:
        return [raw[2].at[:, lanes(quarter * 1024 + half * 512, 512)]]
    return [raw[3].at[pl.ds(half * 512, 512), lanes(quarter * 256, 256)]]


def whole_view(whole, matrix, quarter, shard):
    if matrix in (0, 2):
        return whole[matrix].at[quarter, shard]
    return whole[matrix].at[shard, :, lanes(quarter * 256, 256)]


def whole_views(whole, matrix, quarter, shard):
    if matrix == 0:
        return [whole[0].at[quarter, shard, :, pl.ds(third * 128, 128)] for third in range(3)]
    return [whole_view(whole, matrix, quarter, shard)]


def pieces_view(whole, matrix, first, second):
    if matrix in (0, 2):
        return whole[matrix].at[pl.ds(0, first), pl.ds(0, second)]
    return whole[matrix].at[pl.ds(0, first), :, pl.ds(0, 256 * second)]


class Saved(NamedTuple):
    entry: object
    normed: object
    proj: object
    head_out: object
    scaled: object
    logs: object
    branch: object
    branch_other: object
    residual: object
    ffn_input: object
    gelu: object
    slope: object
    middle: object


def whole_spec(shape):
    return pl.BlockSpec(shape, lambda step: (0,) * len(shape), pipeline_mode=pl.Buffered(1))


def block_spec(rows, columns):
    return pl.BlockSpec((1, rows, columns), lambda step: (step, 0, 0))


def grad_spec(columns):
    return pl.BlockSpec((1, 4, 256, columns), lambda step: (step, 0, 0, 0))


def column_spec(columns):
    return pl.BlockSpec((1024, columns), lambda step: (0, step))


def third_spec(third):
    return pl.BlockSpec((1, 1024, 128), lambda group: (group, 0, third))


def stage(body, ins, outs, hooks=()):
    def hooked(*refs):
        body(*refs)
        for step, action in hooks:
            pl.when(pl.program_id(0) == step)(action)

    pltpu.emit_pipeline(
        hooked, grid=(4,), in_specs=[spec for unused, spec in ins], out_specs=[spec for unused, spec in outs]
    )(*[ref for ref, unused in ins], *[ref for ref, unused in outs])


def after(*actions):
    def run():
        for action, *arguments in actions:
            action(*arguments)

    return run


def block_rows(index):
    return pl.ds(pl.multiple_of(index * 256, 256), 256)


def forward_part(items, raw, small_in, cotangent, wholes, saved, smalls, split_ref, attention_refs, swaps, stats, sems):
    gains, shifts, mid_gain, mid_shift, head_row = smalls
    triangle, turned, walled = attention_refs
    (item_send, item_recv, item_pass, own_send, own_recv, deep_send, deep_recv, hop_send, hop_recv, small_sems,
     swap_send, swap_recv, keep_sem) = sems
    core, place, depth = here()
    arrays = (saved[0].entry, cotangent)
    greet(core, place, depth)

    def items_out(layer):
        @pl.when(core == layer)
        def unused():
            for step in (1, 2, 3):
                send(items.at[partner(place, step)], arrays[layer].at[block_rows(place)], item_send.at[layer, step],
                     item_recv.at[layer, step], {DP: partner(place, step)})
            pltpu.make_async_copy(items.at[place], arrays[layer].at[block_rows(place)], item_send.at[layer, 0]).start()
            send(items.at[place], arrays[layer].at[block_rows(place)], item_pass.at[layer, 0], item_recv.at[layer, 0],
                 {SECTION: 1 - layer})

    def smalls_out():
        for layer in (0, 1):
            @pl.when(core == layer)
            def unused():
                for index, (source, target) in enumerate(zip(small_in, smalls)):
                    pltpu.make_async_copy(source, target.at[layer], small_sems.at[0, index]).start()
                    send(source, target.at[layer], small_sems.at[1, index], small_sems.at[2, index],
                         {SECTION: 1 - layer})

    units = [(layer, matrix) for layer in (0, 1) for matrix in range(4)]

    def deep(unit):
        layer, matrix = units[unit]

        @pl.when(core == layer)
        def unused():
            for step in (1, 2, 3):
                for half in (0, 1):
                    for source, target in zip(
                        raw_views(raw, matrix, half, place), whole_views(wholes[layer], matrix, place, depth)
                    ):
                        send(source, target, deep_send.at[unit], deep_recv.at[unit, step],
                             {SECTION: half, SHARD: lax.rem(depth + 4 - step, 4)})

    def own(unit):
        layer, matrix = units[unit]

        @pl.when(core == layer)
        def unused():
            for quarter in range(4):
                for source, target in zip(
                    raw_views(raw, matrix, layer, quarter), whole_views(wholes[layer], matrix, quarter, depth)
                ):
                    pltpu.make_async_copy(source, target, own_send.at[unit, 0]).start()
                for source, target in zip(
                    raw_views(raw, matrix, 1 - layer, quarter), whole_views(wholes[layer], matrix, quarter, depth)
                ):
                    send(source, target, own_send.at[unit, 1], own_recv.at[unit], {SECTION: 1 - layer})

    def route(unit, step):
        return (1, 2) if (unit + step) % 2 == 0 else (2, 1)

    def piece(unit, offset, step):
        layer, matrix = units[unit]
        return whole_view(wholes[layer], matrix, partner(place, offset), lax.rem(depth + step, 4))

    def first_hop(unit):
        for step in (1, 2, 3):
            first, second = route(unit, step)
            await_bytes(piece(unit, 0, step), deep_recv.at[unit, step])
            for offset in (first, second):
                send(piece(unit, 0, step), piece(unit, 0, step), hop_send.at[unit], hop_recv.at[unit, step - 1, offset - 1],
                     {DP: partner(place, offset)})

    def second_hop(unit):
        for step in (1, 2, 3):
            first, second = route(unit, step)
            await_bytes(piece(unit, first, step), hop_recv.at[unit, step - 1, first - 1])
            send(piece(unit, first, step), piece(unit, first, step), hop_send.at[unit], hop_recv.at[unit, step - 1, 2],
                 {DP: partner(place, second)})

    def ready(unit):
        layer, matrix = units[unit]
        quarters = pieces_view(wholes[layer], matrix, 2, 2)

        @pl.when(core == layer)
        def unused():
            await_bytes(quarters, own_send.at[unit, 0])

        @pl.when(core != layer)
        def unused_too():
            await_bytes(quarters, own_recv.at[unit])

        for step in (1, 2, 3):
            first, second = route(unit, step)
            await_bytes(piece(unit, 0, 0), hop_recv.at[unit, step - 1, second - 1])
            await_bytes(piece(unit, 0, 0), hop_recv.at[unit, step - 1, 2])

    def pass_on(layer):
        @pl.when(core == layer)
        def unused():
            for step in (1, 2, 3):
                block = arrays[layer].at[block_rows(partner(place, step))]
                await_bytes(block, item_recv.at[layer, step])
                send(block, block, item_pass.at[layer, step], item_recv.at[layer, step], {SECTION: 1 - layer})

    def passed(layer):
        @pl.when(core == layer)
        def unused():
            await_bytes(items.at[0], item_send.at[layer, 0])

        @pl.when(core != layer)
        def unused_too():
            for step in range(4):
                await_bytes(items.at[0], item_recv.at[layer, step])

    def take_smalls():
        for index, (source, target) in enumerate(zip(small_in, smalls)):
            for layer in (0, 1):
                @pl.when(core == layer)
                def unused():
                    await_bytes(source, small_sems.at[0, index])

                @pl.when(core != layer)
                def unused_too():
                    await_bytes(source, small_sems.at[2, index])

    def keep(index, source, target):
        pltpu.make_async_copy(source, target, keep_sem.at[index]).start()

    def kept(index, source):
        await_bytes(source, keep_sem.at[index])

    def swap_tile(index, pair, value):
        own_ref, other_ref = pair
        span = block_rows(pl.program_id(0))
        own_ref[span, :] = value
        send(own_ref.at[span], other_ref.at[span], swap_send.at[index], swap_recv.at[index], {SECTION: 1 - core})

    def swapped(index, pair):
        await_bytes(pair[0], swap_send.at[index])
        await_bytes(pair[1], swap_recv.at[index])

    def mid_row(ref, layer, group):
        return ref[layer, :, lanes(group * 1024 + core * 512, 512)]

    def project_rows(layer, x, normed_ref, proj_ref, w_ref):
        unit_x, unused = standard(x)
        normed = (unit_x * gains[layer, 0:1, :] + shifts[layer, 0:1, :]).astype(BF16)
        normed_ref[...] = normed
        for group in range(4):
            proj_ref[group] = dot(normed, w_ref[group].reshape(1024, 384)).astype(BF16)

    def project_stage(layer, hooks):
        own_half = saved[layer]
        weight = (wholes[layer][0], whole_spec((4, 4, 256, 384)))
        made = [(own_half.normed, rows_spec(1024)), (own_half.proj, group_spec(384))]

        def body_first(x_ref, w_ref, normed_ref, proj_ref):
            project_rows(layer, x_ref[...].astype(F32), normed_ref, proj_ref, w_ref)

        def body_next(res_ref, a_ref, b_ref, w_ref, normed_ref, proj_ref, entry_ref):
            entry = (res_ref[...] + (a_ref[...].astype(F32) + b_ref[...].astype(F32))).astype(BF16)
            entry_ref[...] = entry
            project_rows(layer, entry.astype(F32), normed_ref, proj_ref, w_ref)

        if layer == 0:
            stage(body_first, [(own_half.entry, rows_spec(1024)), weight], made, hooks)
        else:
            stage(
                body_next,
                [(saved[0].residual, rows_spec(1024)), (swaps[1][0], rows_spec(1024)), (swaps[1][1], rows_spec(1024)), weight],
                [*made, (own_half.entry, rows_spec(1024))],
                hooks,
            )

    def attention_stage(layer, hooks):
        own_half = saved[layer]

        def body(q_ref, k_ref, v_ref, out_ref, scaled_ref, log_ref):
            scale_row = head_row[layer, :, lanes(pl.program_id(0) * 256 + core * 128, 128)]
            attend(
                q_ref, k_ref, v_ref, scale_row, out_ref, scaled_ref, log_ref, split_ref[place], triangle, turned, walled
            )

        stage(
            body,
            [(own_half.proj, third_spec(0)), (own_half.proj, third_spec(1)), (own_half.proj, third_spec(2))],
            [(own_half.head_out, column_spec(128)), (own_half.scaled, column_spec(128)),
             (own_half.logs, pl.BlockSpec((1, 2, 1024), lambda group: (group, 0, 0)))],
            hooks,
        )

    def out_stage(layer, hooks):
        def body(scaled_ref, w_ref):
            swap_tile(layer * 2, swaps[layer * 2], dot(scaled_ref[...], w_ref[...].reshape(512, 1024)).astype(BF16))

        stage(body, [(saved[layer].scaled, rows_spec(512)), (wholes[layer][1], whole_spec((4, 128, 1024)))], [], hooks)

    def widen_stage(layer, hooks):
        own_half = saved[layer]

        def body(x_ref, a_ref, b_ref, w_ref, res_ref, ffn_ref, gelu_ref, slope_ref):
            branch = a_ref[...].astype(F32) + b_ref[...].astype(F32)
            unit_b, unused = standard(branch)
            residual = x_ref[...].astype(F32) + unit_b * gains[layer, 1:2, :] + shifts[layer, 1:2, :]
            res_ref[...] = residual
            unit_r, unused = standard(residual)
            ffn_input = (unit_r * gains[layer, 2:3, :] + shifts[layer, 2:3, :]).astype(BF16)
            ffn_ref[...] = ffn_input
            first, second = [], []
            for group in range(4):
                hidden = dot(ffn_input, w_ref[group].reshape(1024, 512))
                half = 0.5 + 0.5 * lax.erf(hidden * math.sqrt(0.5))
                gelu = hidden * half
                bell = jnp.exp(-0.5 * hidden * hidden) * (1.0 / math.sqrt(2.0 * math.pi))
                gelu_ref[group] = gelu.astype(BF16)
                slope_ref[group] = (half + hidden * bell).astype(BF16)
                mean = jnp.mean(gelu, axis=-1, keepdims=True)
                centre = gelu - mean
                first.append(mean)
                second.append(jnp.mean(centre * centre, axis=-1, keepdims=True))
            mean = 0.25 * (first[0] + first[1] + first[2] + first[3])
            spread_of = sum(0.25 * (s + (m - mean) * (m - mean)) for m, s in zip(first, second))
            swap_tile(3 + layer, stats[layer], two_columns(mean, spread_of))

        branch_own, branch_other = swaps[layer * 2]
        stage(
            body,
            [(own_half.entry, rows_spec(1024)), (branch_own, rows_spec(1024)), (branch_other, rows_spec(1024)),
             (wholes[layer][2], whole_spec((4, 4, 256, 512)))],
            [(own_half.residual, rows_spec(1024)), (own_half.ffn_input, rows_spec(1024)), (own_half.gelu, group_spec(512)),
             (own_half.slope, group_spec(512))],
            hooks,
        )

    def middle_rows(layer, gelu, mean, scale, group):
        unit_m = (gelu.astype(F32) - mean) * scale
        return (unit_m * mid_row(mid_gain, layer, group) + mid_row(mid_shift, layer, group)).astype(BF16)

    def narrow_stage(layer, hooks):
        own_half = saved[layer]

        def body(g_ref, own_ref, other_ref, w_ref, mid_ref):
            mean, scale = mid_stats(own_ref[...], other_ref[...])
            total = jnp.zeros((TILE, 1024), F32)
            for group in range(4):
                middle = middle_rows(layer, g_ref[group], mean, scale, group)
                mid_ref[group] = middle
                total = total + dot(middle, w_ref[group])
            swap_tile(1, swaps[1], total.astype(BF16))

        stage(
            body,
            [(own_half.gelu, group_spec(512)), (stats[layer][0], rows_spec(128)), (stats[layer][1], rows_spec(128)),
             (wholes[layer][3], whole_spec((4, 512, 1024)))],
            [(own_half.middle, group_spec(512))],
            hooks,
        )

    def middle_stage(layer, hooks):
        own_half = saved[layer]

        def body(g_ref, own_ref, other_ref, mid_ref):
            mean, scale = mid_stats(own_ref[...], other_ref[...])
            for group in range(4):
                mid_ref[group] = middle_rows(layer, g_ref[group], mean, scale, group)

        stage(
            body,
            [(own_half.gelu, group_spec(512)), (stats[layer][0], rows_spec(128)), (stats[layer][1], rows_spec(128))],
            [(own_half.middle, group_spec(512))],
            hooks,
        )

    def layer_forward(layer, hooks, gaps):
        own_half = saved[layer]
        base = layer * 4
        gaps[0]()
        ready(base)
        if layer == 0:
            passed(0)
            take_smalls()
        else:
            swapped(1, swaps[1])
        project_stage(layer, hooks[0])
        attention_stage(layer, hooks[1])
        gaps[1]()
        ready(base + 1)
        out_stage(layer, hooks[2])
        gaps[2]()
        ready(base + 2)
        swapped(layer * 2, swaps[layer * 2])
        for index, (source, target) in enumerate(zip(swaps[layer * 2], (own_half.branch, own_half.branch_other))):
            keep(layer * 2 + index, source, target)
        widen_stage(layer, hooks[3])
        gaps[3]()
        swapped(3 + layer, stats[layer])
        if layer == 0:
            ready(base + 3)
            narrow_stage(layer, hooks[4])
        else:
            middle_stage(layer, hooks[4])

    deep(0)
    items_out(0)
    smalls_out()
    own(0)
    deep(1)
    own(1)
    fill_triangle(triangle)
    first_hop(0)
    deep(2)
    pass_on(0)
    first_hop(1)
    second_hop(0)
    own(2)
    deep(3)
    second_hop(1)
    own(3)
    items_out(1)
    layer_forward(0, ((), ((1, after((first_hop, 2), (deep, 4))),), (), (), ()), (
        after(),
        after((pass_on, 1), (own, 4)),
        after((second_hop, 2), (first_hop, 3), (deep, 5), (own, 5)),
        after((second_hop, 3), (first_hop, 4), (deep, 6), (own, 6)),
    ))
    layer_forward(1, (((1, after((second_hop, 5), (first_hop, 6))),), (), (), (), ()), (
        after((second_hop, 4), (first_hop, 5), (deep, 7), (own, 7)),
        after(),
        after((second_hop, 6), (first_hop, 7)),
        after((second_hop, 7),),
    ))

    for layer in (0, 1):
        for index, source in enumerate(swaps[layer * 2]):
            kept(layer * 2 + index, source)
    passed(1)

    def clean_up():
        for layer in (0, 1):
            @pl.when(core == layer)
            def unused():
                for step in (1, 2, 3):
                    await_bytes(items.at[0], item_send.at[layer, step])
                for step in range(4):
                    await_bytes(items.at[0], item_pass.at[layer, step])
                for index, source in enumerate(small_in):
                    await_bytes(source, small_sems.at[1, index])

        for unit, (layer, matrix) in enumerate(units):
            whole = wholes[layer]

            @pl.when(core == layer)
            def unused_too():
                await_bytes(pieces_view(whole, matrix, 2, 2), own_send.at[unit, 1])
                await_bytes(pieces_view(whole, matrix, 3, 2), deep_send.at[unit])

            await_bytes(pieces_view(whole, matrix, 3, 3), hop_send.at[unit])

    return after((ready, 7)), clean_up


ORDER = tuple((layer, matrix) for layer in (1, 0) for matrix in (3, 2, 1, 0))

class Made(NamedTuple):
    d_middle: object
    d_hidden: object
    d_residual: object
    d_branch: object
    d_heads: object
    d_proj: object
    d_entry: object


def add_up_into(target, *terms):
    rows = target.shape[0]

    def step(index, unused):
        span = pl.ds(pl.multiple_of(index * 32, 32), 32)
        total = target[span, :].astype(F32)
        for term in terms:
            total = total + term[span, :].astype(F32)
        target[span, :] = total.astype(BF16)
        return unused

    lax.fori_loop(0, rows // 32, step, 0)


def whole_kernel(*refs):
    refs = list(refs)

    def take(count):
        found = refs[:count]
        del refs[:count]
        return found

    (split_ref,) = take(1)
    items, *raw = take(5)
    small_in = take(5)
    shares = take(4)
    (ends,) = take(1)
    small_outs = take(5)
    cotangent, output = take(2)
    weights = (take(4), take(4))
    saved = [Saved(*take(13)) for unused in (0, 1)]
    grads = (take(4), take(4))
    made = [Made(*take(7)) for unused in (0, 1)]
    smalls = take(5)
    attention_refs = take(3)
    swaps = [(*take(2),) for unused in range(3)]
    stats = [(*take(2),) for unused in (0, 1)]
    sums = [(*take(2),) for unused in (0, 1)]
    own, first_in, second_in, deep_in = take(4), take(4), take(4), take(4)
    vec, inbox, acc, dk_acc, dv_acc = take(5)
    forward_sems = take(13)
    (load_sem, first_send, first_recv, second_send, second_recv, deep_send, deep_recv, last_send, last_copy,
     last_recv, ends_send, ends_recv, small_send, small_recv, swap_send, swap_recv, credit) = refs
    gains, unused_shifts, mid_gain, unused_mid_shift, head_row = smalls
    triangle, turned, walled = attention_refs
    core, place, depth = here()
    last_ready, clean_up = forward_part(
        items, raw, small_in, cotangent, weights, saved, smalls, split_ref, attention_refs, swaps, stats, forward_sems
    )

    def send_ends(owner, source):
        @pl.when(core == owner)
        def unused():
            for step in (1, 2, 3):
                send(source.at[block_rows(partner(place, step))], ends.at[place], ends_send.at[step], ends_recv.at[step],
                     {DP: partner(place, step)})
            pltpu.make_async_copy(source.at[block_rows(place)], ends.at[place], ends_send.at[0]).start()

    def route(step):
        return (1, 2) if step < 2 else (2, 1)

    def shard_of(step):
        return lax.rem(depth + step, 4)

    def begin(unit):
        layer, matrix = ORDER[unit]
        if unit >= 4:
            pl.semaphore_wait(credit.at[matrix], 2)
        for step in range(4):
            first, second = route(step)
            for index, offset in enumerate((first, 3)):
                send(whole_view(grads[layer], matrix, partner(place, offset), shard_of(step)),
                     first_in[matrix].at[step, index], first_send.at[unit], first_recv.at[unit],
                     {DP: partner(place, first)})
            for index, offset in enumerate((0, second)):
                pltpu.make_async_copy(
                    whole_view(grads[layer], matrix, partner(place, offset), shard_of(step)),
                    own[matrix].at[step, index], load_sem.at[unit],
                ).start()

    def second_hop(unit):
        layer, matrix = ORDER[unit]
        await_bytes(own[matrix], load_sem.at[unit])
        await_bytes(first_in[matrix], first_recv.at[unit])
        for step in range(4):
            first, second = route(step)
            mine = own[matrix].at[step, 1]
            add_up_into(mine, first_in[matrix].at[step, 1])
            send(mine, second_in[matrix].at[step], second_send.at[unit], second_recv.at[unit],
                 {DP: partner(place, second)})

    def deep_hop(unit):
        layer, matrix = ORDER[unit]
        await_bytes(second_in[matrix], second_recv.at[unit])
        for step in (1, 2, 3, 0):
            mine = own[matrix].at[step, 0]
            add_up_into(mine, first_in[matrix].at[step, 0], second_in[matrix].at[step])
            if step:
                send(mine, deep_in[matrix].at[layer, step - 1], deep_send.at[unit], deep_recv.at[unit],
                     {SHARD: shard_of(step)})
        if unit < 4:
            for step in (1, 2):
                pl.semaphore_signal(
                    credit.at[matrix], inc=1, device_id={DP: partner(place, step)}, device_id_type=MESH
                )

    def finish(unit):
        layer, matrix = ORDER[unit]
        await_bytes(deep_in[matrix].at[layer], deep_recv.at[unit])
        mine = own[matrix].at[0, 0]
        add_up_into(mine, *[deep_in[matrix].at[layer, index] for index in range(3)])
        sources = [mine]
        if matrix == 0:
            sources = [mine.at[:, pl.ds(third * 128, 128)] for third in range(3)]
        for half in (0, 1):
            @pl.when(core == half)
            def unused():
                for source, target in zip(sources, raw_views(shares, matrix, half, place)):
                    if half == layer:
                        pltpu.make_async_copy(source, target, last_copy.at[unit]).start()
                        for offset in (1, 2):
                            send(source, target, last_send.at[unit, 0], last_recv.at[unit, half, offset],
                                 {DP: partner(place, offset)})
                    else:
                        send(source, target, last_send.at[unit, 0], last_recv.at[unit, half, 0], {SECTION: layer})

    def forward(unit):
        layer, matrix = ORDER[unit]
        half = 1 - layer

        @pl.when(core == layer)
        def unused():
            views = raw_views(shares, matrix, half, place)
            await_bytes(own[matrix].at[0, 0], last_recv.at[unit, half, 0])
            for view in views:
                for offset in (1, 2):
                    send(view, view, last_send.at[unit, 1], last_recv.at[unit, half, offset],
                         {DP: partner(place, offset)})

    def corner(unit):
        layer, matrix = ORDER[unit]

        @pl.when(core == layer)
        def unused():
            for half in (layer, 1 - layer):
                first, second = (1, 2) if half == 0 else (2, 1)
                await_bytes(own[matrix].at[0, 0], last_recv.at[unit, half, first])
                for view in raw_views(shares, matrix, half, partner(place, first)):
                    send(view, view, last_send.at[unit, 2], last_recv.at[unit, half, 3], {DP: partner(place, second)})

    def free_own(unit):
        layer, matrix = ORDER[unit]

        @pl.when(core == layer)
        def unused():
            await_bytes(own[matrix].at[0], last_send.at[unit, 0])
            await_bytes(own[matrix].at[0, 0], last_copy.at[unit])

        @pl.when(core != layer)
        def unused_too():
            await_bytes(own[matrix].at[0, 0], last_send.at[unit, 0])

    def free_hops(unit):
        layer, matrix = ORDER[unit]
        await_bytes(second_in[matrix], second_send.at[unit])
        await_bytes(deep_in[matrix].at[layer], deep_send.at[unit])
        free_own(unit)

    def clean(unit):
        layer, matrix = ORDER[unit]
        await_bytes(first_in[matrix], first_send.at[unit])
        if unit >= 4:
            free_hops(unit)

        @pl.when(core == layer)
        def unused():
            for row in (1, 2):
                await_bytes(own[matrix].at[0], last_send.at[unit, row])
            for half in (0, 1):
                first, second = (1, 2) if half == 0 else (2, 1)
                await_bytes(own[matrix].at[0, 0], last_recv.at[unit, half, second])
                await_bytes(own[matrix].at[0, 0], last_recv.at[unit, half, 3])

    column = pl.ds(pl.multiple_of(core * 512, 512), 512)
    exchanges = (
        {SECTION: 1 - core},
        {DP: partner(place, 1)},
        {DP: partner(place, 2)},
        {SHARD: partner(depth, 1)},
        {SHARD: partner(depth, 2)},
    )

    def small_step(index):
        if index:
            send(acc.at[index - 1], inbox.at[index], small_send.at[index], small_recv.at[index], exchanges[index])
        else:
            for layer in (0, 1):
                @pl.when(core != layer)
                def unused():
                    vec[layer, 0:6, :] = jnp.zeros((6, 1024), F32)

            for half in (0, 1):
                @pl.when(core == half)
                def unused_too():
                    send(vec.at[1 - half], inbox.at[0], small_send.at[0], small_recv.at[0], exchanges[0])

    def small_take(index):
        await_bytes(inbox.at[index], small_recv.at[index])
        if index:
            acc[index] = acc[index - 1] + inbox[index]
        else:
            for half in (0, 1):
                @pl.when(core == half)
                def unused():
                    acc[0] = vec[half] + inbox[0]

    def swap_tile(index, pair, value):
        own_ref, other_ref = pair
        span = block_rows(pl.program_id(0))
        own_ref[span, :] = value
        send(own_ref.at[span], other_ref.at[span], swap_send.at[index], swap_recv.at[index], {SECTION: 1 - core})

    def swapped(index, pair):
        await_bytes(pair[0], swap_send.at[index])
        await_bytes(pair[1], swap_recv.at[index])

    def mid_row(layer, group):
        return mid_gain[layer, :, lanes(group * 1024 + core * 512, 512)]

    def add_vec(layer, row, value, span=slice(None)):
        vec[layer, row : row + 1, span] += value

    def weight_grad(left, left_spec, right, right_spec, target, target_spec):
        def body(left_ref, right_ref, out_ref):
            a = left_ref[...].reshape(left_ref.shape[-2:])
            b = right_ref[...].reshape(right_ref.shape[-2:])
            value = lax.dot_general(a, b, (((0,), (0,)), ((), ())), preferred_element_type=F32)
            out_ref[...] = value.astype(BF16).reshape(out_ref.shape)

        stage(body, [(left, left_spec), (right, right_spec)], [(target, target_spec)])

    def narrow_stage(layer, grad):
        own_half, make = saved[layer], made[layer]

        def body(c_ref, g_ref, own_ref, other_ref, w_ref, dm_ref):
            mean, scale = mid_stats(own_ref[...], other_ref[...])
            grad_low = c_ref[...]
            first = jnp.zeros((TILE, 1), F32)
            second = jnp.zeros((TILE, 1), F32)
            for group in range(4):
                d_middle = dot_nt(grad_low, w_ref[group])
                dm_ref[group] = d_middle.astype(BF16)
                unit_m = (g_ref[group].astype(F32) - mean) * scale
                product = d_middle * unit_m
                add_vec(layer, 6 + group, jnp.sum(product, axis=0, keepdims=True), column)
                add_vec(layer, 10 + group, jnp.sum(d_middle, axis=0, keepdims=True), column)
                row_gain = mid_row(layer, group)
                first = first + jnp.sum(d_middle * row_gain, axis=-1, keepdims=True)
                second = second + jnp.sum(product * row_gain, axis=-1, keepdims=True)
            swap_tile(layer * 3, sums[layer], two_columns(first, second))

        stage(
            body,
            [(grad, rows_spec(1024)), (own_half.gelu, group_spec(512)), (stats[layer][0], rows_spec(128)),
             (stats[layer][1], rows_spec(128)), (weights[layer][3], whole_spec((4, 512, 1024)))],
            [(make.d_middle, group_spec(512))],
        )

    def widen_stage(layer):
        own_half, make = saved[layer], made[layer]

        def body(dm_ref, g_ref, s_ref, own_ref, other_ref, a_ref, b_ref, w_ref, dh_ref):
            mean, scale = mid_stats(own_ref[...], other_ref[...])
            both = (a_ref[...] + b_ref[...]) * (1.0 / 4096)
            first, second = both[:, 0:1], both[:, 64:65]
            total = jnp.zeros((TILE, 1024), F32)
            for group in range(4):
                unit_m = (g_ref[group].astype(F32) - mean) * scale
                inner = dm_ref[group].astype(F32) * mid_row(layer, group)
                d_gelu = scale * (inner - first - unit_m * second)
                d_hidden = (d_gelu * s_ref[group].astype(F32)).astype(BF16)
                dh_ref[group] = d_hidden
                total = total + dot_nt(d_hidden, w_ref[group].reshape(1024, 512))
            swap_tile(layer * 3 + 1, swaps[0], total.astype(BF16))

        stage(
            body,
            [(make.d_middle, group_spec(512)), (own_half.gelu, group_spec(512)), (own_half.slope, group_spec(512)),
             (stats[layer][0], rows_spec(128)), (stats[layer][1], rows_spec(128)), (sums[layer][0], rows_spec(128)),
             (sums[layer][1], rows_spec(128)), (weights[layer][2], whole_spec((4, 4, 256, 512)))],
            [(make.d_hidden, group_spec(512))],
        )

    def norms_stage(layer, grad):
        own_half, make = saved[layer], made[layer]
        scale_row = jnp.concatenate(
            [head_row[layer, :, lanes(group * 256 + core * 128, 128)] for group in range(4)], axis=1
        )

        def body(c_ref, res_ref, da_ref, db_ref, ba_ref, bb_ref, ho_ref, w_ref, dr_ref, dbr_ref, dh_ref):
            unit_r, scale_r = standard(res_ref[...])
            d_ffn = da_ref[...].astype(F32) + db_ref[...].astype(F32)
            back, gain_third, shift_third = standard_back(unit_r, scale_r, gains[layer, 2:3, :], d_ffn)
            d_residual = c_ref[...].astype(F32) + back
            dr_ref[...] = d_residual
            unit_b, scale_b = standard(ba_ref[...].astype(F32) + bb_ref[...].astype(F32))
            back, gain_second, shift_second = standard_back(unit_b, scale_b, gains[layer, 1:2, :], d_residual)
            d_branch = back.astype(BF16)
            dbr_ref[...] = d_branch
            d_scaled = dot_nt(d_branch, w_ref[...].reshape(512, 1024))
            dh_ref[...] = (d_scaled * scale_row).astype(BF16)
            add_vec(layer, 14, jnp.sum(d_scaled * ho_ref[...].astype(F32), axis=0, keepdims=True), column)
            for row, value in ((1, gain_second), (2, gain_third), (4, shift_second), (5, shift_third)):
                add_vec(layer, row, value)

        stage(
            body,
            [(grad, rows_spec(1024)), (own_half.residual, rows_spec(1024)), (swaps[0][0], rows_spec(1024)),
             (swaps[0][1], rows_spec(1024)), (own_half.branch, rows_spec(1024)),
             (own_half.branch_other, rows_spec(1024)), (own_half.head_out, rows_spec(512)),
             (weights[layer][1], whole_spec((4, 128, 1024)))],
            [(make.d_residual, rows_spec(1024)), (make.d_branch, rows_spec(1024)), (make.d_heads, rows_spec(512))],
        )

    def attention_stage(layer):
        own_half, make = saved[layer], made[layer]

        def body(q_ref, k_ref, v_ref, grad_ref, out_ref, log_ref, back_ref):
            attend_back(
                q_ref, k_ref, v_ref, grad_ref, out_ref, log_ref, back_ref, split_ref[place], triangle, turned, walled, dk_acc, dv_acc
            )

        stage(
            body,
            [(own_half.proj, third_spec(0)), (own_half.proj, third_spec(1)), (own_half.proj, third_spec(2)),
             (make.d_heads, column_spec(128)), (own_half.head_out, column_spec(128)),
             (own_half.logs, pl.BlockSpec((1, 2, 1024), lambda group: (group, 0, 0)))],
            [(make.d_proj, block_spec(1024, 384))],
        )

    def project_stage(layer):
        make = made[layer]

        def body(d_ref, w_ref):
            total = dot_nt(d_ref[0], w_ref[0].reshape(1024, 384))
            for group in range(1, 4):
                total = total + dot_nt(d_ref[group], w_ref[group].reshape(1024, 384))
            swap_tile(layer * 3 + 2, swaps[1], total.astype(BF16))

        stage(
            body, [(make.d_proj, group_spec(384)), (weights[layer][0], whole_spec((4, 4, 256, 384)))], []
        )

    def entry_stage(layer):
        own_half, make = saved[layer], made[layer]

        def body(dr_ref, a_ref, b_ref, x_ref, dx_ref):
            unit_x, scale_x = standard(x_ref[...].astype(F32))
            d_normed = a_ref[...].astype(F32) + b_ref[...].astype(F32)
            back, gain_first, shift_first = standard_back(unit_x, scale_x, gains[layer, 0:1, :], d_normed)
            dx_ref[...] = (dr_ref[...] + back).astype(BF16)
            add_vec(layer, 0, gain_first)
            add_vec(layer, 3, shift_first)

        stage(
            body,
            [(make.d_residual, rows_spec(1024)), (swaps[1][0], rows_spec(1024)),
             (swaps[1][1], rows_spec(1024)), (own_half.entry, rows_spec(1024))],
            [(make.d_entry, rows_spec(1024))],
        )

    def layer_back(layer, grad, events):
        own_half, make = saved[layer], made[layer]
        base = 0 if layer == 1 else 4
        weight_grad(own_half.middle, block_spec(1024, 512), grad, whole_spec((1024, 1024)),
                    grads[layer][3], block_spec(512, 1024))
        events[0]()
        begin(base)
        if layer == 1:
            last_ready()
        narrow_stage(layer, grad)
        events[1]()
        swapped(layer * 3, sums[layer])
        widen_stage(layer)
        events[2]()
        weight_grad(own_half.ffn_input, whole_spec((1024, 1024)), make.d_hidden, block_spec(1024, 512),
                    grads[layer][2], grad_spec(512))
        begin(base + 1)
        swapped(layer * 3 + 1, swaps[0])
        norms_stage(layer, grad)
        events[3]()
        weight_grad(own_half.scaled, column_spec(128), make.d_branch, whole_spec((1024, 1024)),
                    grads[layer][1], block_spec(128, 1024))
        begin(base + 2)
        attention_stage(layer)
        events[4]()
        project_stage(layer)
        events[5]()
        weight_grad(own_half.normed, whole_spec((1024, 1024)), make.d_proj, block_spec(1024, 384),
                    grads[layer][0], grad_spec(384))
        begin(base + 3)
        swapped(layer * 3 + 2, swaps[1])
        entry_stage(layer)
        events[6]()

    def last_stage():
        def body(mid_ref, w_ref):
            total = dot(mid_ref[0], w_ref[0])
            for group in range(1, 4):
                total = total + dot(mid_ref[group], w_ref[group])
            swap_tile(6, swaps[2], total.astype(BF16))

        stage(body, [(saved[1].middle, group_spec(512)), (weights[1][3], whole_spec((4, 512, 1024)))], [])

    def output_stage():
        swapped(6, swaps[2])

        def body(res_ref, a_ref, b_ref, out_ref):
            out_ref[...] = (res_ref[...] + (a_ref[...].astype(F32) + b_ref[...].astype(F32))).astype(BF16)

        stage(
            body,
            [(saved[1].residual, rows_spec(1024)), (swaps[2][0], rows_spec(1024)), (swaps[2][1], rows_spec(1024))],
            [(output, rows_spec(1024))],
        )
        send_ends(1, output)

    def prepare():
        vec[...] = jnp.zeros_like(vec)

    layer_back(1, cotangent, (
        after((prepare,),),
        after(),
        after((second_hop, 0),),
        after((deep_hop, 0),),
        after((second_hop, 1), (finish, 0), (second_hop, 2)),
        after((deep_hop, 1), (forward, 0)),
        after((deep_hop, 2), (corner, 0)),
    ))
    layer_back(0, made[1].d_entry, (
        after((free_hops, 0),),
        after((second_hop, 3), (finish, 1), (finish, 2)),
        after((forward, 1), (forward, 2), (free_hops, 1)),
        after((deep_hop, 3), (second_hop, 4), (corner, 1), (corner, 2), (free_hops, 2)),
        after((deep_hop, 4), (finish, 3), (second_hop, 5), (second_hop, 6)),
        after((forward, 3), (free_hops, 3)),
        after((deep_hop, 5), (finish, 4), (corner, 3), (deep_hop, 6)),
    ))
    small_step(0)
    last_stage()
    second_hop(7)
    output_stage()
    forward(4)
    finish(5)
    finish(6)
    small_take(0)
    small_step(1)
    deep_hop(7)
    send_ends(0, made[0].d_entry)
    corner(4)
    forward(5)
    forward(6)
    small_take(1)
    small_step(2)
    corner(5)
    corner(6)
    small_take(2)
    small_step(3)
    finish(7)
    small_take(3)
    small_step(4)
    forward(7)
    corner(7)
    small_take(4)
    small_outs[0][0] = acc[4, 0:3, :]
    small_outs[1][0] = acc[4, 3:6, :]
    for group in range(4):
        for row in (0, 1):
            small_outs[2 + row][:, group * 1024 : group * 1024 + 1024] = acc[4, 6 + 4 * row + group : 7 + 4 * row + group, :]
    small_outs[4][...] = acc[4, 14:15, :]
    clean_up()
    for unit in range(8):
        clean(unit)
    for index in range(5):
        await_bytes(inbox.at[index], small_send.at[index])
    for step in range(4):
        await_bytes(ends.at[0], ends_send.at[step])
    for step in (1, 2, 3):
        await_bytes(ends.at[0], ends_recv.at[step])


def both_layers(split_at, items, weights, smalls):
    anywhere = pl.BlockSpec(memory_space=pl.ANY)
    local_space = pl.BlockSpec(memory_space=pltpu.VMEM)
    dma = pltpu.SemaphoreType.DMA
    rows, rows_wide = array((1024, 1024), BF16), array((1024, 1024), F32)
    weight_shapes = [
        array((4, 4, 256, 384), BF16),
        array((4, 128, 1024), BF16),
        array((4, 4, 256, 512), BF16),
        array((4, 512, 1024), BF16),
    ]
    wide, heads, proj = array((4, 1024, 512), BF16), array((1024, 512), BF16), array((4, 1024, 384), BF16)
    saved = [rows, rows, proj, heads, heads, array((4, 2, 1024), F32), rows, rows, rows_wide, rows, wide, wide, wide]
    made = [wide, wide, rows_wide, rows, heads, proj, rows]
    small_shapes = [(2,) + operand.shape for operand in smalls]
    shapes = [
        array((256, 3072), BF16),
        array((256, 1024), BF16),
        array((256, 4096), BF16),
        array((1024, 1024), BF16),
        array((4, 256, 1024), BF16),
        array((1, 3, 1024), F32),
        array((1, 3, 1024), F32),
        array((1, 4096), F32),
        array((1, 4096), F32),
        array((1, 1024), F32),
        rows,
        rows,
        *weight_shapes * 2,
        *saved * 2,
        *weight_shapes * 2,
        *made * 2,
    ]
    return pl.pallas_call(
        whole_kernel,
        in_specs=[pl.BlockSpec(memory_space=pltpu.SMEM)] + [anywhere] * 10,
        out_specs=[anywhere] * 5 + [local_space] * 5 + [anywhere] * (len(shapes) - 10),
        out_shape=shapes,
        scratch_shapes=[pltpu.VMEM(shape, F32) for shape in small_shapes]
        + [pltpu.VMEM((256, 256), F32), pltpu.VMEM((128, 1024), BF16), pltpu.VMEM((2, 1024, 128), BF16)]
        + [pltpu.VMEM((1024, 1024), BF16)] * 6
        + [pltpu.VMEM((1024, 128), F32)] * 8
        + [pltpu.VMEM((4, 2) + size, BF16) for size in SIZES]
        + [pltpu.VMEM((4, 2) + size, BF16) for size in SIZES]
        + [pltpu.VMEM((4,) + size, BF16) for size in SIZES]
        + [pltpu.VMEM((2, 3) + size, BF16) for size in SIZES]
        + [pltpu.VMEM((2, 16, 1024), F32), pltpu.VMEM((5, 16, 1024), F32), pltpu.VMEM((5, 16, 1024), F32)]
        + [pltpu.VMEM((1024, 128), F32), pltpu.VMEM((1024, 128), F32)]
        + [
            dma((2, 4)), dma((2, 4)), dma((2, 4)), dma((8, 2)), dma((8,)),
            dma((8,)), dma((8, 4)), dma((8,)), dma((8, 3, 3)), dma((3, 5)),
            dma((5,)), dma((5,)), dma((4,)),
        ]
        + [dma((8,))] * 7
        + [dma((8, 3)), dma((8,)), dma((8, 2, 4)), dma((4,)), dma((4,)), dma((5,)), dma((5,)), dma((7,)), dma((7,))]
        + [pltpu.SemaphoreType.REGULAR((4,))],
        compiler_params=pltpu.CompilerParams(
            collective_id=0, has_side_effects=True, vmem_limit_bytes=62 * 2**20
        ),
    )(split_at, items, *weights, *smalls)[:10]


def local(
    boundary,
    first_len,
    qkv_weight,
    out_weight,
    up_weight,
    down_weight,
    norm_gain,
    norm_shift,
    mid_gain,
    mid_shift,
    head_scale,
):
    *shares, ends, gain_sums, shift_sums, mid_gain_sums, mid_shift_sums, head_sums = both_layers(
        first_len[:, 0],
        boundary.reshape(4, 256, 1024),
        (qkv_weight[0], out_weight[0], up_weight[0], down_weight[0]),
        (norm_gain[0], norm_shift[0], mid_gain, mid_shift, jnp.repeat(head_scale, 64, axis=1)),
    )
    head_sums = jnp.sum(head_sums.reshape(2, 4, 2, 64), axis=3).transpose(1, 0, 2).reshape(1, 16)
    return (
        ends[None, :, None],
        *[share.astype(F32)[None] for share in shares],
        gain_sums,
        shift_sums,
        mid_gain_sums,
        mid_shift_sums,
        head_sums,
    )


def fits(mesh, boundary, mid_gain, head_scale):
    sizes = (mesh.shape["section"], mesh.shape["dp"], mesh.shape["shard"])
    return (
        sizes == (2, 4, 4)
        and boundary == (2, 4, 4, 1024, 1024)
        and mid_gain == (2, 4096)
        and head_scale == (2, 16)
    )


def solution(mesh):
    placed = (
        P("section", None, "shard", "dp", None),
        P(None, "shard"),
        P("section", "shard", None),
        P("section", "shard", None),
        P("section", "shard", None),
        P("section", "shard", None),
        P("section", None, None),
        P("section", None, None),
        P("section", None),
        P("section", None),
        P("section", None),
    )
    results = (
        P("section", None, "shard", "dp", None),
        P("section", "shard", None),
        P("section", "shard", None),
        P("section", "shard", None),
        P("section", "shard", None),
        P("section", None, None),
        P("section", None, None),
        P("section", None),
        P("section", None),
        P("section", None),
    )

    def whole(*arrays):
        fast = fits(mesh, arrays[0].shape, arrays[8].shape, arrays[10].shape)
        body = local if fast else general
        return jax.shard_map(
            body, mesh=mesh, in_specs=placed, out_specs=results, check_vma=False
        )(*arrays)

    return whole
```

```python
import functools
import math
from typing import NamedTuple

import jax
import jax.numpy as jnp
from jax import lax
from jax.experimental import pallas as pl
from jax.experimental.pallas import tpu as pltpu
from jax.sharding import PartitionSpec as P

EPSILON = 1e-05


def shifted(value, axis, steps):
    count = lax.axis_size(axis)
    first, last = (max(0, -steps), min(count, count - steps))
    return lax.ppermute(value, axis, [(source, source + steps) for source in range(first, last)])


def normalize(values_in, gain, shift):
    centre = values_in - jnp.mean(values_in, axis=-1, keepdims=True)
    spread = jnp.mean(centre * centre, axis=-1, keepdims=True)
    return centre * lax.rsqrt(spread + EPSILON) * gain + shift


def middle_norm(hidden, mid_gain, mid_shift):
    return normalize(jax.nn.gelu(hidden, approximate=False), mid_gain, mid_shift)


def contract_rows(left, right):
    return lax.dot_general(
        left, right, (((0,), (0,)), ((), ())), preferred_element_type=jnp.float32
    )


def contract_cols(left, right):
    return lax.dot_general(
        left, right, (((1,), (1,)), ((), ())), preferred_element_type=jnp.float32
    )


def visible(query_place, key_place, split_at):
    same_doc = (query_place[:, None] < split_at) == (key_place[None, :] < split_at)
    return same_doc & (key_place[None, :] <= query_place[:, None])


def forward_parts(stream_in, weights, small, split_at, head_count):
    weight_qkv, weight_out, weight_up, weight_down = weights
    gains, shifts, mid_gain, mid_shift, head_scale = small
    row_count, model_width = stream_in.shape
    head_dim = model_width // head_count
    factor = 1.0 / math.sqrt(head_dim)
    normed = normalize(stream_in, gains[0], shifts[0]).astype(jnp.bfloat16)
    projected = jnp.dot(normed, weight_qkv, preferred_element_type=jnp.float32).astype(jnp.bfloat16)
    queries = projected[:, :model_width].reshape(row_count, head_count, head_dim)
    key_rows = projected[:, model_width : 2 * model_width].reshape(row_count, head_count, head_dim)
    value_rows = projected[:, 2 * model_width :].reshape(row_count, head_count, head_dim)
    keys_all, values_all = (
        lax.all_gather(key_rows, "dp", axis=0, tiled=True),
        lax.all_gather(value_rows, "dp", axis=0, tiled=True),
    )
    seq_len = keys_all.shape[0]
    own_place = lax.axis_index("dp") * row_count + jnp.arange(row_count, dtype=jnp.int32)
    all_place = jnp.arange(seq_len, dtype=jnp.int32)
    allowed = visible(own_place, all_place, split_at)
    scores = (
        jnp.einsum("qhd,khd->hqk", queries, keys_all, preferred_element_type=jnp.float32) * factor
    )
    scores = jnp.where(allowed[None], scores, -1e30)
    row_max = jnp.max(scores, axis=-1, keepdims=True)
    log_total = row_max + jnp.log(jnp.sum(jnp.exp(scores - row_max), axis=-1, keepdims=True))
    attend = jnp.exp(scores - log_total)
    attend_low = attend.astype(jnp.bfloat16)
    head_out = jnp.einsum(
        "hqk,khd->qhd", attend_low, values_all, preferred_element_type=jnp.float32
    )
    scaled = (
        (head_out * head_scale[None, :, None]).astype(jnp.bfloat16).reshape(row_count, model_width)
    )
    branch = jnp.dot(scaled, weight_out, preferred_element_type=jnp.float32)
    residual = stream_in + normalize(branch, gains[1], shifts[1])
    ffn_input = normalize(residual, gains[2], shifts[2]).astype(jnp.bfloat16)
    hidden = jnp.dot(ffn_input, weight_up, preferred_element_type=jnp.float32)
    middle = middle_norm(hidden, mid_gain, mid_shift).astype(jnp.bfloat16)
    return dict(
        normed=normed,
        queries=queries,
        key_rows=key_rows,
        value_rows=value_rows,
        keys_all=keys_all,
        values_all=values_all,
        own_place=own_place,
        all_place=all_place,
        attend=attend,
        attend_low=attend_low,
        log_total=log_total,
        head_out=head_out,
        scaled=scaled,
        branch=branch,
        residual=residual,
        ffn_input=ffn_input,
        hidden=hidden,
        middle=middle,
        factor=factor,
    )


def backward_parts(stream_in, grad_in, weights, small, split_at, head_count):
    weight_qkv, weight_out, weight_up, weight_down = weights
    gains, shifts, mid_gain, mid_shift, head_scale = small
    parts = forward_parts(stream_in, weights, small, split_at, head_count)
    row_count, model_width = stream_in.shape
    head_dim = model_width // head_count
    factor = parts["factor"]
    grad_down = contract_rows(parts["middle"], grad_in)
    d_middle = contract_cols(grad_in, weight_down)
    unused, pull_middle = jax.vjp(middle_norm, parts["hidden"], mid_gain, mid_shift)
    d_hidden, grad_mid_gain, grad_mid_shift = pull_middle(d_middle)
    d_hidden = d_hidden.astype(jnp.bfloat16)
    grad_up = contract_rows(parts["ffn_input"], d_hidden)
    d_ffn_input = contract_cols(d_hidden, weight_up)
    unused, pull_third = jax.vjp(normalize, parts["residual"], gains[2], shifts[2])
    d_residual, gain_third, shift_third = pull_third(d_ffn_input)
    d_residual = d_residual + grad_in.astype(jnp.float32)
    unused, pull_second = jax.vjp(normalize, parts["branch"], gains[1], shifts[1])
    d_branch, gain_second, shift_second = pull_second(d_residual)
    d_branch = d_branch.astype(jnp.bfloat16)
    grad_out = contract_rows(parts["scaled"], d_branch)
    d_scaled = contract_cols(d_branch, weight_out).reshape(row_count, head_count, head_dim)
    grad_head_scale = jnp.sum(d_scaled * parts["head_out"], axis=(0, 2))
    d_heads = (d_scaled * head_scale[None, :, None]).astype(jnp.bfloat16)
    attend = parts["attend"]
    d_attend = jnp.einsum(
        "qhd,khd->hqk", d_heads, parts["values_all"], preferred_element_type=jnp.float32
    )
    row_dot = jnp.sum(attend * d_attend, axis=-1, keepdims=True)
    d_scores = (attend * (d_attend - row_dot)).astype(jnp.bfloat16)
    d_query = (
        jnp.einsum("hqk,khd->qhd", d_scores, parts["keys_all"], preferred_element_type=jnp.float32)
        * factor
    ).astype(jnp.bfloat16)
    full_keys = (
        jnp.einsum("hqk,qhd->khd", d_scores, parts["queries"], preferred_element_type=jnp.float32)
        * factor
    )
    full_values = jnp.einsum(
        "hqk,qhd->khd", parts["attend_low"], d_heads, preferred_element_type=jnp.float32
    )
    d_keys, d_values = (
        lax.psum_scatter(full_keys, "dp", scatter_dimension=0, tiled=True),
        lax.psum_scatter(full_values, "dp", scatter_dimension=0, tiled=True),
    )
    d_projected = jnp.concatenate(
        [
            d_query.reshape(row_count, model_width),
            d_keys.astype(jnp.bfloat16).reshape(row_count, model_width),
            d_values.astype(jnp.bfloat16).reshape(row_count, model_width),
        ],
        axis=1,
    )
    grad_qkv = contract_rows(parts["normed"], d_projected)
    d_normed = contract_cols(d_projected, weight_qkv)
    unused, pull_first = jax.vjp(normalize, stream_in, gains[0], shifts[0])
    d_entry, gain_first, shift_first = pull_first(d_normed)
    d_entry = d_entry + d_residual
    big_grads = (grad_qkv, grad_out, grad_up, grad_down)
    small_grads = (
        jnp.stack([gain_first, gain_second, gain_third]),
        jnp.stack([shift_first, shift_second, shift_third]),
        grad_mid_gain,
        grad_mid_shift,
        grad_head_scale,
    )
    return (d_entry, big_grads, small_grads)


def add_up(first_term, second_term):
    return first_term + second_term


def general(
    boundary,
    first_len,
    qkv_weight,
    out_weight,
    up_weight,
    down_weight,
    norm_gain,
    norm_shift,
    mid_gain,
    mid_shift,
    head_scale,
):
    section_index = lax.axis_index("section")
    gathered = (
        lax.all_gather(qkv_weight, "shard", axis=1, tiled=True),
        lax.all_gather(out_weight, "shard", axis=1, tiled=True),
        lax.all_gather(up_weight, "shard", axis=1, tiled=True),
        lax.all_gather(down_weight, "shard", axis=1, tiled=True),
    )
    weights = tuple((piece[0] for piece in gathered))
    small = (norm_gain[0], norm_shift[0], mid_gain[0], mid_shift[0], head_scale[0])
    head_count = head_scale.shape[1]
    micro = boundary.shape[1]
    row_count = boundary.shape[3]
    model_width = boundary.shape[4]
    local_ends = boundary[0, :, 0]
    splits = first_len[:, 0]

    def forward_tick(step_index, carry):
        incoming, kept, ends = carry
        index = step_index - section_index
        active = (index >= 0) & (index < micro)
        slot = jnp.clip(index, 0, micro - 1)
        entry = jnp.where(section_index == 0, local_ends[slot], incoming)
        parts = forward_parts(entry.astype(jnp.float32), weights, small, splits[slot], head_count)
        result = (
            parts["residual"]
            + jnp.dot(parts["middle"], weights[3], preferred_element_type=jnp.float32)
        ).astype(jnp.bfloat16)
        kept = kept.at[slot].set(jnp.where(active, entry, kept[slot]))
        ends = ends.at[slot].set(jnp.where(active, result, ends[slot]))
        incoming = shifted(result, "section", 1)
        return (incoming, kept, ends)

    blank = jnp.zeros((row_count, model_width), jnp.bfloat16)
    stack_blank = jnp.zeros((micro, row_count, model_width), jnp.bfloat16)
    unused, kept, ends = lax.fori_loop(
        0, micro + 1, forward_tick, (blank, stack_blank, stack_blank)
    )

    def backward_tick(step_index, carry):
        incoming, ends, big_sums, small_sums = carry
        index = micro - step_index - section_index
        active = (index >= 0) & (index < micro)
        slot = jnp.clip(index, 0, micro - 1)
        grad_in = jnp.where(section_index == 1, local_ends[slot], incoming)
        grad_in = jnp.where(active, grad_in, jnp.zeros_like(grad_in))
        d_entry, big_grads, small_grads = backward_parts(
            kept[slot].astype(jnp.float32), grad_in, weights, small, splits[slot], head_count
        )
        d_low = d_entry.astype(jnp.bfloat16)
        ends = ends.at[slot].set(jnp.where(active & (section_index == 0), d_low, ends[slot]))
        big_sums = jax.tree.map(add_up, big_sums, big_grads)
        small_sums = jax.tree.map(add_up, small_sums, small_grads)
        incoming = shifted(d_low, "section", -1)
        return (incoming, ends, big_sums, small_sums)

    big_zero = tuple((jnp.zeros(item.shape, jnp.float32) for item in weights))
    small_zero = tuple((jnp.zeros(item.shape, jnp.float32) for item in small))
    unused, ends, big_sums, small_sums = lax.fori_loop(
        0, micro + 1, backward_tick, (blank, ends, big_zero, small_zero)
    )
    shares = (
        lax.psum_scatter(big_sums[0][None], "shard", scatter_dimension=1, tiled=True),
        lax.psum_scatter(big_sums[1][None], "shard", scatter_dimension=1, tiled=True),
        lax.psum_scatter(big_sums[2][None], "shard", scatter_dimension=1, tiled=True),
        lax.psum_scatter(big_sums[3][None], "shard", scatter_dimension=1, tiled=True),
    )
    shares = lax.psum((shares[0], shares[1], shares[2], shares[3]), "dp")
    totals = lax.psum(
        (small_sums[0], small_sums[1], small_sums[2], small_sums[3], small_sums[4]), ("dp", "shard")
    )
    return (
        ends[None, :, None],
        shares[0],
        shares[1],
        shares[2],
        shares[3],
        totals[0][None],
        totals[1][None],
        totals[2][None],
        totals[3][None],
        totals[4][None],
    )


BF16 = jnp.bfloat16
F32 = jnp.float32
TILE = 256
SECTION, DP, SHARD = "section", "dp", "shard"


def rows_spec(columns):
    return pl.BlockSpec((TILE, columns), lambda step: (step, 0))


def group_spec(columns):
    return pl.BlockSpec((4, TILE, columns), lambda step: (0, step, 0))


def array(shape, dtype):
    return jax.ShapeDtypeStruct(shape, dtype)


def dot(left, right):
    return jnp.dot(left, right, preferred_element_type=F32)


def dot_nt(left, right):
    return lax.dot_general(left, right, (((1,), (1,)), ((), ())), preferred_element_type=F32)


def standard(values_in):
    centre = values_in - jnp.mean(values_in, axis=-1, keepdims=True)
    spread_of = jnp.mean(centre * centre, axis=-1, keepdims=True)
    scale = lax.rsqrt(spread_of + EPSILON)
    return centre * scale, scale


def standard_back(unit_values, scale, gain, grad):
    inner = grad * gain
    first = jnp.mean(inner, axis=-1, keepdims=True)
    second = jnp.mean(inner * unit_values, axis=-1, keepdims=True)
    back = scale * (inner - first - unit_values * second)
    return back, jnp.sum(grad * unit_values, axis=0, keepdims=True), jnp.sum(grad, axis=0, keepdims=True)


def lane_masks(rows):
    lanes = lax.broadcasted_iota(jnp.int32, (rows, 128), 1)
    return lanes < 64


def two_columns(first, second):
    return jnp.where(lane_masks(first.shape[0]), first, second)


def mid_stats(own, other):
    mean_own, mean_other = own[:, 0:1], other[:, 0:1]
    gap = mean_own - mean_other
    spread_of = 0.5 * (own[:, 64:65] + other[:, 64:65]) + 0.25 * gap * gap
    return 0.5 * (mean_own + mean_other), lax.rsqrt(spread_of + EPSILON)


def fill_triangle(triangle_ref):
    keys = lax.broadcasted_iota(jnp.int32, (256, 256), 0)
    queries = lax.broadcasted_iota(jnp.int32, (256, 256), 1)
    triangle_ref[...] = jnp.where(keys <= queries, 0.0, -1e30)


def own_lanes(rows, half):
    lane = lax.broadcasted_iota(jnp.int32, (rows, 128), 1)
    return (lane < 64 if half == 0 else lane >= 64), lane == 64 * (1 - half)


def walled_keys(keys, split_at, half):
    mine, spare = own_lanes(1024, half)
    row = lax.broadcasted_iota(jnp.int32, (1024, 128), 0)
    return jnp.where(mine, keys, jnp.where(spare & (row < split_at), -1e30, 0.0).astype(BF16))


def walled_queries(queries, split_at, half, start):
    mine, spare = own_lanes(256, half)
    row = lax.broadcasted_iota(jnp.int32, (256, 128), 0) + start
    return jnp.where(mine, queries, jnp.where(spare & (row >= split_at), 1.0, 0.0).astype(BF16))


def score_parts(keys_ref, queries, block, triangle_ref):
    parts = []
    for part in range(2 * (block + 1)):
        scores = dot_nt(keys_ref[part * 128 : part * 128 + 128, :], queries)
        if part >= 2 * block:
            scores = scores + triangle_ref[(part - 2 * block) * 128 : (part - 2 * block) * 128 + 128, :]
        parts.append(scores)
    return parts


def run_lagged(first, second):
    tasks = [(block, half) for block in (3, 2, 1, 0) for half in (0, 1)]
    before = None
    for task in tasks:
        held = first(*task)
        if before is not None:
            second(*before)
        before = (*task, held)
    second(*before)


def attend(q_ref, k_ref, v_ref, scale_row, out_ref, scaled_ref, log_ref, split_at, triangle_ref, turned_ref, keys_ref):
    turned_ref[...] = v_ref[0].astype(F32).T.astype(BF16)
    for half in range(2):
        keys_ref[half] = walled_keys(k_ref[0], split_at, half)
    found = {}

    def score(block, half):
        queries = (q_ref[0, pl.ds(block * 256, 256), :] * 0.125).astype(BF16)
        parts = score_parts(keys_ref.at[half], walled_queries(queries, split_at, half, block * 256), block, triangle_ref)
        tops = functools.reduce(jnp.maximum, [jnp.max(part.reshape(16, 8, 256), axis=0) for part in parts])
        return parts, jnp.max(tops, axis=0, keepdims=True)

    def mix(block, half, held):
        parts, top = held
        span = pl.ds(block * 256, 256)
        powers = [jnp.exp(part - top) for part in parts]
        total = functools.reduce(jnp.add, [jnp.sum(power.reshape(16, 8, 256), axis=0) for power in powers])
        total = jnp.sum(total, axis=0, keepdims=True)
        low = jnp.concatenate([power.astype(BF16) for power in powers], axis=0)
        mixed = dot(turned_ref[half * 64 : half * 64 + 64, : (block + 1) * 256], low)
        log_ref[0, half : half + 1, span] = top + jnp.log(total)
        found[half] = mixed * (1.0 / total)
        if half == 1:
            head_out = jnp.concatenate([found[0], found[1]], axis=0).T
            out_ref[span, :] = head_out.astype(BF16)
            scaled_ref[span, :] = (head_out * scale_row).astype(BF16)

    run_lagged(score, mix)


def attend_back(
    q_ref, k_ref, v_ref, grad_ref, out_ref, log_ref, back_ref, split_at, triangle_ref, turned_ref, keys_ref, dk_ref, dv_ref
):
    turned_ref[...] = k_ref[0].astype(F32).T.astype(BF16)
    for half in range(2):
        keys_ref[half] = walled_keys(k_ref[0], split_at, half)
    products, found = {}, {}

    def score(block, half):
        span = pl.ds(block * 256, 256)
        mine, unused = own_lanes(256, half)
        queries = (q_ref[0, span, :] * 0.125).astype(BF16)
        grad = grad_ref[span, :]
        own_grad = jnp.where(mine, grad, 0.0).astype(BF16)
        if half == 0:
            products[block] = (grad.astype(F32) * out_ref[span, :].astype(F32)).T
        row_dot = jnp.sum(products[block][half * 64 : half * 64 + 64, :], axis=0, keepdims=True)
        parts = score_parts(keys_ref.at[half], walled_queries(queries, split_at, half, block * 256), block, triangle_ref)
        lows, grads = [], []
        for part, scores in enumerate(parts):
            attend_part = jnp.exp(scores - log_ref[0, half : half + 1, span])
            d_attend = dot_nt(v_ref[0, part * 128 : part * 128 + 128, :], own_grad)
            lows.append(attend_part.astype(BF16))
            grads.append((attend_part * (d_attend - row_dot)).astype(BF16))
        own_queries = jnp.where(mine, queries, 0.0).astype(BF16)
        return jnp.concatenate(lows, axis=0), jnp.concatenate(grads, axis=0), own_queries, own_grad

    def mix(block, half, held):
        low, d_scores, own_queries, own_grad = held
        seen = pl.ds(0, (block + 1) * 256)
        found[half] = dot(turned_ref[half * 64 : half * 64 + 64, : (block + 1) * 256], d_scores)
        if (block, half) == (3, 0):
            dv_ref[...] = dot(low, own_grad)
            dk_ref[...] = dot(d_scores, own_queries)
        else:
            dv_ref[seen, :] += dot(low, own_grad)
            dk_ref[seen, :] += dot(d_scores, own_queries)
        if half == 1:
            d_query = jnp.concatenate([found[0], found[1]], axis=0).T * 0.125
            back_ref[0, pl.ds(block * 256, 256), 0:128] = d_query.astype(BF16)

    run_lagged(score, mix)
    back_ref[0, :, 128:256] = dk_ref[...].astype(BF16)
    back_ref[0, :, 256:384] = dv_ref[...].astype(BF16)


MESH = pl.DeviceIdType.MESH
SIZES = ((256, 384), (128, 256), (256, 512), (512, 256))


def partner(place, step):
    return {0: place, 1: place + 1 - 2 * lax.rem(place, 2), 2: lax.rem(place + 2, 4), 3: 3 - place}[step]


def here():
    return lax.axis_index("section"), lax.axis_index("dp"), lax.axis_index("shard")


def greet(core, place, depth):
    barrier = pltpu.get_barrier_semaphore()
    targets = [{SHARD: lax.rem(depth + step, 4)} for step in (1, 2, 3)]
    targets += [{SECTION: 1 - core, SHARD: lax.rem(depth + step, 4)} for step in range(4)]
    targets += [{DP: partner(place, step)} for step in (1, 2, 3)]
    for target in targets:
        pl.semaphore_signal(barrier, inc=1, device_id=target, device_id_type=MESH)
    pl.semaphore_wait(barrier, len(targets))


def send(source, target, send_sem, recv_sem, device):
    copy = pltpu.make_async_remote_copy(
        src_ref=source, dst_ref=target, send_sem=send_sem, recv_sem=recv_sem,
        device_id=device, device_id_type=MESH,
    )
    copy.start()


def await_bytes(view, sem):
    pltpu.make_async_copy(view, view, sem).wait()


def lanes(start, size):
    return pl.ds(pl.multiple_of(start, 128), size)


def raw_views(raw, matrix, half, quarter):
    if matrix == 0:
        return [raw[0].at[:, lanes(third * 1024 + quarter * 256 + half * 128, 128)] for third in range(3)]
    if matrix == 1:
        return [raw[1].at[pl.ds(half * 128, 128), lanes(quarter * 256, 256)]]
    if matrix == 2:
        return [raw[2].at[:, lanes(quarter * 1024 + half * 512, 512)]]
    return [raw[3].at[pl.ds(half * 512, 512), lanes(quarter * 256, 256)]]


def whole_view(whole, matrix, quarter, shard):
    if matrix in (0, 2):
        return whole[matrix].at[quarter, shard]
    return whole[matrix].at[shard, :, lanes(quarter * 256, 256)]


def whole_views(whole, matrix, quarter, shard):
    if matrix == 0:
        return [whole[0].at[quarter, shard, :, pl.ds(third * 128, 128)] for third in range(3)]
    return [whole_view(whole, matrix, quarter, shard)]


def pieces_view(whole, matrix, first, second):
    if matrix in (0, 2):
        return whole[matrix].at[pl.ds(0, first), pl.ds(0, second)]
    return whole[matrix].at[pl.ds(0, first), :, pl.ds(0, 256 * second)]


class Saved(NamedTuple):
    entry: object
    normed: object
    proj: object
    head_out: object
    scaled: object
    logs: object
    branch: object
    branch_other: object
    residual: object
    ffn_input: object
    gelu: object
    slope: object
    middle: object


def whole_spec(shape):
    return pl.BlockSpec(shape, lambda step: (0,) * len(shape), pipeline_mode=pl.Buffered(1))


def block_spec(rows, columns):
    return pl.BlockSpec((1, rows, columns), lambda step: (step, 0, 0))


def grad_spec(columns):
    return pl.BlockSpec((1, 4, 256, columns), lambda step: (step, 0, 0, 0))


def column_spec(columns):
    return pl.BlockSpec((1024, columns), lambda step: (0, step))


def third_spec(third):
    return pl.BlockSpec((1, 1024, 128), lambda group: (group, 0, third))


def stage(body, ins, outs, hooks=()):
    def hooked(*refs):
        body(*refs)
        for step, action in hooks:
            pl.when(pl.program_id(0) == step)(action)

    pltpu.emit_pipeline(
        hooked, grid=(4,), in_specs=[spec for unused, spec in ins], out_specs=[spec for unused, spec in outs]
    )(*[ref for ref, unused in ins], *[ref for ref, unused in outs])


def after(*actions):
    def run():
        for action, *arguments in actions:
            action(*arguments)

    return run


def block_rows(index):
    return pl.ds(pl.multiple_of(index * 256, 256), 256)


def forward_part(items, raw, small_in, cotangent, wholes, saved, smalls, split_ref, attention_refs, swaps, stats, sems):
    gains, shifts, mid_gain, mid_shift, head_row = smalls
    triangle, turned, walled = attention_refs
    (item_send, item_recv, item_pass, own_send, own_recv, deep_send, deep_recv, hop_send, hop_recv, small_sems,
     swap_send, swap_recv, keep_sem) = sems
    core, place, depth = here()
    arrays = (saved[0].entry, cotangent)
    greet(core, place, depth)

    def items_out(layer):
        @pl.when(core == layer)
        def unused():
            for step in (1, 2, 3):
                send(items.at[partner(place, step)], arrays[layer].at[block_rows(place)], item_send.at[layer, step],
                     item_recv.at[layer, step], {DP: partner(place, step)})
            pltpu.make_async_copy(items.at[place], arrays[layer].at[block_rows(place)], item_send.at[layer, 0]).start()
            send(items.at[place], arrays[layer].at[block_rows(place)], item_pass.at[layer, 0], item_recv.at[layer, 0],
                 {SECTION: 1 - layer})

    def smalls_out():
        for layer in (0, 1):
            @pl.when(core == layer)
            def unused():
                for index, (source, target) in enumerate(zip(small_in, smalls)):
                    pltpu.make_async_copy(source, target.at[layer], small_sems.at[0, index]).start()
                    send(source, target.at[layer], small_sems.at[1, index], small_sems.at[2, index],
                         {SECTION: 1 - layer})

    units = [(layer, matrix) for layer in (0, 1) for matrix in range(4)]

    def deep(unit):
        layer, matrix = units[unit]

        @pl.when(core == layer)
        def unused():
            for step in (1, 2, 3):
                for half in (0, 1):
                    for source, target in zip(
                        raw_views(raw, matrix, half, place), whole_views(wholes[layer], matrix, place, depth)
                    ):
                        send(source, target, deep_send.at[unit], deep_recv.at[unit, step],
                             {SECTION: half, SHARD: lax.rem(depth + 4 - step, 4)})

    def own(unit):
        layer, matrix = units[unit]

        @pl.when(core == layer)
        def unused():
            for quarter in range(4):
                for source, target in zip(
                    raw_views(raw, matrix, layer, quarter), whole_views(wholes[layer], matrix, quarter, depth)
                ):
                    pltpu.make_async_copy(source, target, own_send.at[unit, 0]).start()
                for source, target in zip(
                    raw_views(raw, matrix, 1 - layer, quarter), whole_views(wholes[layer], matrix, quarter, depth)
                ):
                    send(source, target, own_send.at[unit, 1], own_recv.at[unit], {SECTION: 1 - layer})

    def route(unit, step):
        return (1, 2) if (unit + step) % 2 == 0 else (2, 1)

    def piece(unit, offset, step):
        layer, matrix = units[unit]
        return whole_view(wholes[layer], matrix, partner(place, offset), lax.rem(depth + step, 4))

    def first_hop(unit):
        for step in (1, 2, 3):
            first, second = route(unit, step)
            await_bytes(piece(unit, 0, step), deep_recv.at[unit, step])
            for offset in (first, second):
                send(piece(unit, 0, step), piece(unit, 0, step), hop_send.at[unit], hop_recv.at[unit, step - 1, offset - 1],
                     {DP: partner(place, offset)})

    def second_hop(unit):
        for step in (1, 2, 3):
            first, second = route(unit, step)
            await_bytes(piece(unit, first, step), hop_recv.at[unit, step - 1, first - 1])
            send(piece(unit, first, step), piece(unit, first, step), hop_send.at[unit], hop_recv.at[unit, step - 1, 2],
                 {DP: partner(place, second)})

    def ready(unit):
        layer, matrix = units[unit]
        quarters = pieces_view(wholes[layer], matrix, 2, 2)

        @pl.when(core == layer)
        def unused():
            await_bytes(quarters, own_send.at[unit, 0])

        @pl.when(core != layer)
        def unused_too():
            await_bytes(quarters, own_recv.at[unit])

        for step in (1, 2, 3):
            first, second = route(unit, step)
            await_bytes(piece(unit, 0, 0), hop_recv.at[unit, step - 1, second - 1])
            await_bytes(piece(unit, 0, 0), hop_recv.at[unit, step - 1, 2])

    def pass_on(layer):
        @pl.when(core == layer)
        def unused():
            for step in (1, 2, 3):
                block = arrays[layer].at[block_rows(partner(place, step))]
                await_bytes(block, item_recv.at[layer, step])
                send(block, block, item_pass.at[layer, step], item_recv.at[layer, step], {SECTION: 1 - layer})

    def passed(layer):
        @pl.when(core == layer)
        def unused():
            await_bytes(items.at[0], item_send.at[layer, 0])

        @pl.when(core != layer)
        def unused_too():
            for step in range(4):
                await_bytes(items.at[0], item_recv.at[layer, step])

    def take_smalls():
        for index, (source, target) in enumerate(zip(small_in, smalls)):
            for layer in (0, 1):
                @pl.when(core == layer)
                def unused():
                    await_bytes(source, small_sems.at[0, index])

                @pl.when(core != layer)
                def unused_too():
                    await_bytes(source, small_sems.at[2, index])

    def keep(index, source, target):
        pltpu.make_async_copy(source, target, keep_sem.at[index]).start()

    def kept(index, source):
        await_bytes(source, keep_sem.at[index])

    def swap_tile(index, pair, value):
        own_ref, other_ref = pair
        span = block_rows(pl.program_id(0))
        own_ref[span, :] = value
        send(own_ref.at[span], other_ref.at[span], swap_send.at[index], swap_recv.at[index], {SECTION: 1 - core})

    def swapped(index, pair):
        await_bytes(pair[0], swap_send.at[index])
        await_bytes(pair[1], swap_recv.at[index])

    def mid_row(ref, layer, group):
        return ref[layer, :, lanes(group * 1024 + core * 512, 512)]

    def project_rows(layer, x, normed_ref, proj_ref, w_ref):
        unit_x, unused = standard(x)
        normed = (unit_x * gains[layer, 0:1, :] + shifts[layer, 0:1, :]).astype(BF16)
        normed_ref[...] = normed
        for group in range(4):
            proj_ref[group] = dot(normed, w_ref[group].reshape(1024, 384)).astype(BF16)

    def project_stage(layer, hooks):
        own_half = saved[layer]
        weight = (wholes[layer][0], whole_spec((4, 4, 256, 384)))
        made = [(own_half.normed, rows_spec(1024)), (own_half.proj, group_spec(384))]

        def body_first(x_ref, w_ref, normed_ref, proj_ref):
            project_rows(layer, x_ref[...].astype(F32), normed_ref, proj_ref, w_ref)

        def body_next(res_ref, a_ref, b_ref, w_ref, normed_ref, proj_ref, entry_ref):
            entry = (res_ref[...] + (a_ref[...].astype(F32) + b_ref[...].astype(F32))).astype(BF16)
            entry_ref[...] = entry
            project_rows(layer, entry.astype(F32), normed_ref, proj_ref, w_ref)

        if layer == 0:
            stage(body_first, [(own_half.entry, rows_spec(1024)), weight], made, hooks)
        else:
            stage(
                body_next,
                [(saved[0].residual, rows_spec(1024)), (swaps[1][0], rows_spec(1024)), (swaps[1][1], rows_spec(1024)), weight],
                [*made, (own_half.entry, rows_spec(1024))],
                hooks,
            )

    def attention_stage(layer, hooks):
        own_half = saved[layer]

        def body(q_ref, k_ref, v_ref, out_ref, scaled_ref, log_ref):
            scale_row = head_row[layer, :, lanes(pl.program_id(0) * 256 + core * 128, 128)]
            attend(
                q_ref, k_ref, v_ref, scale_row, out_ref, scaled_ref, log_ref, split_ref[place], triangle, turned, walled
            )

        stage(
            body,
            [(own_half.proj, third_spec(0)), (own_half.proj, third_spec(1)), (own_half.proj, third_spec(2))],
            [(own_half.head_out, column_spec(128)), (own_half.scaled, column_spec(128)),
             (own_half.logs, pl.BlockSpec((1, 2, 1024), lambda group: (group, 0, 0)))],
            hooks,
        )

    def out_stage(layer, hooks):
        def body(scaled_ref, w_ref):
            swap_tile(layer * 2, swaps[layer * 2], dot(scaled_ref[...], w_ref[...].reshape(512, 1024)).astype(BF16))

        stage(body, [(saved[layer].scaled, rows_spec(512)), (wholes[layer][1], whole_spec((4, 128, 1024)))], [], hooks)

    def widen_stage(layer, hooks):
        own_half = saved[layer]

        def body(x_ref, a_ref, b_ref, w_ref, res_ref, ffn_ref, gelu_ref, slope_ref):
            branch = a_ref[...].astype(F32) + b_ref[...].astype(F32)
            unit_b, unused = standard(branch)
            residual = x_ref[...].astype(F32) + unit_b * gains[layer, 1:2, :] + shifts[layer, 1:2, :]
            res_ref[...] = residual
            unit_r, unused = standard(residual)
            ffn_input = (unit_r * gains[layer, 2:3, :] + shifts[layer, 2:3, :]).astype(BF16)
            ffn_ref[...] = ffn_input
            first, second = [], []
            for group in range(4):
                hidden = dot(ffn_input, w_ref[group].reshape(1024, 512))
                half = 0.5 + 0.5 * lax.erf(hidden * math.sqrt(0.5))
                gelu = hidden * half
                bell = jnp.exp(-0.5 * hidden * hidden) * (1.0 / math.sqrt(2.0 * math.pi))
                gelu_ref[group] = gelu.astype(BF16)
                slope_ref[group] = (half + hidden * bell).astype(BF16)
                mean = jnp.mean(gelu, axis=-1, keepdims=True)
                centre = gelu - mean
                first.append(mean)
                second.append(jnp.mean(centre * centre, axis=-1, keepdims=True))
            mean = 0.25 * (first[0] + first[1] + first[2] + first[3])
            spread_of = sum(0.25 * (s + (m - mean) * (m - mean)) for m, s in zip(first, second))
            swap_tile(3 + layer, stats[layer], two_columns(mean, spread_of))

        branch_own, branch_other = swaps[layer * 2]
        stage(
            body,
            [(own_half.entry, rows_spec(1024)), (branch_own, rows_spec(1024)), (branch_other, rows_spec(1024)),
             (wholes[layer][2], whole_spec((4, 4, 256, 512)))],
            [(own_half.residual, rows_spec(1024)), (own_half.ffn_input, rows_spec(1024)), (own_half.gelu, group_spec(512)),
             (own_half.slope, group_spec(512))],
            hooks,
        )

    def middle_rows(layer, gelu, mean, scale, group):
        unit_m = (gelu.astype(F32) - mean) * scale
        return (unit_m * mid_row(mid_gain, layer, group) + mid_row(mid_shift, layer, group)).astype(BF16)

    def narrow_stage(layer, hooks):
        own_half = saved[layer]

        def body(g_ref, own_ref, other_ref, w_ref, mid_ref):
            mean, scale = mid_stats(own_ref[...], other_ref[...])
            total = jnp.zeros((TILE, 1024), F32)
            for group in range(4):
                middle = middle_rows(layer, g_ref[group], mean, scale, group)
                mid_ref[group] = middle
                total = total + dot(middle, w_ref[group])
            swap_tile(1, swaps[1], total.astype(BF16))

        stage(
            body,
            [(own_half.gelu, group_spec(512)), (stats[layer][0], rows_spec(128)), (stats[layer][1], rows_spec(128)),
             (wholes[layer][3], whole_spec((4, 512, 1024)))],
            [(own_half.middle, group_spec(512))],
            hooks,
        )

    def middle_stage(layer, hooks):
        own_half = saved[layer]

        def body(g_ref, own_ref, other_ref, mid_ref):
            mean, scale = mid_stats(own_ref[...], other_ref[...])
            for group in range(4):
                mid_ref[group] = middle_rows(layer, g_ref[group], mean, scale, group)

        stage(
            body,
            [(own_half.gelu, group_spec(512)), (stats[layer][0], rows_spec(128)), (stats[layer][1], rows_spec(128))],
            [(own_half.middle, group_spec(512))],
            hooks,
        )

    def layer_forward(layer, hooks, gaps):
        own_half = saved[layer]
        base = layer * 4
        gaps[0]()
        ready(base)
        if layer == 0:
            passed(0)
            take_smalls()
        else:
            swapped(1, swaps[1])
        project_stage(layer, hooks[0])
        attention_stage(layer, hooks[1])
        gaps[1]()
        ready(base + 1)
        out_stage(layer, hooks[2])
        gaps[2]()
        ready(base + 2)
        swapped(layer * 2, swaps[layer * 2])
        for index, (source, target) in enumerate(zip(swaps[layer * 2], (own_half.branch, own_half.branch_other))):
            keep(layer * 2 + index, source, target)
        widen_stage(layer, hooks[3])
        gaps[3]()
        swapped(3 + layer, stats[layer])
        if layer == 0:
            ready(base + 3)
            narrow_stage(layer, hooks[4])
        else:
            middle_stage(layer, hooks[4])

    deep(0)
    items_out(0)
    smalls_out()
    own(0)
    deep(1)
    own(1)
    fill_triangle(triangle)
    first_hop(0)
    deep(2)
    pass_on(0)
    first_hop(1)
    second_hop(0)
    own(2)
    deep(3)
    second_hop(1)
    own(3)
    items_out(1)
    layer_forward(0, ((), ((1, after((first_hop, 2), (deep, 4))),), (), (), ()), (
        after(),
        after((pass_on, 1), (own, 4)),
        after((second_hop, 2), (first_hop, 3), (deep, 5), (own, 5)),
        after((second_hop, 3), (first_hop, 4), (deep, 6), (own, 6)),
    ))
    layer_forward(1, (((1, after((second_hop, 5), (first_hop, 6))),), (), (), (), ()), (
        after((second_hop, 4), (first_hop, 5), (deep, 7), (own, 7)),
        after(),
        after((second_hop, 6), (first_hop, 7)),
        after((second_hop, 7),),
    ))

    for layer in (0, 1):
        for index, source in enumerate(swaps[layer * 2]):
            kept(layer * 2 + index, source)
    passed(1)

    def clean_up():
        for layer in (0, 1):
            @pl.when(core == layer)
            def unused():
                for step in (1, 2, 3):
                    await_bytes(items.at[0], item_send.at[layer, step])
                for step in range(4):
                    await_bytes(items.at[0], item_pass.at[layer, step])
                for index, source in enumerate(small_in):
                    await_bytes(source, small_sems.at[1, index])

        for unit, (layer, matrix) in enumerate(units):
            whole = wholes[layer]

            @pl.when(core == layer)
            def unused_too():
                await_bytes(pieces_view(whole, matrix, 2, 2), own_send.at[unit, 1])
                await_bytes(pieces_view(whole, matrix, 3, 2), deep_send.at[unit])

            await_bytes(pieces_view(whole, matrix, 3, 3), hop_send.at[unit])

    return after((ready, 7)), clean_up


ORDER = tuple((layer, matrix) for layer in (1, 0) for matrix in (3, 2, 1, 0))

class Made(NamedTuple):
    d_middle: object
    d_hidden: object
    d_residual: object
    d_branch: object
    d_heads: object
    d_proj: object
    d_entry: object


def add_up_into(target, *terms):
    rows = target.shape[0]

    def step(index, unused):
        span = pl.ds(pl.multiple_of(index * 32, 32), 32)
        total = target[span, :].astype(F32)
        for term in terms:
            total = total + term[span, :].astype(F32)
        target[span, :] = total.astype(BF16)
        return unused

    lax.fori_loop(0, rows // 32, step, 0)


def whole_kernel(*refs):
    refs = list(refs)

    def take(count):
        found = refs[:count]
        del refs[:count]
        return found

    (split_ref,) = take(1)
    items, *raw = take(5)
    small_in = take(5)
    shares = take(4)
    (ends,) = take(1)
    small_outs = take(5)
    cotangent, output = take(2)
    weights = (take(4), take(4))
    saved = [Saved(*take(13)) for unused in (0, 1)]
    grads = (take(4), take(4))
    made = [Made(*take(7)) for unused in (0, 1)]
    smalls = take(5)
    attention_refs = take(3)
    swaps = [(*take(2),) for unused in range(3)]
    stats = [(*take(2),) for unused in (0, 1)]
    sums = [(*take(2),) for unused in (0, 1)]
    own, first_in, second_in, deep_in = take(4), take(4), take(4), take(4)
    vec, inbox, acc, dk_acc, dv_acc = take(5)
    forward_sems = take(13)
    (load_sem, first_send, first_recv, second_send, second_recv, deep_send, deep_recv, last_send, last_copy,
     last_recv, ends_send, ends_recv, small_send, small_recv, swap_send, swap_recv, credit) = refs
    gains, unused_shifts, mid_gain, unused_mid_shift, head_row = smalls
    triangle, turned, walled = attention_refs
    core, place, depth = here()
    last_ready, clean_up = forward_part(
        items, raw, small_in, cotangent, weights, saved, smalls, split_ref, attention_refs, swaps, stats, forward_sems
    )

    def send_ends(owner, source):
        @pl.when(core == owner)
        def unused():
            for step in (1, 2, 3):
                send(source.at[block_rows(partner(place, step))], ends.at[place], ends_send.at[step], ends_recv.at[step],
                     {DP: partner(place, step)})
            pltpu.make_async_copy(source.at[block_rows(place)], ends.at[place], ends_send.at[0]).start()

    def route(step):
        return (1, 2) if step < 2 else (2, 1)

    def shard_of(step):
        return lax.rem(depth + step, 4)

    def begin(unit):
        layer, matrix = ORDER[unit]
        if unit >= 4:
            pl.semaphore_wait(credit.at[matrix], 2)
        for step in range(4):
            first, second = route(step)
            for index, offset in enumerate((first, 3)):
                send(whole_view(grads[layer], matrix, partner(place, offset), shard_of(step)),
                     first_in[matrix].at[step, index], first_send.at[unit], first_recv.at[unit],
                     {DP: partner(place, first)})
            for index, offset in enumerate((0, second)):
                pltpu.make_async_copy(
                    whole_view(grads[layer], matrix, partner(place, offset), shard_of(step)),
                    own[matrix].at[step, index], load_sem.at[unit],
                ).start()

    def second_hop(unit):
        layer, matrix = ORDER[unit]
        await_bytes(own[matrix], load_sem.at[unit])
        await_bytes(first_in[matrix], first_recv.at[unit])
        for step in range(4):
            first, second = route(step)
            mine = own[matrix].at[step, 1]
            add_up_into(mine, first_in[matrix].at[step, 1])
            send(mine, second_in[matrix].at[step], second_send.at[unit], second_recv.at[unit],
                 {DP: partner(place, second)})

    def deep_hop(unit):
        layer, matrix = ORDER[unit]
        await_bytes(second_in[matrix], second_recv.at[unit])
        for step in (1, 2, 3, 0):
            mine = own[matrix].at[step, 0]
            add_up_into(mine, first_in[matrix].at[step, 0], second_in[matrix].at[step])
            if step:
                send(mine, deep_in[matrix].at[layer, step - 1], deep_send.at[unit], deep_recv.at[unit],
                     {SHARD: shard_of(step)})
        if unit < 4:
            for step in (1, 2):
                pl.semaphore_signal(
                    credit.at[matrix], inc=1, device_id={DP: partner(place, step)}, device_id_type=MESH
                )

    def finish(unit):
        layer, matrix = ORDER[unit]
        await_bytes(deep_in[matrix].at[layer], deep_recv.at[unit])
        mine = own[matrix].at[0, 0]
        add_up_into(mine, *[deep_in[matrix].at[layer, index] for index in range(3)])
        sources = [mine]
        if matrix == 0:
            sources = [mine.at[:, pl.ds(third * 128, 128)] for third in range(3)]
        for half in (0, 1):
            @pl.when(core == half)
            def unused():
                for source, target in zip(sources, raw_views(shares, matrix, half, place)):
                    if half == layer:
                        pltpu.make_async_copy(source, target, last_copy.at[unit]).start()
                        for offset in (1, 2):
                            send(source, target, last_send.at[unit, 0], last_recv.at[unit, half, offset],
                                 {DP: partner(place, offset)})
                    else:
                        send(source, target, last_send.at[unit, 0], last_recv.at[unit, half, 0], {SECTION: layer})

    def forward(unit):
        layer, matrix = ORDER[unit]
        half = 1 - layer

        @pl.when(core == layer)
        def unused():
            views = raw_views(shares, matrix, half, place)
            await_bytes(own[matrix].at[0, 0], last_recv.at[unit, half, 0])
            for view in views:
                for offset in (1, 2):
                    send(view, view, last_send.at[unit, 1], last_recv.at[unit, half, offset],
                         {DP: partner(place, offset)})

    def corner(unit):
        layer, matrix = ORDER[unit]

        @pl.when(core == layer)
        def unused():
            for half in (layer, 1 - layer):
                first, second = (1, 2) if half == 0 else (2, 1)
                await_bytes(own[matrix].at[0, 0], last_recv.at[unit, half, first])
                for view in raw_views(shares, matrix, half, partner(place, first)):
                    send(view, view, last_send.at[unit, 2], last_recv.at[unit, half, 3], {DP: partner(place, second)})

    def free_own(unit):
        layer, matrix = ORDER[unit]

        @pl.when(core == layer)
        def unused():
            await_bytes(own[matrix].at[0], last_send.at[unit, 0])
            await_bytes(own[matrix].at[0, 0], last_copy.at[unit])

        @pl.when(core != layer)
        def unused_too():
            await_bytes(own[matrix].at[0, 0], last_send.at[unit, 0])

    def free_hops(unit):
        layer, matrix = ORDER[unit]
        await_bytes(second_in[matrix], second_send.at[unit])
        await_bytes(deep_in[matrix].at[layer], deep_send.at[unit])
        free_own(unit)

    def clean(unit):
        layer, matrix = ORDER[unit]
        await_bytes(first_in[matrix], first_send.at[unit])
        if unit >= 4:
            free_hops(unit)

        @pl.when(core == layer)
        def unused():
            for row in (1, 2):
                await_bytes(own[matrix].at[0], last_send.at[unit, row])
            for half in (0, 1):
                first, second = (1, 2) if half == 0 else (2, 1)
                await_bytes(own[matrix].at[0, 0], last_recv.at[unit, half, second])
                await_bytes(own[matrix].at[0, 0], last_recv.at[unit, half, 3])

    column = pl.ds(pl.multiple_of(core * 512, 512), 512)
    exchanges = (
        {SECTION: 1 - core},
        {DP: partner(place, 1)},
        {DP: partner(place, 2)},
        {SHARD: partner(depth, 1)},
        {SHARD: partner(depth, 2)},
    )

    def small_step(index):
        if index:
            send(acc.at[index - 1], inbox.at[index], small_send.at[index], small_recv.at[index], exchanges[index])
        else:
            for layer in (0, 1):
                @pl.when(core != layer)
                def unused():
                    vec[layer, 0:6, :] = jnp.zeros((6, 1024), F32)

            for half in (0, 1):
                @pl.when(core == half)
                def unused_too():
                    send(vec.at[1 - half], inbox.at[0], small_send.at[0], small_recv.at[0], exchanges[0])

    def small_take(index):
        await_bytes(inbox.at[index], small_recv.at[index])
        if index:
            acc[index] = acc[index - 1] + inbox[index]
        else:
            for half in (0, 1):
                @pl.when(core == half)
                def unused():
                    acc[0] = vec[half] + inbox[0]

    def swap_tile(index, pair, value):
        own_ref, other_ref = pair
        span = block_rows(pl.program_id(0))
        own_ref[span, :] = value
        send(own_ref.at[span], other_ref.at[span], swap_send.at[index], swap_recv.at[index], {SECTION: 1 - core})

    def swapped(index, pair):
        await_bytes(pair[0], swap_send.at[index])
        await_bytes(pair[1], swap_recv.at[index])

    def mid_row(layer, group):
        return mid_gain[layer, :, lanes(group * 1024 + core * 512, 512)]

    def add_vec(layer, row, value, span=slice(None)):
        vec[layer, row : row + 1, span] += value

    def weight_grad(left, left_spec, right, right_spec, target, target_spec):
        def body(left_ref, right_ref, out_ref):
            a = left_ref[...].reshape(left_ref.shape[-2:])
            b = right_ref[...].reshape(right_ref.shape[-2:])
            value = lax.dot_general(a, b, (((0,), (0,)), ((), ())), preferred_element_type=F32)
            out_ref[...] = value.astype(BF16).reshape(out_ref.shape)

        stage(body, [(left, left_spec), (right, right_spec)], [(target, target_spec)])

    def narrow_stage(layer, grad):
        own_half, make = saved[layer], made[layer]

        def body(c_ref, g_ref, own_ref, other_ref, w_ref, dm_ref):
            mean, scale = mid_stats(own_ref[...], other_ref[...])
            grad_low = c_ref[...]
            first = jnp.zeros((TILE, 1), F32)
            second = jnp.zeros((TILE, 1), F32)
            for group in range(4):
                d_middle = dot_nt(grad_low, w_ref[group])
                dm_ref[group] = d_middle.astype(BF16)
                unit_m = (g_ref[group].astype(F32) - mean) * scale
                product = d_middle * unit_m
                add_vec(layer, 6 + group, jnp.sum(product, axis=0, keepdims=True), column)
                add_vec(layer, 10 + group, jnp.sum(d_middle, axis=0, keepdims=True), column)
                row_gain = mid_row(layer, group)
                first = first + jnp.sum(d_middle * row_gain, axis=-1, keepdims=True)
                second = second + jnp.sum(product * row_gain, axis=-1, keepdims=True)
            swap_tile(layer * 3, sums[layer], two_columns(first, second))

        stage(
            body,
            [(grad, rows_spec(1024)), (own_half.gelu, group_spec(512)), (stats[layer][0], rows_spec(128)),
             (stats[layer][1], rows_spec(128)), (weights[layer][3], whole_spec((4, 512, 1024)))],
            [(make.d_middle, group_spec(512))],
        )

    def widen_stage(layer):
        own_half, make = saved[layer], made[layer]

        def body(dm_ref, g_ref, s_ref, own_ref, other_ref, a_ref, b_ref, w_ref, dh_ref):
            mean, scale = mid_stats(own_ref[...], other_ref[...])
            both = (a_ref[...] + b_ref[...]) * (1.0 / 4096)
            first, second = both[:, 0:1], both[:, 64:65]
            total = jnp.zeros((TILE, 1024), F32)
            for group in range(4):
                unit_m = (g_ref[group].astype(F32) - mean) * scale
                inner = dm_ref[group].astype(F32) * mid_row(layer, group)
                d_gelu = scale * (inner - first - unit_m * second)
                d_hidden = (d_gelu * s_ref[group].astype(F32)).astype(BF16)
                dh_ref[group] = d_hidden
                total = total + dot_nt(d_hidden, w_ref[group].reshape(1024, 512))
            swap_tile(layer * 3 + 1, swaps[0], total.astype(BF16))

        stage(
            body,
            [(make.d_middle, group_spec(512)), (own_half.gelu, group_spec(512)), (own_half.slope, group_spec(512)),
             (stats[layer][0], rows_spec(128)), (stats[layer][1], rows_spec(128)), (sums[layer][0], rows_spec(128)),
             (sums[layer][1], rows_spec(128)), (weights[layer][2], whole_spec((4, 4, 256, 512)))],
            [(make.d_hidden, group_spec(512))],
        )

    def norms_stage(layer, grad):
        own_half, make = saved[layer], made[layer]
        scale_row = jnp.concatenate(
            [head_row[layer, :, lanes(group * 256 + core * 128, 128)] for group in range(4)], axis=1
        )

        def body(c_ref, res_ref, da_ref, db_ref, ba_ref, bb_ref, ho_ref, w_ref, dr_ref, dbr_ref, dh_ref):
            unit_r, scale_r = standard(res_ref[...])
            d_ffn = da_ref[...].astype(F32) + db_ref[...].astype(F32)
            back, gain_third, shift_third = standard_back(unit_r, scale_r, gains[layer, 2:3, :], d_ffn)
            d_residual = c_ref[...].astype(F32) + back
            dr_ref[...] = d_residual
            unit_b, scale_b = standard(ba_ref[...].astype(F32) + bb_ref[...].astype(F32))
            back, gain_second, shift_second = standard_back(unit_b, scale_b, gains[layer, 1:2, :], d_residual)
            d_branch = back.astype(BF16)
            dbr_ref[...] = d_branch
            d_scaled = dot_nt(d_branch, w_ref[...].reshape(512, 1024))
            dh_ref[...] = (d_scaled * scale_row).astype(BF16)
            add_vec(layer, 14, jnp.sum(d_scaled * ho_ref[...].astype(F32), axis=0, keepdims=True), column)
            for row, value in ((1, gain_second), (2, gain_third), (4, shift_second), (5, shift_third)):
                add_vec(layer, row, value)

        stage(
            body,
            [(grad, rows_spec(1024)), (own_half.residual, rows_spec(1024)), (swaps[0][0], rows_spec(1024)),
             (swaps[0][1], rows_spec(1024)), (own_half.branch, rows_spec(1024)),
             (own_half.branch_other, rows_spec(1024)), (own_half.head_out, rows_spec(512)),
             (weights[layer][1], whole_spec((4, 128, 1024)))],
            [(make.d_residual, rows_spec(1024)), (make.d_branch, rows_spec(1024)), (make.d_heads, rows_spec(512))],
        )

    def attention_stage(layer):
        own_half, make = saved[layer], made[layer]

        def body(q_ref, k_ref, v_ref, grad_ref, out_ref, log_ref, back_ref):
            attend_back(
                q_ref, k_ref, v_ref, grad_ref, out_ref, log_ref, back_ref, split_ref[place], triangle, turned, walled, dk_acc, dv_acc
            )

        stage(
            body,
            [(own_half.proj, third_spec(0)), (own_half.proj, third_spec(1)), (own_half.proj, third_spec(2)),
             (make.d_heads, column_spec(128)), (own_half.head_out, column_spec(128)),
             (own_half.logs, pl.BlockSpec((1, 2, 1024), lambda group: (group, 0, 0)))],
            [(make.d_proj, block_spec(1024, 384))],
        )

    def project_stage(layer):
        make = made[layer]

        def body(d_ref, w_ref):
            total = dot_nt(d_ref[0], w_ref[0].reshape(1024, 384))
            for group in range(1, 4):
                total = total + dot_nt(d_ref[group], w_ref[group].reshape(1024, 384))
            swap_tile(layer * 3 + 2, swaps[1], total.astype(BF16))

        stage(
            body, [(make.d_proj, group_spec(384)), (weights[layer][0], whole_spec((4, 4, 256, 384)))], []
        )

    def entry_stage(layer):
        own_half, make = saved[layer], made[layer]

        def body(dr_ref, a_ref, b_ref, x_ref, dx_ref):
            unit_x, scale_x = standard(x_ref[...].astype(F32))
            d_normed = a_ref[...].astype(F32) + b_ref[...].astype(F32)
            back, gain_first, shift_first = standard_back(unit_x, scale_x, gains[layer, 0:1, :], d_normed)
            dx_ref[...] = (dr_ref[...] + back).astype(BF16)
            add_vec(layer, 0, gain_first)
            add_vec(layer, 3, shift_first)

        stage(
            body,
            [(make.d_residual, rows_spec(1024)), (swaps[1][0], rows_spec(1024)),
             (swaps[1][1], rows_spec(1024)), (own_half.entry, rows_spec(1024))],
            [(make.d_entry, rows_spec(1024))],
        )

    def layer_back(layer, grad, events):
        own_half, make = saved[layer], made[layer]
        base = 0 if layer == 1 else 4
        weight_grad(own_half.middle, block_spec(1024, 512), grad, whole_spec((1024, 1024)),
                    grads[layer][3], block_spec(512, 1024))
        events[0]()
        begin(base)
        if layer == 1:
            last_ready()
        narrow_stage(layer, grad)
        events[1]()
        swapped(layer * 3, sums[layer])
        widen_stage(layer)
        events[2]()
        weight_grad(own_half.ffn_input, whole_spec((1024, 1024)), make.d_hidden, block_spec(1024, 512),
                    grads[layer][2], grad_spec(512))
        begin(base + 1)
        swapped(layer * 3 + 1, swaps[0])
        norms_stage(layer, grad)
        events[3]()
        weight_grad(own_half.scaled, column_spec(128), make.d_branch, whole_spec((1024, 1024)),
                    grads[layer][1], block_spec(128, 1024))
        begin(base + 2)
        attention_stage(layer)
        events[4]()
        if layer == 1:
            project_stage(layer)
            events[5]()
        weight_grad(own_half.normed, whole_spec((1024, 1024)), make.d_proj, block_spec(1024, 384),
                    grads[layer][0], grad_spec(384))
        if layer == 0:
            events[5]()
        begin(base + 3)
        if layer == 0:
            project_stage(layer)
        swapped(layer * 3 + 2, swaps[1])
        entry_stage(layer)
        events[6]()

    def last_stage():
        def body(mid_ref, w_ref):
            total = dot(mid_ref[0], w_ref[0])
            for group in range(1, 4):
                total = total + dot(mid_ref[group], w_ref[group])
            swap_tile(6, swaps[2], total.astype(BF16))

        stage(body, [(saved[1].middle, group_spec(512)), (weights[1][3], whole_spec((4, 512, 1024)))], [])

    def output_stage():
        swapped(6, swaps[2])

        def body(res_ref, a_ref, b_ref, out_ref):
            out_ref[...] = (res_ref[...] + (a_ref[...].astype(F32) + b_ref[...].astype(F32))).astype(BF16)

        stage(
            body,
            [(saved[1].residual, rows_spec(1024)), (swaps[2][0], rows_spec(1024)), (swaps[2][1], rows_spec(1024))],
            [(output, rows_spec(1024))],
        )
        send_ends(1, output)

    def prepare():
        vec[...] = jnp.zeros_like(vec)

    layer_back(1, cotangent, (
        after((prepare,),),
        after(),
        after((second_hop, 0),),
        after((deep_hop, 0),),
        after((second_hop, 1), (finish, 0), (second_hop, 2)),
        after((deep_hop, 1), (forward, 0)),
        after((deep_hop, 2), (corner, 0)),
    ))
    layer_back(0, made[1].d_entry, (
        after((free_hops, 0),),
        after((second_hop, 3), (finish, 1), (finish, 2)),
        after((forward, 1), (forward, 2), (free_hops, 1)),
        after((deep_hop, 3), (second_hop, 4), (corner, 1), (corner, 2), (free_hops, 2)),
        after((deep_hop, 4), (finish, 3), (second_hop, 5), (second_hop, 6)),
        after((forward, 3), (free_hops, 3)),
        after((deep_hop, 5), (finish, 4), (corner, 3), (deep_hop, 6)),
    ))
    small_step(0)
    last_stage()
    second_hop(7)
    output_stage()
    forward(4)
    finish(5)
    finish(6)
    small_take(0)
    small_step(1)
    deep_hop(7)
    send_ends(0, made[0].d_entry)
    corner(4)
    forward(5)
    forward(6)
    small_take(1)
    small_step(2)
    corner(5)
    corner(6)
    small_take(2)
    small_step(3)
    finish(7)
    small_take(3)
    small_step(4)
    forward(7)
    corner(7)
    small_take(4)
    small_outs[0][0] = acc[4, 0:3, :]
    small_outs[1][0] = acc[4, 3:6, :]
    for group in range(4):
        for row in (0, 1):
            small_outs[2 + row][:, group * 1024 : group * 1024 + 1024] = acc[4, 6 + 4 * row + group : 7 + 4 * row + group, :]
    small_outs[4][...] = acc[4, 14:15, :]
    clean_up()
    for unit in range(8):
        clean(unit)
    for index in range(5):
        await_bytes(inbox.at[index], small_send.at[index])
    for step in range(4):
        await_bytes(ends.at[0], ends_send.at[step])
    for step in (1, 2, 3):
        await_bytes(ends.at[0], ends_recv.at[step])


def both_layers(split_at, items, weights, smalls):
    anywhere = pl.BlockSpec(memory_space=pl.ANY)
    local_space = pl.BlockSpec(memory_space=pltpu.VMEM)
    dma = pltpu.SemaphoreType.DMA
    rows, rows_wide = array((1024, 1024), BF16), array((1024, 1024), F32)
    weight_shapes = [
        array((4, 4, 256, 384), BF16),
        array((4, 128, 1024), BF16),
        array((4, 4, 256, 512), BF16),
        array((4, 512, 1024), BF16),
    ]
    wide, heads, proj = array((4, 1024, 512), BF16), array((1024, 512), BF16), array((4, 1024, 384), BF16)
    saved = [rows, rows, proj, heads, heads, array((4, 2, 1024), F32), rows, rows, rows_wide, rows, wide, wide, wide]
    made = [wide, wide, rows_wide, rows, heads, proj, rows]
    small_shapes = [(2,) + operand.shape for operand in smalls]
    shapes = [
        array((256, 3072), BF16),
        array((256, 1024), BF16),
        array((256, 4096), BF16),
        array((1024, 1024), BF16),
        array((4, 256, 1024), BF16),
        array((1, 3, 1024), F32),
        array((1, 3, 1024), F32),
        array((1, 4096), F32),
        array((1, 4096), F32),
        array((1, 1024), F32),
        rows,
        rows,
        *weight_shapes * 2,
        *saved * 2,
        *weight_shapes * 2,
        *made * 2,
    ]
    return pl.pallas_call(
        whole_kernel,
        in_specs=[pl.BlockSpec(memory_space=pltpu.SMEM)] + [anywhere] * 10,
        out_specs=[anywhere] * 5 + [local_space] * 5 + [anywhere] * (len(shapes) - 10),
        out_shape=shapes,
        scratch_shapes=[pltpu.VMEM(shape, F32) for shape in small_shapes]
        + [pltpu.VMEM((256, 256), F32), pltpu.VMEM((128, 1024), BF16), pltpu.VMEM((2, 1024, 128), BF16)]
        + [pltpu.VMEM((1024, 1024), BF16)] * 6
        + [pltpu.VMEM((1024, 128), F32)] * 8
        + [pltpu.VMEM((4, 2) + size, BF16) for size in SIZES]
        + [pltpu.VMEM((4, 2) + size, BF16) for size in SIZES]
        + [pltpu.VMEM((4,) + size, BF16) for size in SIZES]
        + [pltpu.VMEM((2, 3) + size, BF16) for size in SIZES]
        + [pltpu.VMEM((2, 16, 1024), F32), pltpu.VMEM((5, 16, 1024), F32), pltpu.VMEM((5, 16, 1024), F32)]
        + [pltpu.VMEM((1024, 128), F32), pltpu.VMEM((1024, 128), F32)]
        + [
            dma((2, 4)), dma((2, 4)), dma((2, 4)), dma((8, 2)), dma((8,)),
            dma((8,)), dma((8, 4)), dma((8,)), dma((8, 3, 3)), dma((3, 5)),
            dma((5,)), dma((5,)), dma((4,)),
        ]
        + [dma((8,))] * 7
        + [dma((8, 3)), dma((8,)), dma((8, 2, 4)), dma((4,)), dma((4,)), dma((5,)), dma((5,)), dma((7,)), dma((7,))]
        + [pltpu.SemaphoreType.REGULAR((4,))],
        compiler_params=pltpu.CompilerParams(
            collective_id=0, has_side_effects=True, vmem_limit_bytes=62 * 2**20
        ),
    )(split_at, items, *weights, *smalls)[:10]


def local(
    boundary,
    first_len,
    qkv_weight,
    out_weight,
    up_weight,
    down_weight,
    norm_gain,
    norm_shift,
    mid_gain,
    mid_shift,
    head_scale,
):
    *shares, ends, gain_sums, shift_sums, mid_gain_sums, mid_shift_sums, head_sums = both_layers(
        first_len[:, 0],
        boundary.reshape(4, 256, 1024),
        (qkv_weight[0], out_weight[0], up_weight[0], down_weight[0]),
        (norm_gain[0], norm_shift[0], mid_gain, mid_shift, jnp.repeat(head_scale, 64, axis=1)),
    )
    head_sums = jnp.sum(head_sums.reshape(2, 4, 2, 64), axis=3).transpose(1, 0, 2).reshape(1, 16)
    return (
        ends[None, :, None],
        *[share.astype(F32)[None] for share in shares],
        gain_sums,
        shift_sums,
        mid_gain_sums,
        mid_shift_sums,
        head_sums,
    )


def fits(mesh, boundary, mid_gain, head_scale):
    sizes = (mesh.shape["section"], mesh.shape["dp"], mesh.shape["shard"])
    return (
        sizes == (2, 4, 4)
        and boundary == (2, 4, 4, 1024, 1024)
        and mid_gain == (2, 4096)
        and head_scale == (2, 16)
    )


def solution(mesh):
    placed = (
        P("section", None, "shard", "dp", None),
        P(None, "shard"),
        P("section", "shard", None),
        P("section", "shard", None),
        P("section", "shard", None),
        P("section", "shard", None),
        P("section", None, None),
        P("section", None, None),
        P("section", None),
        P("section", None),
        P("section", None),
    )
    results = (
        P("section", None, "shard", "dp", None),
        P("section", "shard", None),
        P("section", "shard", None),
        P("section", "shard", None),
        P("section", "shard", None),
        P("section", None, None),
        P("section", None, None),
        P("section", None),
        P("section", None),
        P("section", None),
    )

    def whole(*arrays):
        fast = fits(mesh, arrays[0].shape, arrays[8].shape, arrays[10].shape)
        body = local if fast else general
        return jax.shard_map(
            body, mesh=mesh, in_specs=placed, out_specs=results, check_vma=False
        )(*arrays)

    return whole
```
